32 devices in a mesh: gz: 4 (over y, x), dev: 8 (over z, core).
Axes of the slice: x: 2, y: 2, z: 4, core: 2. Of those that a mesh axis runs over, the one named last changes fastest.
Arguments:
- source: float32 [512, 8, 2048], P(None, None, ('gz', 'dev')), may hold values from -6 to 6
- interior_inverse: float32 [512, 512], replicated, as said below
- coupling: float32 [512, 384], replicated, may hold values from -0.25 to 0.25
- trace_operator: float32 [384, 384], replicated, as said below
- face_ids: int32 [2048, 4], P(('gz', 'dev')), may hold values from 0 to 1023, as said below
- orientation: int32 [2048, 6], P(('gz', 'dev')), may hold values from 0 to 7
- element_scale: int32 [2048], P(('gz', 'dev')), may hold values from 1 to 4
Outputs:
- interior: float32 [512, 8, 2048], P(None, None, ('gz', 'dev'))
- side_traces: float32 [64, 8, 4096], P(None, None, ('gz', 'dev'))
- top_traces: float32 [64, 8, 2048], P(None, None, ('gz', 'dev'))
The draws below stay inside these ranges and needn't reach their ends.
Inputs may be any that keep to these rules, and one draw needn't show every extreme that they name: `face_ids`: elements come in blocks of 64 (block b of a layer is the layer's elements b * 64 onward) and a layer's side faces in blocks of 128; face f of a layer belongs to block f // 128. Columns 0 and 1 of a block's elements name each face of that block exactly once. Columns 2 and 3 of a layer's elements name each face of the layer exactly once. The elements of one block name, in columns 2 and 3, at most 8 faces of any one other block, and in every layer some block reaches 8 with some other block. `interior_inverse`: symmetric positive definite. `trace_operator`: symmetric positive definite.
All inputs are finite; a program needn't handle non-finite values.
Results may differ from the reference program's by a relative error of at most 0.0001.
Values sent between devices are 32-bit elements; how exact they have to be, the bound alone decides.
No kernel may reach another device: no remote copies, remote signals or barrier semaphores. Data moves between devices by JAX's collectives and lax.ppermute only.
A program may use at most 64 MiB of HBM per device.

```python
import math
import jax
import jax.numpy as jnp
from jax import lax

NODES = 512
FACE_NODES = 64
RIGHT_SIDES = 8
ITERATIONS = 2
ELEMENTS_DEV = 64
FACES_DEV = 128
CAPACITY = 8
ELEMENTS = 2048
SIDE_FACES = 4096
N_GZ = 4
N_DEV = 8


def definite(key, order):
    factor = jax.random.normal(key, (order, order), jnp.float32)
    shift = 0.5
    gram = jnp.dot(factor, factor.T, precision=lax.Precision.HIGHEST) / order
    return 0.5 * (gram + gram.T) + shift * jnp.eye(order, dtype=jnp.float32)


def draw_interior_inverse(key, part):
    return definite(jax.random.fold_in(key, 11), NODES)


def draw_trace_operator(key, part):
    return definite(jax.random.fold_in(key, 12), 6 * FACE_NODES)


def shuffled(key, blocks, length):
    return jax.vmap(lambda single: jax.random.permutation(single, length))(jax.random.split(key, blocks)).astype(jnp.int32)


def layer_faces(key):
    blocks = N_DEV
    length = 2 * ELEMENTS_DEV
    limit = CAPACITY
    keys = jax.random.split(key, 6)
    raw = jax.random.randint(keys[0], (blocks, blocks), max(1, limit // 2), limit + 1).astype(jnp.int32)
    upper = jnp.triu(raw, 1)
    counts = upper + upper.T
    first = jax.random.randint(keys[1], (), 0, blocks)
    other = (first + jax.random.randint(keys[2], (), 1, blocks)) % blocks
    counts = counts.at[first, other].set(limit).at[other, first].set(limit)
    identity = jnp.eye(blocks, dtype=jnp.int32)
    counts = counts * (1 - identity)
    counts = counts + identity * (length - jnp.sum(counts, axis=1))[:, None]
    ends = jnp.cumsum(counts, axis=1)
    starts = ends - counts
    placed = shuffled(keys[3], blocks, length)
    target = jnp.sum((placed[:, :, None] >= ends[:, None, :]).astype(jnp.int32), axis=2)
    within = placed - jnp.take_along_axis(starts, target, axis=1)
    column_start = jnp.cumsum(counts, axis=0) - counts
    arrival = jnp.take_along_axis(column_start, target, axis=1) + within
    settle = shuffled(keys[4], blocks, length)
    second = target * length + settle[target, arrival]
    owned = shuffled(keys[5], blocks, length)
    first_ids = jnp.arange(blocks, dtype=jnp.int32)[:, None] * length + owned
    joined = jnp.concatenate([first_ids.reshape(blocks, ELEMENTS_DEV, 2), second.reshape(blocks, ELEMENTS_DEV, 2)], axis=2)
    return joined.reshape(blocks * ELEMENTS_DEV, 4).astype(jnp.int32)


def draw_face_ids(key, part):
    layers = jax.random.split(jax.random.fold_in(key, 13), N_GZ)
    return jax.vmap(layer_faces)(layers).reshape(ELEMENTS, 4).astype(jnp.int32)


def touch_ends(entries, key, low, high):
    extent = entries.shape
    spot = [jax.random.randint(jax.random.fold_in(key, axis), (), 0, extent[axis]) for axis in range(len(extent))]
    entries = entries.at[tuple(spot)].set(low)
    longest = extent.index(max(extent))
    spot[longest] = (spot[longest] + 1) % extent[longest]
    return entries.at[tuple(spot)].set(high)


def block_scale(key, extent, cuts, low, top_value):
    loudness = 1.0
    for axis_at, parts in cuts:
        draws = jax.random.uniform(jax.random.fold_in(jax.random.fold_in(key, 6), axis_at), (parts,), jnp.float32, low / len(cuts), top_value / len(cuts))
        loudness = loudness * jnp.repeat(jnp.exp(draws), extent[axis_at] // parts).reshape((-1,) + (1,) * (len(extent) - 1 - axis_at))
    return loudness


def noise(own_key, extent, spread, most, cuts=(), kind=jnp.bfloat16):
    result = jax.random.normal(own_key, extent, jnp.float32) * spread
    if len(cuts) > 0:
        result = block_scale(own_key, extent, cuts, -0.22, 0.18) * result
    return jnp.clip(result, min=-most, max=most).astype(kind)


def setup_inputs(seed: int = 0) -> dict:
    splits = jax.random.split(jax.random.key(seed), 8)
    source = noise(splits[0], (NODES, RIGHT_SIDES, ELEMENTS), 1.0, 6.0, ((2, 32),), jnp.float32)
    interior_inverse = draw_interior_inverse(jax.random.fold_in(splits[7], 71), 0)
    coupling = noise(splits[2], (NODES, 6 * FACE_NODES), NODES ** -0.5, 0.25, (), jnp.float32)
    trace_operator = draw_trace_operator(jax.random.fold_in(splits[7], 71), 0)
    face_ids = draw_face_ids(jax.random.fold_in(splits[7], 71), 0)
    orientation = touch_ends(jax.random.randint(splits[5], (ELEMENTS, 6), 0, 8), jax.random.fold_in(splits[5], 1), 0, 7).astype(jnp.int32)
    element_scale = touch_ends(jax.random.randint(splits[6], (ELEMENTS,), 1, 5), jax.random.fold_in(splits[6], 1), 1, 4).astype(jnp.int32)
    return dict(source=source, interior_inverse=interior_inverse, coupling=coupling, trace_operator=trace_operator, face_ids=face_ids, orientation=orientation, element_scale=element_scale)


def orient_traces(traces, codes, inverse):
    side_count, face_nodes, right_count, element_count = traces.shape
    edge = math.isqrt(face_nodes)
    grid = traces.reshape(side_count, edge, edge, right_count, element_count)
    swapped = (codes // 4 % 2 == 1)[:, None, None, None, :]
    flip_first = (codes // 2 % 2 == 1)[:, None, None, None, :]
    flip_second = (codes % 2 == 1)[:, None, None, None, :]
    if inverse:
        grid = jnp.where(flip_second, grid[:, :, ::-1], grid)
        grid = jnp.where(flip_first, grid[:, ::-1], grid)
        grid = jnp.where(swapped, jnp.swapaxes(grid, 1, 2), grid)
    else:
        grid = jnp.where(swapped, jnp.swapaxes(grid, 1, 2), grid)
        grid = jnp.where(flip_first, grid[:, ::-1], grid)
        grid = jnp.where(flip_second, grid[:, :, ::-1], grid)
    return grid.reshape(side_count, face_nodes, right_count, element_count)

def element_operator(local, trace_operator, element_scale):
    side_count, face_nodes, right_count, element_count = local.shape
    flat = local.reshape(side_count * face_nodes, right_count * element_count)
    image = jnp.dot(trace_operator, flat, precision=lax.Precision.HIGHEST, preferred_element_type=jnp.float32)
    return image.reshape(local.shape) * element_scale.astype(jnp.float32)

def layer_of():
    return jnp.arange(ELEMENTS, dtype=jnp.int32) // (ELEMENTS_DEV * N_DEV)

def global_faces(face_ids):
    return face_ids + (layer_of() * (FACES_DEV * N_DEV))[:, None]

def to_faces(local, global_ids, codes):
    layer_size = ELEMENTS_DEV * N_DEV
    placed = orient_traces(local, codes, True)
    sides = jnp.zeros((FACE_NODES, RIGHT_SIDES, SIDE_FACES), jnp.float32)
    for column in range(4):
        sides = sides.at[:, :, global_ids[:, column]].add(placed[column])
    above = jnp.concatenate([placed[4][:, :, layer_size:], jnp.zeros((FACE_NODES, RIGHT_SIDES, layer_size), jnp.float32)], axis=2)
    keep = (layer_of() < N_GZ - 1).astype(jnp.float32)
    tops = (placed[5] + above) * keep
    return (sides, tops)

def to_elements(traces, global_ids, codes):
    layer_size = ELEMENTS_DEV * N_DEV
    sides, tops = traces
    below = jnp.concatenate([jnp.zeros((FACE_NODES, RIGHT_SIDES, layer_size), jnp.float32), tops[:, :, :-layer_size]], axis=2)
    pieces = [jnp.take(sides, global_ids[:, column], axis=2) for column in range(4)]
    pieces = pieces + [below, tops]
    return orient_traces(jnp.stack(pieces), codes, False)

def inner(first, second):
    return lax.optimization_barrier(jnp.sum(first[0] * second[0], axis=(0, 2))) + lax.optimization_barrier(jnp.sum(first[1] * second[1], axis=(0, 2)))

def advance(first, factor, second):
    return tuple((left + factor[None, :, None] * right for left, right in zip(first, second)))

def reference(source, interior_inverse, coupling, trace_operator, face_ids, orientation, element_scale):
    codes = orientation.T
    global_ids = global_faces(face_ids)
    solved = jnp.dot(interior_inverse, source.reshape(NODES, RIGHT_SIDES * ELEMENTS), precision=lax.Precision.HIGHEST, preferred_element_type=jnp.float32)
    condensed = lax.dot_general(coupling, solved, (((0,), (0,)), ((), ())), precision=lax.Precision.HIGHEST, preferred_element_type=jnp.float32)
    condensed = condensed.reshape(6, FACE_NODES, RIGHT_SIDES, ELEMENTS)
    residual = to_faces(condensed, global_ids, codes)
    solution = (jnp.zeros_like(residual[0]), jnp.zeros_like(residual[1]))
    direction = residual
    norm_now = inner(residual, residual)
    for step in range(ITERATIONS):
        local = to_elements(direction, global_ids, codes)
        image = to_faces(element_operator(local, trace_operator, element_scale), global_ids, codes)
        alpha = norm_now / inner(direction, image)
        solution = advance(solution, alpha, direction)
        residual = tuple((left - alpha[None, :, None] * right for left, right in zip(residual, image)))
        norm_next = inner(residual, residual)
        direction = advance(residual, norm_next / norm_now, direction)
        norm_now = norm_next
    traces = to_elements(solution, global_ids, codes)
    coupled = jnp.dot(coupling, traces.reshape(6 * FACE_NODES, RIGHT_SIDES * ELEMENTS), precision=lax.Precision.HIGHEST, preferred_element_type=jnp.float32)
    correction = jnp.dot(interior_inverse, coupled, precision=lax.Precision.HIGHEST, preferred_element_type=jnp.float32)
    interior = solved.reshape(source.shape) / element_scale.astype(jnp.float32) - correction.reshape(source.shape)
    return (interior, solution[0], solution[1])
```

```python
import functools
import math

import jax
import jax.numpy as jnp
from jax import lax
from jax.experimental import pallas as pl
from jax.experimental.pallas import tpu as pltpu
from jax.sharding import PartitionSpec as P

F32, BF16, I32 = jnp.float32, jnp.bfloat16, jnp.int32
VMEM_BYTES = 24 * 1024 * 1024
STATS = 9


def call(body, outs, args, scratch=(), flops=0):
    return pl.pallas_call(
        body,
        out_shape=[jax.ShapeDtypeStruct(shape, kind) for shape, kind in outs],
        scratch_shapes=list(scratch),
        compiler_params=pltpu.CompilerParams(vmem_limit_bytes=VMEM_BYTES),
        cost_estimate=pl.CostEstimate(
            flops=flops, bytes_accessed=sum(arg.size * 4 for arg in args), transcendentals=0
        ),
    )(*args)


def halves(value):
    high = value.astype(BF16)
    return high, (value - high.astype(F32)).astype(BF16)


def dot(left, right):
    return jnp.dot(left, right, preferred_element_type=F32)


def dot_split(left, right):
    return dot(left[0], right[0]) + (dot(left[1], right[0]) + dot(left[0], right[1]))


def pick(onehot, value):
    high, low = halves(value)
    return dot(onehot, high) + dot(onehot, low)


def iota(shape, axis):
    return lax.broadcasted_iota(I32, shape, axis)


def column_of(row):
    size = row.shape[1]
    mask = iota((size, size), 0) == iota((size, size), 1)
    spread = jnp.where(mask, row.astype(F32), 0.0)
    return jnp.sum(spread, axis=1, keepdims=True).astype(I32)


def swap_blocks(source, target, rows, columns, block):
    low = iota((block, 2 * block), 1) < block
    for r in range(0, rows, 2):
        for c in range(0, columns, 2):
            lanes = slice(c * block, (c + 2) * block)
            first = source[r * block : (r + 1) * block, lanes]
            second = source[(r + 1) * block : (r + 2) * block, lanes]
            lanes = slice(r * block, (r + 2) * block)
            target[c * block : (c + 1) * block, lanes] = jnp.where(
                low, first, pltpu.roll(second, block, 1)
            )
            target[(c + 1) * block : (c + 2) * block, lanes] = jnp.where(
                low, pltpu.roll(first, block, 1), second
            )


def turn(value, table):
    width = table.shape[1]
    return jnp.concatenate(
        [
            jnp.take_along_axis(
                value[:, at : at + width], table, axis=1, mode="promise_in_bounds"
            )
            for at in range(0, value.shape[1], width)
        ],
        axis=1,
    )


def second_sides(ids_ref, owned, capacity):
    row = jnp.concatenate([ids_ref[2:3, :], ids_ref[3:4, :]], axis=1)
    owner, slot = lax.div(row, owned), lax.rem(row, owned)
    count = row.shape[1]
    crossing = owner != lax.axis_index("dev")
    owner_column = column_of(owner)
    same = (owner_column == owner) & (iota((count, count), 0) < iota((count, count), 1))
    rank = jnp.sum(jnp.where(same, 1.0, 0.0), axis=0, keepdims=True).astype(I32)
    return owner, slot, crossing, rank


def wishes_body(owned, capacity, ids, out):
    owner, slot, crossing, rank = second_sides(ids, owned, capacity)
    shape = (out.shape[0], owner.shape[1])
    place = jnp.where(crossing, owner * capacity + rank, -1)
    line = iota(shape, 0)
    position = lax.div(line, 2 * capacity) * capacity + lax.rem(line, capacity)
    chosen = jnp.where(position == place, (slot + 1).astype(F32), 0.0)
    out[...] = jnp.broadcast_to(
        jnp.sum(chosen, axis=1, keepdims=True).astype(I32), out.shape
    )


def start_body(
    face_nodes, source, inverse, coupling, orientation, solved, sides, bottom, top, forward, back,
    flat, grid
):
    columns = orientation.shape[0]
    count = orientation.shape[1]
    edge = math.isqrt(face_nodes)
    pair = 2 * face_nodes
    lane = iota((count, pair), 1)
    half = lane - lax.rem(lane, face_nodes)
    node = lax.rem(lane, face_nodes)
    a, b = lax.div(node, edge), lax.rem(node, edge)
    for c in range(columns):
        code = jnp.broadcast_to(column_of(orientation[c : c + 1, :]), (count, pair))
        swapped = (code & 4) != 0
        first = (code & 2) != 0
        second = (code & 1) != 0
        i = jnp.where(first, edge - 1 - a, a)
        j = jnp.where(second, edge - 1 - b, b)
        forward[c * count : (c + 1) * count, :] = half + jnp.where(
            swapped, j * edge + i, i * edge + j
        )
        i, j = jnp.where(swapped, b, a), jnp.where(swapped, a, b)
        i = jnp.where(first, edge - 1 - i, i)
        j = jnp.where(second, edge - 1 - j, j)
        back[c * count : (c + 1) * count, :] = half + i * edge + j
    image = dot_split(halves(source[...]), halves(inverse[...]))
    solved[...] = image
    flat[...] = dot_split(halves(image), halves(coupling[...]))
    swap_blocks(flat, grid, flat.shape[0] // count, columns, count)
    store_faces(grid, back, sides, bottom, top)


def store_faces(grid, back, sides, bottom, top):
    side_count = sides.shape[0]
    count = bottom.shape[0]
    layer = lax.axis_index("gz")
    has_below = (layer > 0).astype(F32)
    has_above = (layer < lax.axis_size("gz") - 1).astype(F32)
    sides[...] = turn(grid[:side_count, :], back[:side_count, :])
    below = slice(side_count, side_count + count)
    bottom[...] = turn(grid[below, :], back[below, :]) * has_below
    above = slice(side_count + count, side_count + 2 * count)
    top[...] = turn(grid[above, :], back[above, :]) * has_above


def send_body(owned, capacity, ids, wanted, sides, send, chooser):
    owner, slot, crossing, rank = second_sides(ids, owned, capacity)
    shape = (send.shape[0], owner.shape[1])
    line = iota(shape, 0)
    place = jnp.where(crossing, owner * (2 * capacity) + rank, -1)
    given = line == place
    first = lax.rem(jnp.concatenate([ids[0:1, :], ids[1:2, :]], axis=1), owned)
    own = lax.rem(line, 2 * capacity) >= capacity
    held = own & (wanted[:, : shape[1]] == first + 1)
    chooser[...] = jnp.concatenate([held, given], axis=1).astype(F32).astype(BF16)
    send[...] = pick(chooser[...], sides[...])


def tables_body(
    owned, capacity, ids, wanted, sides, inverse, coupling, operator,
    partner, taker, sorter, lift, operator_high, operator_low, near
):
    owner, slot, crossing, rank = second_sides(ids, owned, capacity)
    lines = wanted.shape[0]
    shape = (lines, owner.shape[1])
    line = iota(shape, 0)
    place = jnp.where(crossing, owner * (2 * capacity) + capacity + rank, -1)
    given = line == place
    first = lax.rem(jnp.concatenate([ids[0:1, :], ids[1:2, :]], axis=1), owned)
    own = lax.rem(line, 2 * capacity) < capacity
    held = own & (wanted[:, : shape[1]] == first + 1)
    both = jnp.concatenate([held, given], axis=1).astype(F32)
    taker[...] = both.T.astype(BF16)
    here = jnp.where(crossing, -1, slot)
    count = slot.shape[1]
    across = (column_of(first) == here).astype(F32)
    partner[0] = across.astype(BF16)
    partner[1] = across.T.astype(BF16)
    sorter[...] = (iota((owned, count), 0) == first).astype(F32).astype(BF16)
    high, low = halves(dot_split(halves(inverse[...]), halves(coupling[...])))
    lift[0] = high
    lift[1] = low
    high, low = halves(operator[...])
    operator_high[...] = high
    operator_low[...] = low
    add_near(partner, sides, near)


def add_near(partner, sides, near):
    count = sides.shape[0] // 2
    near[:count, :] = pick(partner[0], sides[count:, :])
    near[count:, :] = pick(partner[1], sides[:count, :])


def add_up(sides, near, taker, received, bottom, top, up, down, grid):
    side_count = sides.shape[0]
    count = bottom.shape[0]
    grid[:side_count, :] = (sides[...] + near[...]) + pick(taker[...], received[...])
    grid[side_count : side_count + count, :] = bottom[...] + up[...]
    grid[side_count + count :, :] = top[...] + down[...]


def scales(scale, columns):
    return jnp.concatenate([column_of(scale[...])] * columns, axis=0).astype(F32)


def apply_body(
    sides, near, taker, received, bottom, top, up, down, forward, back, high, low, scale, chooser,
    total, local, local_flat, image, sides_out, bottom_out, top_out, send, flat
):
    count = bottom.shape[0]
    columns = total.shape[0] // count
    rights = flat.shape[0] // count
    add_up(sides, near, taker, received, bottom, top, up, down, total)
    local[...] = turn(total[...], forward[...])
    swap_blocks(local, local_flat, columns, rights, count)
    flat[...] = dot_split(halves(local_flat[...]), (high[...], low[...])) * scales(scale, rights)
    swap_blocks(flat, image, rights, columns, count)
    store_faces(image, back, sides_out, bottom_out, top_out)
    send[...] = pick(chooser[...], sides_out[...])


def dot_across(left, right):
    return lax.dot_general(left, right, (((1,), (1,)), ((), ())), preferred_element_type=F32)


def lifted(flat, lift):
    high, low = halves(flat)
    return dot_across(high, lift[0]) + (dot_across(low, lift[0]) + dot_across(high, lift[1]))


def store_traces(total, sorter, side_traces, top_traces, rights):
    owned = sorter.shape[0]
    count = top_traces.shape[1]
    sides = pick(sorter[...], total[:owned, :]).T
    tops = total[total.shape[0] - count :, :].T
    nodes = sides.shape[0] // rights
    for r in range(rights):
        rows = slice(r * nodes, (r + 1) * nodes)
        side_traces[pl.ds(r, nodes, stride=rights), :] = sides[rows, :]
        top_traces[pl.ds(r, nodes, stride=rights), :] = tops[rows, :]


def beside_body(
    partner, sides, total, local_flat, lift, solved, scale, sorter,
    near, lifted_out, scaled, side_traces, top_traces
):
    rights = solved.shape[0] // scale.shape[1]
    add_near(partner, sides, near)
    lifted_out[...] = lifted(local_flat[...], lift)
    scaled[...] = solved[...] / scales(scale, rights)
    store_traces(total, sorter, side_traces, top_traces, rights)


def after_body(total, local_flat, lift, sorter, lifted_out, side_traces, top_traces):
    lifted_out[...] = lifted(local_flat[...], lift)
    store_traces(total, sorter, side_traces, top_traces, local_flat.shape[0] // top_traces.shape[1])


def total_rows(value):
    return jnp.sum(value, axis=0, keepdims=True)


def grouped(rows, group):
    high, rest = halves(rows)
    middle = rest.astype(F32)
    low = (rows - high.astype(F32) - middle).astype(BF16)
    return dot(high, group) + (dot(rest, group) + dot(low, group))


def stats_body(
    sides, near, taker, received, bottom, top, up, down, forward, high, low, scale,
    total, local, image, total_next, next_flat, stats, next_local, flat, next_image
):
    count = bottom.shape[0]
    columns = total.shape[0] // count
    rights = flat.shape[0] // count
    owned = sides.shape[0] // 2
    lanes = total.shape[1]
    width = lanes // rights
    add_up(sides, near, taker, received, bottom, top, up, down, total_next)
    next_local[...] = turn(total_next[...], forward[...])
    swap_blocks(next_local, next_flat, columns, rights, count)
    flat[...] = dot_split(halves(next_flat[...]), (high[...], low[...])) * scales(scale, rights)
    swap_blocks(flat, next_image, rights, columns, count)
    last = (columns - 1) * count
    b = jnp.concatenate([total[:owned, :], total[last:, :]], axis=0)
    w = jnp.concatenate([total_next[:owned, :], total_next[last:, :]], axis=0)
    group = lax.div(iota((lanes, lanes), 0), width) == lax.div(iota((lanes, lanes), 1), width)
    ww = total_rows(w * w)
    ones = jnp.ones((6, lanes), F32)
    pair = grouped(
        jnp.concatenate([total_rows(b * w), ww, ones], axis=0), group.astype(F32).astype(BF16)
    )
    sigma = jnp.where(pair[1:2] > 0.0, pair[0:1] / pair[1:2], 0.0)
    r = b - sigma * w
    g = local[...] - sigma * next_local[...]
    h = image[...] - sigma * next_image[...]
    every = jnp.concatenate(
        [
            total_rows(b * b),
            total_rows(local[...] * image[...]),
            total_rows(r * r),
            total_rows(r * w),
            ww,
            total_rows(g * h),
            total_rows(g * next_image[...]),
            total_rows(next_local[...] * next_image[...]),
            sigma * (1.0 / width),
            jnp.zeros((16 - STATS, lanes), F32),
        ],
        axis=0,
    )
    out = stats.shape[2]
    spread = lax.div(iota((lanes, out), 0), width) == lax.rem(iota((lanes, out), 1), rights)
    sums = grouped(every, spread.astype(F32).astype(BF16))
    mine = lax.div(iota(sums.shape, 1), rights) == iota(sums.shape, 0)
    packed = jnp.sum(jnp.where(mine, sums, 0.0), axis=0, keepdims=True)
    stats[...] = jnp.broadcast_to(packed[None], stats.shape)


def finish_body(
    stats, side_first, side_next, top_first, top_next, scaled, lifted_first, lifted_next,
    interior, side_traces, top_traces
):
    rights = side_traces.shape[1]
    every = stats[:, 0, :]
    lanes = every.shape[1]

    def quantity(index):
        return every if index == 0 else pltpu.roll(every, lanes - index * rights, 1)

    mu0, mu1 = total_rows(quantity(0)), total_rows(quantity(1))
    alpha = mu0 / mu1
    shift = quantity(8) - alpha
    norm = total_rows(quantity(2) + shift * (2.0 * quantity(3) + shift * quantity(4)))
    energy = total_rows(quantity(5) + shift * (2.0 * quantity(6) + shift * quantity(7)))
    beta = norm / mu0
    alpha_next = norm / (energy - beta * norm / alpha)
    diagonal = iota((rights, lanes), 0) == iota((rights, lanes), 1)

    def column(row):
        return jnp.sum(jnp.where(diagonal, row, 0.0), axis=1, keepdims=True)

    first = column(alpha + alpha_next * (1.0 + beta))
    following = column(-alpha_next * alpha)
    side_traces[...] = first[None] * side_first[...] + following[None] * side_next[...]
    top_traces[...] = first[None] * top_first[...] + following[None] * top_next[...]
    block = scaled.shape[0] // rights
    for r in range(rights):
        rows = slice(r * block, (r + 1) * block)
        interior[rows, :] = scaled[rows, :] - (
            first[r : r + 1, :] * lifted_first[rows, :]
            + following[r : r + 1, :] * lifted_next[rows, :]
        )


def per_device(
    source, interior_inverse, coupling, trace_operator, face_ids, orientation, element_scale
):
    nodes, rights, count = source.shape
    traces = trace_operator.shape[0]
    columns = orientation.shape[1]
    face_nodes = traces // columns
    blocks = lax.axis_size("dev")
    layers = lax.axis_size("gz")
    capacity = count // blocks
    owned = 2 * count
    lines = 2 * blocks * capacity
    flat_rows = rights * count
    lanes = rights * face_nodes
    grid_rows = columns * count
    side_rows = (columns - 2) * count
    ids, codes = face_ids.T, orientation.T
    scale = element_scale.reshape(1, count)
    flat_source = source.transpose(1, 2, 0).reshape(flat_rows, nodes)
    grid = ((grid_rows, lanes), F32)
    faces = [((side_rows, lanes), F32), ((count, lanes), F32), ((count, lanes), F32)]
    flat = ((flat_rows, traces), F32)
    whole = ((flat_rows, nodes), F32)
    table = ((grid_rows, 2 * face_nodes), I32)
    message = ((lines, lanes), F32)
    side_shape = ((face_nodes * rights, owned), F32)
    top_shape = ((face_nodes * rights, count), F32)

    def vmem(entry):
        return pltpu.VMEM(*entry)

    def across(message):
        parts = message.reshape(blocks, 2 * capacity, message.shape[1])
        return lax.all_to_all(parts, "dev", 0, 0, tiled=True).reshape(message.shape)

    def climb(value):
        return lax.ppermute(value, "gz", [(at, (at + 1) % layers) for at in range(layers)])

    def sink(value):
        return lax.ppermute(value, "gz", [((at + 1) % layers, at) for at in range(layers)])

    (wishes,) = call(
        functools.partial(wishes_body, owned, capacity), [((lines, owned), I32)], [ids]
    )
    wanted = across(wishes)
    solved, sides, bottom, top, forward, back = call(
        functools.partial(start_body, face_nodes),
        [whole] + faces + [table, table],
        [flat_source, interior_inverse, coupling, codes],
        [vmem(flat), vmem(grid)],
        flops=6 * flat_rows * nodes * (nodes + traces),
    )
    send, chooser = call(
        functools.partial(send_body, owned, capacity),
        [message, ((lines, side_rows), BF16)],
        [ids, wanted, sides],
        flops=4 * lines * side_rows * lanes,
    )
    up, down, received = climb(top), sink(bottom), across(send)
    partner, taker, sorter, lift, high, low, near = call(
        functools.partial(tables_body, owned, capacity),
        [
            ((2, owned, owned), BF16),
            ((side_rows, lines), BF16),
            ((owned, owned), BF16),
            ((2, nodes, traces), BF16),
            ((traces, traces), BF16),
            ((traces, traces), BF16),
            faces[0],
        ],
        [ids, wanted, sides, interior_inverse, coupling, trace_operator],
        flops=6 * nodes * nodes * traces,
    )
    total, local, local_flat, image, sides, bottom, top, send = call(
        apply_body,
        [grid, grid, flat, grid] + faces + [message],
        [sides, near, taker, received, bottom, top, up, down, forward, back, high, low, scale,
         chooser],
        [vmem(flat)],
        flops=6 * flat_rows * traces * traces,
    )
    up, down, received = climb(top), sink(bottom), across(send)
    near, lifted_first, scaled, side_first, top_first = call(
        beside_body,
        [faces[0], whole, whole, side_shape, top_shape],
        [partner, sides, total, local_flat, lift, solved, scale, sorter],
        flops=6 * flat_rows * traces * nodes,
    )
    total_next, next_flat, stats = call(
        stats_body,
        [grid, flat, ((layers * blocks, 1, 128), F32)],
        [sides, near, taker, received, bottom, top, up, down, forward, high, low, scale, total,
         local, image],
        [vmem(grid), vmem(flat), vmem(grid)],
        flops=6 * flat_rows * traces * traces,
    )
    stats = lax.all_to_all(stats, ("gz", "dev"), 0, 0, tiled=True)
    lifted_next, side_next, top_next = call(
        after_body,
        [whole, side_shape, top_shape],
        [total_next, next_flat, lift, sorter],
        flops=6 * flat_rows * traces * nodes,
    )
    side_form = (face_nodes, rights, owned)
    top_form = (face_nodes, rights, count)
    interior, side_traces, top_traces = call(
        finish_body,
        [whole, (side_form, F32), (top_form, F32)],
        [stats, side_first.reshape(side_form), side_next.reshape(side_form),
         top_first.reshape(top_form), top_next.reshape(top_form), scaled, lifted_first,
         lifted_next],
    )
    interior = interior.reshape(rights, count, nodes).transpose(2, 0, 1)
    return (interior, side_traces, top_traces)


def solution(mesh):
    placed = (
        P(None, None, ("gz", "dev")),
        P(),
        P(),
        P(),
        P(("gz", "dev"), None),
        P(("gz", "dev"), None),
        P(("gz", "dev")),
    )
    return jax.shard_map(
        per_device,
        mesh=mesh,
        in_specs=placed,
        out_specs=(
            P(None, None, ("gz", "dev")),
            P(None, None, ("gz", "dev")),
            P(None, None, ("gz", "dev")),
        ),
        check_vma=False,
    )
```

```python
import functools
import math

import jax
import jax.numpy as jnp
from jax import lax
from jax.experimental import pallas as pl
from jax.experimental.pallas import tpu as pltpu
from jax.sharding import PartitionSpec as P

F32, BF16, I32 = jnp.float32, jnp.bfloat16, jnp.int32
VMEM_BYTES = 24 * 1024 * 1024
STATS = 9


def far(arg):
    return pltpu.with_memory_space_constraint(arg, pltpu.HBM)


class Raw:
    def __init__(self, arg):
        self.arg = arg


def call(body, outs, args, scratch=(), copies=0, flops=0):
    anywhere, near = pl.BlockSpec(memory_space=pl.ANY), pl.BlockSpec(memory_space=pltpu.VMEM)
    scratch = [pltpu.VMEM(*entry) for entry in scratch]
    if copies:
        scratch.append(pltpu.SemaphoreType.DMA((copies,)))
    specs = [anywhere if isinstance(arg, Raw) else near for arg in args]
    args = [far(arg.arg) if isinstance(arg, Raw) else arg for arg in args]
    return pl.pallas_call(
        body,
        out_shape=[
            pltpu.HBM(*out[:2]) if len(out) > 2 else jax.ShapeDtypeStruct(*out) for out in outs
        ],
        in_specs=specs,
        out_specs=[anywhere if out[2:] == ("raw",) else near for out in outs],
        scratch_shapes=scratch,
        compiler_params=pltpu.CompilerParams(vmem_limit_bytes=VMEM_BYTES),
        cost_estimate=pl.CostEstimate(
            flops=flops, bytes_accessed=sum(arg.size * 4 for arg in args), transcendentals=0
        ),
    )(*args)


def begin(source, target, semaphore):
    copy = pltpu.make_async_copy(source, target, semaphore)
    copy.start()
    return copy


def halves(value):
    high = value.astype(BF16)
    return high, (value - high.astype(F32)).astype(BF16)


def dot(left, right):
    return jnp.dot(left, right, preferred_element_type=F32)


def dot_split(left, right):
    return dot(left[0], right[0]) + (dot(left[1], right[0]) + dot(left[0], right[1]))


def pick(onehot, value):
    high, low = halves(value)
    return dot(onehot, high) + dot(onehot, low)


def iota(shape, axis):
    return lax.broadcasted_iota(I32, shape, axis)


def column_of(row):
    size = row.shape[1]
    mask = iota((size, size), 0) == iota((size, size), 1)
    spread = jnp.where(mask, row.astype(F32), 0.0)
    return jnp.sum(spread, axis=1, keepdims=True).astype(I32)


def swap_blocks(source, target, rows, columns, block):
    low = iota((block, 2 * block), 1) < block
    for r in range(0, rows, 2):
        for c in range(0, columns, 2):
            lanes = slice(c * block, (c + 2) * block)
            first = source[r * block : (r + 1) * block, lanes]
            second = source[(r + 1) * block : (r + 2) * block, lanes]
            lanes = slice(r * block, (r + 2) * block)
            target[c * block : (c + 1) * block, lanes] = jnp.where(
                low, first, pltpu.roll(second, block, 1)
            )
            target[(c + 1) * block : (c + 2) * block, lanes] = jnp.where(
                low, pltpu.roll(first, block, 1), second
            )


def turn(value, table):
    width = table.shape[1]
    return jnp.concatenate(
        [
            jnp.take_along_axis(
                value[:, at : at + width], table, axis=1, mode="promise_in_bounds"
            )
            for at in range(0, value.shape[1], width)
        ],
        axis=1,
    )


def wishes_body(owned, capacity, faces, out, marks, ids, semaphores):
    begin(faces, ids, semaphores.at[0]).wait()
    row = jnp.concatenate([ids[2:3, :], ids[3:4, :]], axis=1)
    owner, slot = lax.div(row, owned), lax.rem(row, owned)
    count = row.shape[1]
    crossing = owner != lax.axis_index("dev")
    same = (column_of(owner) == owner) & (iota((count, count), 0) < iota((count, count), 1))
    rank = jnp.sum(jnp.where(same, 1.0, 0.0), axis=0, keepdims=True).astype(I32)
    first = lax.rem(jnp.concatenate([ids[0:1, :], ids[1:2, :]], axis=1), owned)
    place = jnp.where(crossing, owner * (2 * capacity) + rank, -1)
    here = jnp.where(crossing, -1, slot)
    marks[...] = jnp.concatenate(
        [place, first, here, jnp.zeros((marks.shape[0] - 3, count), I32)], axis=0
    )
    shape = (out.shape[0], count)
    line = iota(shape, 0)
    line = line - jnp.where(lax.rem(line, 2 * capacity) >= capacity, capacity, 0)
    chosen = jnp.where(line == place, (slot + 1).astype(F32), 0.0)
    out[...] = jnp.broadcast_to(
        jnp.sum(chosen, axis=1, keepdims=True).astype(I32), out.shape
    )


def start_body(
    face_nodes, source, inverse, coupling, codes, scales, solved, sides, bottom, top, table,
    source_here, inverse_here, coupling_here, orientation, scale, image, flat, grid, semaphores
):
    small = [begin(codes, orientation, semaphores.at[4]), begin(scales, scale, semaphores.at[5])]
    reads = [
        begin(source, source_here, semaphores.at[0]),
        begin(inverse, inverse_here, semaphores.at[1]),
        begin(coupling, coupling_here, semaphores.at[2]),
    ]
    columns = orientation.shape[0]
    count = orientation.shape[1]
    edge = math.isqrt(face_nodes)
    pair = 2 * face_nodes
    lane = iota((count, pair), 1)
    half = lane - lax.rem(lane, face_nodes)
    node = lax.rem(lane, face_nodes)
    a, b = lax.div(node, edge), lax.rem(node, edge)
    for read in small:
        read.wait()
    scaled = column_of(scale[...]) * (pair * pair)
    for c in range(columns):
        code = jnp.broadcast_to(column_of(orientation[c : c + 1, :]), (count, pair))
        swapped = (code & 4) != 0
        first = (code & 2) != 0
        second = (code & 1) != 0
        i = jnp.where(first, edge - 1 - a, a)
        j = jnp.where(second, edge - 1 - b, b)
        forward = half + jnp.where(swapped, j * edge + i, i * edge + j)
        i, j = jnp.where(swapped, b, a), jnp.where(swapped, a, b)
        i = jnp.where(first, edge - 1 - i, i)
        j = jnp.where(second, edge - 1 - j, j)
        back = half + i * edge + j
        table[c * count : (c + 1) * count, :] = forward + pair * back + scaled
    reads[0].wait()
    reads[1].wait()
    image[...] = dot_split(halves(source_here[...]), halves(inverse_here[...]))
    write = begin(image, solved, semaphores.at[3])
    reads[2].wait()
    flat[...] = dot_split(halves(image[...]), halves(coupling_here[...]))
    swap_blocks(flat, grid, flat.shape[0] // count, columns, count)
    store_faces(grid, table, sides, bottom, top)
    write.wait()


def forward_of(table):
    return lax.rem(table, table.shape[1])


def back_of(table):
    return lax.rem(lax.div(table, table.shape[1]), table.shape[1])


def scale_of(table):
    return lax.div(table, table.shape[1] * table.shape[1]).astype(F32)


def store_faces(grid, table, sides, bottom, top):
    side_count = sides.shape[0]
    count = bottom.shape[0]
    layer = lax.axis_index("gz")
    has_below = (layer > 0).astype(F32)
    has_above = (layer < lax.axis_size("gz") - 1).astype(F32)
    sides[...] = turn(grid[:side_count, :], back_of(table[:side_count, :]))
    below = slice(side_count, side_count + count)
    bottom[...] = turn(grid[below, :], back_of(table[below, :])) * has_below
    above = slice(side_count + count, side_count + 2 * count)
    top[...] = turn(grid[above, :], back_of(table[above, :])) * has_above


def places(capacity, marks, wanted):
    place, first = marks[0:1, :], marks[1:2, :]
    line = iota(wanted.shape, 0)
    named = wanted[...] == first + 1
    later = lax.rem(line, 2 * capacity) >= capacity
    taken = jnp.concatenate([later & named, line == place], axis=1).astype(F32)
    given = jnp.concatenate([~later & named, later & (line - capacity == place)], axis=1)
    return taken, given.astype(F32)


def send_body(capacity, marks, wanted, sides, send):
    taken, _ = places(capacity, marks, wanted)
    send[...] = pick(taken.astype(BF16), sides[...])


class Maps:
    def __init__(self, ref, owned):
        self.ref, self.owned = ref, owned

    def part(self, index, width=1):
        return self.ref[:, index * self.owned : (index + width) * self.owned]

    def message(self, sides):
        return pick(self.part(0, 2), sides)

    def with_partners(self, sides):
        near, far_side = sides[: self.owned, :], sides[self.owned :, :]
        return near + pick(self.part(4), far_side), far_side + pick(self.part(5), near)

    def from_message(self, received):
        high, low = halves(received)
        first, second = self.part(2), self.part(3)
        return dot(first, high) + dot(first, low), dot(second, high) + dot(second, low)

    def by_face(self, sides):
        return pick(self.part(6), sides)


def tables_body(
    owned, capacity, marks, wanted, sides, inverse, coupling, maps, base, lift
):
    taken, given = places(capacity, marks, wanted)
    first, here = marks[1:2, :], marks[2:3, :]
    across = (column_of(first) == here).astype(F32)
    sorter = (iota((owned, owned), 0) == first).astype(F32)
    maps[...] = jnp.concatenate(
        [taken, given[:, :owned].T, given[:, owned:].T, across, across.T, sorter], axis=1
    ).astype(BF16)
    base[:owned, :], base[owned:, :] = Maps(maps, owned).with_partners(sides[...])
    high, low = halves(dot_split(halves(inverse[...]), halves(coupling[...])))
    lift[0] = high
    lift[1] = low


def add_up(base, maps, received, bottom, top, up, down, grid):
    owned = maps.owned
    count = bottom.shape[0]
    first, second = maps.from_message(received[...])
    grid[:owned, :] = base[0] + first
    grid[owned : 2 * owned, :] = base[1] + second
    grid[2 * owned : 2 * owned + count, :] = bottom[...] + up[...]
    grid[2 * owned + count :, :] = top[...] + down[...]


def operate(total, table, operator, read, local, flat, image, count):
    columns = total.shape[0] // count
    rights = flat.shape[0] // count
    local[...] = turn(total[...], forward_of(table[...]))
    swap_blocks(local, flat, columns, rights, count)
    read.wait()
    flat[...] = dot_split(halves(flat[...]), halves(operator[...]))
    swap_blocks(flat, image, rights, columns, count)
    scale = scale_of(table[...])
    image[...] = image[...] * jnp.concatenate([scale] * (rights // 2), axis=1)


def apply_body(
    owned, base, maps, received, bottom, top, up, down, table, operator,
    total_out, sides_out, bottom_out, top_out, send, total, operator_here, grid, flat, semaphores
):
    maps = Maps(maps, owned)
    read = begin(operator, operator_here, semaphores.at[0])
    add_up((base[:owned, :], base[owned:, :]), maps, received, bottom, top, up, down, total)
    write = begin(total, total_out, semaphores.at[1])
    operate(total, table, operator_here, read, grid, flat, grid, bottom.shape[0])
    store_faces(grid, table, sides_out, bottom_out, top_out)
    send[...] = maps.message(sides_out[...])
    write.wait()


def dot_across(left, right):
    return lax.dot_general(left, right, (((1,), (1,)), ((), ())), preferred_element_type=F32)


def lifted(flat, lift):
    high, low = halves(flat)
    return dot_across(high, lift[0]) + (dot_across(low, lift[0]) + dot_across(high, lift[1]))


def store_traces(total, maps, side_traces, top_traces, rights):
    count = top_traces.shape[1]
    sides = maps.by_face(total[: maps.owned, :]).T
    tops = total[total.shape[0] - count :, :].T
    nodes = sides.shape[0] // rights
    for r in range(rights):
        rows = slice(r * nodes, (r + 1) * nodes)
        side_traces[pl.ds(r, nodes, stride=rights), :] = sides[rows, :]
        top_traces[pl.ds(r, nodes, stride=rights), :] = tops[rows, :]


def lift_total(total, table, lift, count, grid, flat):
    grid[...] = turn(total[...], forward_of(table[...]))
    swap_blocks(grid, flat, total.shape[0] // count, flat.shape[0] // count, count)
    return lifted(flat[...], lift)


def beside_body(
    owned, total, table, lift, solved, maps,
    lifted_out, scaled, side_traces, top_traces, grid, flat
):
    count = top_traces.shape[1]
    rights = solved.shape[0] // count
    lifted_out[...] = lift_total(total, table, lift, count, grid, flat)
    scale = jnp.concatenate([scale_of(table[:count, :])] * rights, axis=0)
    copies = solved.shape[1] // scale.shape[1]
    scaled[...] = solved[...] / jnp.concatenate([scale] * copies, axis=1)
    store_traces(total, Maps(maps, owned), side_traces, top_traces, rights)


def after_body(
    owned, total, table, lift, maps, lifted_first, lifted_out, side_traces, top_traces, first_out,
    grid, flat, semaphores
):
    count = top_traces.shape[1]
    read = begin(lifted_first, first_out, semaphores.at[0])
    lifted_out[...] = lift_total(total, table, lift, count, grid, flat)
    store_traces(total, Maps(maps, owned), side_traces, top_traces, flat.shape[0] // count)
    read.wait()


def total_rows(value):
    return jnp.sum(value, axis=0, keepdims=True)


def grouped(rows, group):
    high, rest = halves(rows)
    middle = rest.astype(F32)
    low = (rows - high.astype(F32) - middle).astype(BF16)
    return dot(high, group) + (dot(rest, group) + dot(low, group))


def stats_body(
    owned, sides, maps, received, bottom, top, up, down, table, operator, total_in,
    next_out, stats, total, total_next, operator_here, grid, flat, semaphores
):
    count = bottom.shape[0]
    columns = total.shape[0] // count
    rights = flat.shape[0] // count
    lanes = total.shape[1]
    width = lanes // rights
    maps = Maps(maps, owned)
    read = begin(operator, operator_here, semaphores.at[0])
    read_total = begin(total_in, total, semaphores.at[1])
    add_up(maps.with_partners(sides[...]), maps, received, bottom, top, up, down, total_next)
    write = begin(total_next, next_out, semaphores.at[2])
    operate(total_next, table, operator_here, read, grid, flat, grid, count)
    read_total.wait()
    next_image = turn(grid[...], back_of(table[...]))
    image = jnp.concatenate([sides[...], bottom[...], top[...]], axis=0)
    last = (columns - 1) * count
    b = jnp.concatenate([total[:owned, :], total[last:, :]], axis=0)
    w = jnp.concatenate([total_next[:owned, :], total_next[last:, :]], axis=0)
    group = lax.div(iota((lanes, lanes), 0), width) == lax.div(iota((lanes, lanes), 1), width)
    ww = total_rows(w * w)
    ones = jnp.ones((6, lanes), F32)
    pair = grouped(
        jnp.concatenate([total_rows(b * w), ww, ones], axis=0), group.astype(F32).astype(BF16)
    )
    sigma = jnp.where(pair[1:2] > 0.0, pair[0:1] / pair[1:2], 0.0)
    r = b - sigma * w
    g = total[...] - sigma * total_next[...]
    h = image - sigma * next_image
    every = jnp.concatenate(
        [
            total_rows(b * b),
            total_rows(total[...] * image),
            total_rows(r * r),
            total_rows(r * w),
            ww,
            total_rows(g * h),
            total_rows(g * next_image),
            total_rows(total_next[...] * next_image),
            sigma * (1.0 / width),
            jnp.zeros((16 - STATS, lanes), F32),
        ],
        axis=0,
    )
    out = stats.shape[2]
    spread = lax.div(iota((lanes, out), 0), width) == lax.rem(iota((lanes, out), 1), rights)
    sums = grouped(every, spread.astype(F32).astype(BF16))
    mine = lax.div(iota(sums.shape, 1), rights) == iota(sums.shape, 0)
    packed = jnp.sum(jnp.where(mine, sums, 0.0), axis=0, keepdims=True)
    stats[...] = jnp.broadcast_to(packed[None], stats.shape)
    write.wait()


def finish_body(
    stats, side_first, side_next, top_first, top_next, scaled, lifted_first, lifted_next,
    interior, side_traces, top_traces, scaled_here, side_here, top_here, semaphores
):
    rights = side_traces.shape[1]
    block = scaled.shape[0] // rights
    parts = [pl.ds(r * block, block) for r in range(rights)]
    reads = [
        begin(scaled.at[part], scaled_here.at[part], semaphores.at[r])
        for r, part in enumerate(parts)
    ]
    reads.append(begin(side_first, side_here, semaphores.at[rights]))
    reads.append(begin(top_first, top_here, semaphores.at[rights + 1]))
    every = stats[:, 0, :]
    lanes = every.shape[1]

    def quantity(index):
        return every if index == 0 else pltpu.roll(every, lanes - index * rights, 1)

    mu0, mu1 = total_rows(quantity(0)), total_rows(quantity(1))
    alpha = mu0 / mu1
    shift = quantity(8) - alpha
    norm = total_rows(quantity(2) + shift * (2.0 * quantity(3) + shift * quantity(4)))
    energy = total_rows(quantity(5) + shift * (2.0 * quantity(6) + shift * quantity(7)))
    beta = norm / mu0
    alpha_next = norm / (energy - beta * norm / alpha)
    diagonal = iota((rights, lanes), 0) == iota((rights, lanes), 1)

    def column(row):
        return jnp.sum(jnp.where(diagonal, row, 0.0), axis=1, keepdims=True)

    first = column(alpha + alpha_next * (1.0 + beta))
    following = column(-alpha_next * alpha)
    writes = []
    for r, part in enumerate(parts):
        reads[r].wait()
        scaled_here[part, :] = scaled_here[part, :] - (
            first[r : r + 1, :] * lifted_first[part, :]
            + following[r : r + 1, :] * lifted_next[part, :]
        )
        writes.append(begin(scaled_here.at[part], interior.at[part], semaphores.at[rights + 2 + r]))
    reads[rights].wait()
    side_here[...] = first[None] * side_here[...] + following[None] * side_next[...]
    writes.append(begin(side_here, side_traces, semaphores.at[2 * rights + 2]))
    reads[rights + 1].wait()
    top_here[...] = first[None] * top_here[...] + following[None] * top_next[...]
    writes.append(begin(top_here, top_traces, semaphores.at[2 * rights + 3]))
    for write in writes:
        write.wait()


def per_device(
    source, interior_inverse, coupling, trace_operator, face_ids, orientation, element_scale
):
    nodes, rights, count = source.shape
    traces = trace_operator.shape[0]
    columns = orientation.shape[1]
    face_nodes = traces // columns
    blocks = lax.axis_size("dev")
    layers = lax.axis_size("gz")
    capacity = count // blocks
    owned = 2 * count
    lines = 2 * blocks * capacity
    flat_rows = rights * count
    lanes = rights * face_nodes
    grid_rows = columns * count
    side_rows = (columns - 2) * count
    ids, codes = face_ids.T, orientation.T
    scale = element_scale.reshape(1, count)
    flat_source = source.transpose(1, 2, 0).reshape(flat_rows, nodes)
    grid = ((grid_rows, lanes), F32)
    faces = [((side_rows, lanes), F32), ((count, lanes), F32), ((count, lanes), F32)]
    flat = ((flat_rows, traces), F32)
    whole = ((flat_rows, nodes), F32)
    table = ((grid_rows, 2 * face_nodes), I32)
    message = ((lines, lanes), F32)
    side_shape = ((face_nodes * rights, owned), F32)
    top_shape = ((face_nodes * rights, count), F32)

    def across(message):
        parts = message.reshape(blocks, 2 * capacity, message.shape[1])
        return lax.all_to_all(parts, "dev", 0, 0, tiled=True).reshape(message.shape)

    def climb(value):
        return lax.ppermute(value, "gz", [(at, (at + 1) % layers) for at in range(layers)])

    def sink(value):
        return lax.ppermute(value, "gz", [((at + 1) % layers, at) for at in range(layers)])

    wishes, marks = call(
        functools.partial(wishes_body, owned, capacity),
        [((lines, owned), I32), ((8, owned), I32)],
        [Raw(ids)],
        [(ids.shape, I32)],
        copies=1,
    )
    wanted = across(wishes)
    solved, sides, bottom, top, table = call(
        functools.partial(start_body, face_nodes),
        [whole + ("raw",)] + faces + [table],
        [Raw(flat_source), Raw(interior_inverse), Raw(coupling), Raw(codes), Raw(scale)],
        [whole, ((nodes, nodes), F32), ((nodes, traces), F32), (codes.shape, I32),
         (scale.shape, I32), whole, flat, grid],
        copies=6,
        flops=6 * flat_rows * nodes * (nodes + traces),
    )
    (send,) = call(
        functools.partial(send_body, capacity),
        [message],
        [marks, wanted, sides],
        flops=4 * lines * side_rows * lanes,
    )
    up, down, received = climb(top), sink(bottom), across(send)
    maps, base, lift = call(
        functools.partial(tables_body, owned, capacity),
        [((lines, 7 * owned), BF16), faces[0], ((2, nodes, traces), BF16, "far")],
        [marks, wanted, sides, far(interior_inverse), far(coupling)],
        flops=6 * nodes * nodes * traces,
    )
    square = ((traces, traces), F32)
    total, sides, bottom, top, send = call(
        functools.partial(apply_body, owned),
        [grid + ("raw",)] + faces + [message],
        [base, maps, received, bottom, top, up, down, table, Raw(trace_operator)],
        [grid, square, grid, flat],
        copies=2,
        flops=6 * flat_rows * traces * traces,
    )
    up, down, received = climb(top), sink(bottom), across(send)
    lifted_first, scaled, side_first, top_first = call(
        functools.partial(beside_body, owned),
        [whole + ("far",), whole + ("far",), side_shape + ("far",), top_shape + ("far",)],
        [far(total), table, far(lift), far(solved), maps],
        [grid, flat],
        flops=6 * flat_rows * traces * nodes,
    )
    total_next, stats = call(
        functools.partial(stats_body, owned),
        [grid + ("raw",), ((layers * blocks, 1, 128), F32)],
        [sides, maps, received, bottom, top, up, down, table, Raw(trace_operator),
         Raw(total)],
        [grid, grid, square, grid, flat],
        copies=3,
        flops=6 * flat_rows * traces * traces,
    )
    stats = lax.all_to_all(stats, ("gz", "dev"), 0, 0, tiled=True)
    lifted_next, side_next, top_next, lifted_first = call(
        functools.partial(after_body, owned),
        [whole, side_shape, top_shape, whole],
        [far(total_next), table, far(lift), maps, Raw(lifted_first)],
        [grid, flat],
        copies=1,
        flops=6 * flat_rows * traces * nodes,
    )
    side_form = ((face_nodes, rights, owned), F32)
    top_form = ((face_nodes, rights, count), F32)
    interior, side_traces, top_traces = call(
        finish_body,
        [whole + ("raw",), side_form + ("raw",), top_form + ("raw",)],
        [stats, Raw(side_first.reshape(side_form[0])), side_next.reshape(side_form[0]),
         Raw(top_first.reshape(top_form[0])), top_next.reshape(top_form[0]), Raw(scaled),
         lifted_first, lifted_next],
        [whole, side_form, top_form],
        copies=2 * rights + 4,
    )
    interior = interior.reshape(rights, count, nodes).transpose(2, 0, 1)
    return (interior, side_traces, top_traces)


def solution(mesh):
    placed = (
        P(None, None, ("gz", "dev")),
        P(),
        P(),
        P(),
        P(("gz", "dev"), None),
        P(("gz", "dev"), None),
        P(("gz", "dev")),
    )
    return jax.shard_map(
        per_device,
        mesh=mesh,
        in_specs=placed,
        out_specs=(
            P(None, None, ("gz", "dev")),
            P(None, None, ("gz", "dev")),
            P(None, None, ("gz", "dev")),
        ),
        check_vma=False,
    )
```

```python
import functools
import math

import jax
import jax.numpy as jnp
from jax import lax
from jax.experimental import pallas as pl
from jax.experimental.pallas import tpu as pltpu
from jax.sharding import PartitionSpec as P

F32, BF16, I32 = jnp.float32, jnp.bfloat16, jnp.int32
VMEM_BYTES = 24 * 1024 * 1024
STATS = 9


def far(arg):
    return pltpu.with_memory_space_constraint(arg, pltpu.HBM)


class Raw:
    def __init__(self, arg):
        self.arg = arg


def call(body, outs, args, scratch=(), copies=0, flops=0):
    anywhere, near = pl.BlockSpec(memory_space=pl.ANY), pl.BlockSpec(memory_space=pltpu.VMEM)
    scratch = [pltpu.VMEM(*entry) for entry in scratch]
    if copies:
        scratch.append(pltpu.SemaphoreType.DMA((copies,)))
    specs = [anywhere if isinstance(arg, Raw) else near for arg in args]
    args = [far(arg.arg) if isinstance(arg, Raw) else arg for arg in args]
    return pl.pallas_call(
        body,
        out_shape=[
            pltpu.HBM(*out[:2]) if len(out) > 2 else jax.ShapeDtypeStruct(*out) for out in outs
        ],
        in_specs=specs,
        out_specs=[anywhere if out[2:] == ("raw",) else near for out in outs],
        scratch_shapes=scratch,
        compiler_params=pltpu.CompilerParams(vmem_limit_bytes=VMEM_BYTES),
        cost_estimate=pl.CostEstimate(
            flops=flops, bytes_accessed=sum(arg.size * 4 for arg in args), transcendentals=0
        ),
    )(*args)


def begin(source, target, semaphore):
    copy = pltpu.make_async_copy(source, target, semaphore)
    copy.start()
    return copy


def halves(value):
    high = value.astype(BF16)
    return high, (value - high.astype(F32)).astype(BF16)


def dot(left, right):
    return jnp.dot(left, right, preferred_element_type=F32)


def dot_split(left, right):
    rows = left[0].shape[0]
    both = dot(jnp.concatenate(left, axis=0), right[0])
    return both[:rows, :] + (both[rows:, :] + dot(left[0], right[1]))


def pick(onehot, value):
    high, low = halves(value)
    return dot(onehot, high) + dot(onehot, low)


def iota(shape, axis):
    return lax.broadcasted_iota(I32, shape, axis)


def column_of(row):
    size = row.shape[1]
    mask = iota((size, size), 0) == iota((size, size), 1)
    spread = jnp.where(mask, row.astype(F32), 0.0)
    return jnp.sum(spread, axis=1, keepdims=True).astype(I32)


def gather_lanes(value, table):
    return jnp.take_along_axis(value, table, axis=1, mode="promise_in_bounds")


def flip_halves(value):
    return pltpu.roll(value, value.shape[1] // 2, 1)


def lower_half(value):
    return iota(value.shape, 1) < value.shape[1] // 2


def to_flat(total, table, flat, count, pairs):
    width = table.shape[1]
    for c in range(0, total.shape[0] // count, 2):
        rows = slice(c * count, (c + 1) * count)
        rows_next = slice((c + 1) * count, (c + 2) * count)
        forward, forward_next = forward_of(table[rows, :]), forward_of(table[rows_next, :])
        for pair in pairs:
            lanes = slice(pair * width, (pair + 1) * width)
            first = gather_lanes(total[rows, lanes], forward)
            second = gather_lanes(total[rows_next, lanes], forward_next)
            low = lower_half(first)
            at = 2 * pair * count
            lanes = slice(c // 2 * width, (c // 2 + 1) * width)
            flat[at : at + count, lanes] = jnp.where(low, first, second)
            flat[at + count : at + 2 * count, lanes] = flip_halves(jnp.where(low, second, first))


def from_flat(flat, table, placed, count, pairs, columns):
    width = table.shape[1]
    for c in columns[::2]:
        back = back_of(table[c * count : (c + 1) * count, :])
        back_next = back_of(table[(c + 1) * count : (c + 2) * count, :])
        for pair in pairs:
            at = 2 * pair * count
            lanes = slice(c // 2 * width, (c // 2 + 1) * width)
            first = flat[at : at + count, lanes]
            second = flip_halves(flat[at + count : at + 2 * count, lanes])
            low = lower_half(first)
            lanes = slice(pair * width, (pair + 1) * width)
            placed(c, lanes, gather_lanes(jnp.where(low, first, second), back))
            placed(c + 1, lanes, gather_lanes(jnp.where(low, second, first), back_next))


def wishes_body(owned, capacity, faces, out, marks, ids, semaphores):
    begin(faces, ids, semaphores.at[0]).wait()
    row = jnp.concatenate([ids[2:3, :], ids[3:4, :]], axis=1)
    owner, slot = lax.div(row, owned), lax.rem(row, owned)
    count = row.shape[1]
    crossing = owner != lax.axis_index("dev")
    same = (column_of(owner) == owner) & (iota((count, count), 0) < iota((count, count), 1))
    rank = jnp.sum(jnp.where(same, 1.0, 0.0), axis=0, keepdims=True).astype(I32)
    first = lax.rem(jnp.concatenate([ids[0:1, :], ids[1:2, :]], axis=1), owned)
    place = jnp.where(crossing, owner * (2 * capacity) + rank, -1)
    here = jnp.where(crossing, -1, slot)
    marks[...] = jnp.concatenate(
        [place, first, here, jnp.zeros((marks.shape[0] - 3, count), I32)], axis=0
    )
    shape = (out.shape[0], count)
    line = iota(shape, 0)
    line = line - jnp.where(lax.rem(line, 2 * capacity) >= capacity, capacity, 0)
    chosen = jnp.where(line == place, (slot + 1).astype(F32), 0.0)
    out[...] = jnp.broadcast_to(
        jnp.sum(chosen, axis=1, keepdims=True).astype(I32), out.shape
    )


def start_body(
    face_nodes, source, inverse, coupling, codes, scales, solved, sides, bottom, top, table,
    source_here, inverse_here, coupling_here, orientation, scale, image, flat, semaphores
):
    small = [begin(codes, orientation, semaphores.at[4]), begin(scales, scale, semaphores.at[5])]
    reads = [
        begin(source, source_here, semaphores.at[0]),
        begin(inverse, inverse_here, semaphores.at[1]),
        begin(coupling, coupling_here, semaphores.at[2]),
    ]
    columns = orientation.shape[0]
    count = orientation.shape[1]
    edge = math.isqrt(face_nodes)
    pair = 2 * face_nodes
    lane = iota((count, pair), 1)
    half = lane - lax.rem(lane, face_nodes)
    node = lax.rem(lane, face_nodes)
    a, b = lax.div(node, edge), lax.rem(node, edge)
    for read in small:
        read.wait()
    scaled = column_of(scale[...]) * (pair * pair)
    for c in range(columns):
        turned = half if c % 2 == 0 else face_nodes - half
        code = jnp.broadcast_to(column_of(orientation[c : c + 1, :]), (count, pair))
        swapped = (code & 4) != 0
        first = (code & 2) != 0
        second = (code & 1) != 0
        i = jnp.where(first, edge - 1 - a, a)
        j = jnp.where(second, edge - 1 - b, b)
        forward = turned + jnp.where(swapped, j * edge + i, i * edge + j)
        i, j = jnp.where(swapped, b, a), jnp.where(swapped, a, b)
        i = jnp.where(first, edge - 1 - i, i)
        j = jnp.where(second, edge - 1 - j, j)
        back = turned + i * edge + j
        table[c * count : (c + 1) * count, :] = forward + pair * back + scaled
    has_below, has_above = layer_masks()
    side_columns = columns - 2

    def placed(column, lanes, value):
        if column < side_columns:
            sides[column * count : (column + 1) * count, lanes] = value
        elif column == side_columns:
            bottom[:, lanes] = value * has_below
        else:
            top[:, lanes] = value * has_above

    reads[0].wait()
    reads[1].wait()
    pairs = sides.shape[1] // pair
    parts = [range(0, pairs // 2), range(pairs // 2, pairs)]
    split = halves(inverse_here[...])
    split_coupling = None
    for part in parts:
        rows = slice(2 * part[0] * count, 2 * (part[-1] + 1) * count)
        image[rows, :] = dot_split(halves(source_here[rows, :]), split)
        if split_coupling is None:
            reads[2].wait()
            split_coupling = halves(coupling_here[...])
        flat[rows, :] = dot_split(halves(image[rows, :]), split_coupling)
    write = begin(image, solved, semaphores.at[3])
    for part in parts:
        from_flat(flat, table, placed, count, part, range(columns))
    write.wait()


def forward_of(table):
    return table & (table.shape[1] - 1)


def back_of(table):
    bits = table.shape[1].bit_length() - 1
    return (table >> bits) & (table.shape[1] - 1)


def scale_of(table):
    bits = table.shape[1].bit_length() - 1
    return (table >> (2 * bits)).astype(F32)


def places(capacity, marks, wanted):
    place, first = marks[0:1, :], marks[1:2, :]
    line = iota(wanted.shape, 0)
    named = wanted[...] == first + 1
    later = lax.rem(line, 2 * capacity) >= capacity
    taken = jnp.concatenate([later & named, line == place], axis=1).astype(F32)
    given = jnp.concatenate([~later & named, later & (line - capacity == place)], axis=1)
    return taken, given.astype(F32)


def send_body(capacity, marks, wanted, sides, send):
    taken, _ = places(capacity, marks, wanted)
    send[...] = pick(taken.astype(BF16), sides[...])


class Maps:
    def __init__(self, ref, owned):
        self.ref, self.owned = ref, owned

    def part(self, index, width=1):
        return self.ref[:, index * self.owned : (index + width) * self.owned]

    def message(self, sides):
        return pick(self.part(0, 2), sides)

    def with_partners(self, sides):
        near, far_side = sides[: self.owned, :], sides[self.owned :, :]
        return near + pick(self.part(4), far_side), far_side + pick(self.part(5), near)

    def from_message(self, received):
        return pick(self.part(2), received), pick(self.part(3), received)

    def by_face(self, sides):
        return pick(self.part(6), sides)


def tables_body(
    owned, capacity, marks, wanted, sides, inverse, coupling, operator, maps, base, lift, split
):
    taken, given = places(capacity, marks, wanted)
    first, here = marks[1:2, :], marks[2:3, :]
    across = (column_of(first) == here).astype(F32)
    sorter = (iota((owned, owned), 0) == first).astype(F32)
    maps[...] = jnp.concatenate(
        [taken, given[:, :owned].T, given[:, owned:].T, across, across.T, sorter], axis=1
    ).astype(BF16)
    base[:owned, :], base[owned:, :] = Maps(maps, owned).with_partners(sides[...])
    high, low = halves(dot_split(halves(inverse[...]), halves(coupling[...])))
    lift[0] = high
    lift[1] = low
    split[0], split[1] = halves(operator[...])


def add_up(base, maps, received, bottom, top, up, down, total):
    owned = maps.owned
    count = bottom.shape[0]
    total[2 * owned : 2 * owned + count, :] = bottom[...] + up[...]
    total[2 * owned + count :, :] = top[...] + down[...]
    first, second = maps.from_message(received[...])
    total[:owned, :] = base[:owned, :] + first
    total[owned : 2 * owned, :] = base[owned : 2 * owned, :] + second


def own_faces(total, owned, count):
    return jnp.concatenate([total[:owned, :], total[total.shape[0] - count :, :]], axis=0)


def operate(total, table, split, flat, image, count, turned):
    pairs = total.shape[1] // table.shape[1]
    scale = scale_of(table[:count, :])
    scale = jnp.concatenate([scale] * (flat.shape[1] // scale.shape[1]), axis=1)
    parts = [range(0, pairs // 2), range(pairs // 2, pairs)]
    for part in parts:
        to_flat(total, table, flat, count, part)
        rows = slice(2 * part[0] * count, 2 * (part[-1] + 1) * count)
        turned(pl.ds(rows.start, rows.stop - rows.start))
        product = dot_split(halves(flat[rows, :]), (split[0], split[1]))
        image[rows, :] = product * jnp.concatenate([scale] * (product.shape[0] // count), axis=0)
    return parts


def layer_masks():
    layer = lax.axis_index("gz")
    return (layer > 0).astype(F32), (layer < lax.axis_size("gz") - 1).astype(F32)


def apply_body(
    owned, base, maps, received, bottom, top, up, down, table, split,
    mine, flat_out, sides_out, bottom_out, top_out, send,
    total, mine_here, flat, image, message, semaphores
):
    count = bottom.shape[0]
    maps = Maps(maps, owned)
    add_up(base, maps, received, bottom, top, up, down, total)
    mine_here[...] = own_faces(total, owned, count)
    writes = [begin(mine_here, mine, semaphores.at[0])]
    has_below, has_above = layer_masks()
    columns = total.shape[0] // count
    side_columns = columns - 2

    def placed(column, lanes, value):
        if column < side_columns:
            sides_out[column * count : (column + 1) * count, lanes] = value
        elif column == side_columns:
            bottom_out[:, lanes] = value * has_below
        else:
            top_out[:, lanes] = value * has_above

    def turned(rows):
        writes.append(begin(flat.at[rows], flat_out.at[rows], semaphores.at[len(writes)]))

    parts = operate(total, table, split, flat, image, count, turned)
    for part in parts:
        from_flat(image, table, placed, count, part, range(side_columns))
        lanes = slice(part[0] * table.shape[1], (part[-1] + 1) * table.shape[1])
        message[:, lanes] = maps.message(sides_out[:, lanes])
        writes.append(
            begin(message.at[:, lanes], send.at[:, lanes], semaphores.at[len(writes)])
        )
    for part in parts:
        from_flat(image, table, placed, count, part, range(side_columns, columns))
    for write in writes:
        write.wait()


def dot_across(left, right):
    return lax.dot_general(left, right, (((1,), (1,)), ((), ())), preferred_element_type=F32)


def lifted(flat, lift):
    high, low = halves(flat)
    return dot_across(high, lift[0]) + (dot_across(low, lift[0]) + dot_across(high, lift[1]))


def store_traces(mine, maps, side_traces, top_traces, rights):
    sides = maps.by_face(mine[: maps.owned, :]).T
    tops = mine[maps.owned :, :].T
    nodes = sides.shape[0] // rights
    for r in range(rights):
        rows = slice(r * nodes, (r + 1) * nodes)
        side_traces[pl.ds(r, nodes, stride=rights), :] = sides[rows, :]
        top_traces[pl.ds(r, nodes, stride=rights), :] = tops[rows, :]


def by_right(rows, rights):
    width = 2 * rows.shape[1] // rights
    low = iota((1, width), 1) < width // 2
    tiles = [rows[:, at : at + width] for at in range(0, rows.shape[1], width)]
    return [jnp.where(low == (r % 2 == 0), tiles[r // 2], 0.0) for r in range(rights)]


def beside_body(
    owned, mine, flat, table, lift, solved, maps, sides, bottom, top,
    lifted_out, scaled, side_traces, top_traces, image_out, base, known, shifts,
    placed, image, semaphores
):
    count = top_traces.shape[1]
    rights = solved.shape[0] // count
    maps = Maps(maps, owned)
    placed[: 2 * owned, :] = sides[...]
    placed[2 * owned : 2 * owned + count, :] = bottom[...]
    placed[2 * owned + count :, :] = top[...]
    to_flat(placed, table, image, count, range(rights // 2))
    write = begin(image, image_out, semaphores.at[0])
    first, second = maps.with_partners(sides[...])
    base[:owned, :], base[owned:, :] = first, second
    inside = jnp.sum(maps.part(4).astype(F32), axis=1, keepdims=True)
    b, w = mine[:owned, :], first * inside
    lanes = mine.shape[1]
    width = lanes // rights
    group = lax.div(iota((lanes, lanes), 0), width) == lax.div(iota((lanes, lanes), 1), width)
    rows = [total_rows(b * w), total_rows(w * w), jnp.ones((6, lanes), F32)]
    pair = grouped(jnp.concatenate(rows, axis=0), group.astype(F32).astype(BF16))
    sigma = jnp.where(pair[1:2] > 0.0, pair[0:1] / pair[1:2], 0.0)
    tile = 2 * width
    spread = []
    for r in range(rights):
        piece = sigma[:, r // 2 * tile : (r // 2 + 1) * tile]
        low = lower_half(piece) == (r % 2 == 0)
        spread.append(jnp.where(low, piece, flip_halves(piece)))
    spread = jnp.concatenate(spread, axis=0)
    shifts[...] = jnp.broadcast_to(sigma, shifts.shape)
    known[...] = jnp.concatenate(
        by_right(total_rows(mine[...] * mine[...]), rights)
        + [
            flat_sums(flat[at : at + count, :] * image[at : at + count, :], tile)
            for at in range(0, flat.shape[0], count)
        ]
        + [jnp.where(iota(spread.shape, 1) == 0, spread, 0.0), spread],
        axis=0,
    )
    lifted_out[...] = lifted(flat[...], lift)
    scale = jnp.concatenate([scale_of(table[:count, :])] * rights, axis=0)
    copies = solved.shape[1] // scale.shape[1]
    scaled[...] = solved[...] / jnp.concatenate([scale] * copies, axis=1)
    store_traces(mine, maps, side_traces, top_traces, rights)
    write.wait()


def after_body(
    owned, mine, flat, lift, maps, lifted_first, lifted_out, side_traces, top_traces, first_out,
    semaphores
):
    count = top_traces.shape[1]
    read = begin(lifted_first, first_out, semaphores.at[0])
    lifted_out[...] = lifted(flat[...], lift)
    store_traces(mine, Maps(maps, owned), side_traces, top_traces, flat.shape[0] // count)
    read.wait()


def total_rows(value):
    return jnp.sum(value, axis=0, keepdims=True)


def grouped(rows, group):
    high, rest = halves(rows)
    middle = rest.astype(F32)
    low = (rows - high.astype(F32) - middle).astype(BF16)
    return dot(high, group) + (dot(rest, group) + dot(low, group))


def fold(value):
    return jnp.sum(value.reshape(value.shape[0] // 8, 8, value.shape[1]), axis=0)


def flat_sums(value, tile):
    value = fold(value)
    parts = [value[:, at : at + tile] for at in range(0, value.shape[1], tile)]
    return total_rows(functools.reduce(jnp.add, parts))


def stats_body(
    owned, base, maps, received, bottom, top, up, down, table, split, known, shifts, mine_in,
    flat_in, image_in, next_mine_out, next_flat_out, stats,
    total_next, mine, flat, image, next_mine, next_flat, next_image, semaphores
):
    count = bottom.shape[0]
    rights = flat.shape[0] // count
    reads = [
        begin(mine_in, mine, semaphores.at[0]),
        begin(flat_in, flat, semaphores.at[1]),
        begin(image_in, image, semaphores.at[2]),
    ]
    maps = Maps(maps, owned)
    add_up(base, maps, received, bottom, top, up, down, total_next)
    next_mine[...] = own_faces(total_next, owned, count)
    writes = [begin(next_mine, next_mine_out, semaphores.at[3])]

    def turned(rows):
        writes.append(
            begin(next_flat.at[rows], next_flat_out.at[rows], semaphores.at[3 + len(writes)])
        )

    operate(total_next, table, split, next_flat, next_image, count, turned)
    for read in reads:
        read.wait()
    sigma = shifts[0:1, :]
    rr = rw = ww = 0.0
    for at in range(0, mine.shape[0], count):
        w = next_mine[at : at + count, :]
        r = mine[at : at + count, :] - sigma * w
        rr, rw, ww = rr + fold(r * r), rw + fold(r * w), ww + fold(w * w)
    rows = []
    for part in (rr, rw, ww):
        rows += by_right(total_rows(part), rights)
    tile = stats.shape[2]
    gh, gz, lz = [], [], []
    for r in range(rights):
        part = slice(r * count, (r + 1) * count)
        shift = known[3 * rights + r : 3 * rights + r + 1, :]
        shift = jnp.concatenate([shift] * (flat.shape[1] // tile), axis=1)
        after, z = next_flat[part, :], next_image[part, :]
        g, h = flat[part, :] - shift * after, image[part, :] - shift * z
        gh.append(flat_sums(g * h, tile))
        gz.append(flat_sums(g * z, tile))
        lz.append(flat_sums(after * z, tile))
    rows = jnp.concatenate(
        [known[: 2 * rights, :]]
        + rows + gh + gz + lz
        + [known[2 * rights : 3 * rights, :], jnp.zeros((tile - STATS * rights, tile), F32)],
        axis=0,
    )
    high, low = halves(rows)
    rest = (rows - high.astype(F32) - low.astype(F32)).astype(BF16)
    ones = jnp.ones((8, tile), BF16)
    sums = dot_across(ones, high) + (dot_across(ones, low) + dot_across(ones, rest))
    stats[...] = jnp.broadcast_to(sums[0:1, :][None], stats.shape)
    for write in writes:
        write.wait()


def finish_body(
    stats, side_first, side_next, top_first, top_next, scaled, lifted_first, lifted_next,
    interior, side_traces, top_traces,
    scaled_here, side_here, side_next_here, top_here, top_next_here, semaphores
):
    rights = side_traces.shape[1]
    block = scaled.shape[0] // rights
    parts = [pl.ds(r * block, block) for r in range(rights)]
    reads = [
        begin(scaled.at[part], scaled_here.at[part], semaphores.at[r])
        for r, part in enumerate(parts)
    ]
    traces = (
        (side_first, side_here), (side_next, side_next_here), (top_first, top_here),
        (top_next, top_next_here),
    )
    for k, (source, target) in enumerate(traces):
        reads.append(begin(source, target, semaphores.at[rights + k]))
    every = stats[:, 0, :]
    lanes = every.shape[1]

    def quantity(index):
        return every if index == 0 else pltpu.roll(every, lanes - index * rights, 1)

    mu0, mu1 = total_rows(quantity(0)), total_rows(quantity(1))
    alpha = mu0 / mu1
    shift = quantity(8) - alpha
    norm = total_rows(quantity(2) + shift * (2.0 * quantity(3) + shift * quantity(4)))
    energy = total_rows(quantity(5) + shift * (2.0 * quantity(6) + shift * quantity(7)))
    beta = norm / mu0
    alpha_next = norm / (energy - beta * norm / alpha)
    diagonal = iota((rights, lanes), 0) == iota((rights, lanes), 1)

    def column(row):
        return jnp.sum(jnp.where(diagonal, row, 0.0), axis=1, keepdims=True)

    first = column(alpha + alpha_next * (1.0 + beta))
    following = column(-alpha_next * alpha)
    writes = []
    for r, part in enumerate(parts):
        reads[r].wait()
        scaled_here[part, :] = scaled_here[part, :] - (
            first[r : r + 1, :] * lifted_first[part, :]
            + following[r : r + 1, :] * lifted_next[part, :]
        )
        writes.append(begin(scaled_here.at[part], interior.at[part], semaphores.at[rights + 4 + r]))
    for k, (here, next_here, out) in enumerate(
        ((side_here, side_next_here, side_traces), (top_here, top_next_here, top_traces))
    ):
        reads[rights + 2 * k].wait()
        reads[rights + 2 * k + 1].wait()
        here[...] = first[None] * here[...] + following[None] * next_here[...]
        writes.append(begin(here, out, semaphores.at[2 * rights + 4 + k]))
    for write in writes:
        write.wait()


def per_device(
    source, interior_inverse, coupling, trace_operator, face_ids, orientation, element_scale
):
    nodes, rights, count = source.shape
    traces = trace_operator.shape[0]
    columns = orientation.shape[1]
    face_nodes = traces // columns
    blocks = lax.axis_size("dev")
    layers = lax.axis_size("gz")
    capacity = count // blocks
    owned = 2 * count
    lines = 2 * blocks * capacity
    flat_rows = rights * count
    lanes = rights * face_nodes
    grid_rows = columns * count
    side_rows = (columns - 2) * count
    ids, codes = face_ids.T, orientation.T
    scale = element_scale.reshape(1, count)
    flat_source = source.transpose(1, 2, 0).reshape(flat_rows, nodes)
    grid = ((grid_rows, lanes), F32)
    faces = [((side_rows, lanes), F32), ((count, lanes), F32), ((count, lanes), F32)]
    flat = ((flat_rows, traces), F32)
    whole = ((flat_rows, nodes), F32)
    table = ((grid_rows, 2 * face_nodes), I32)
    message = ((lines, lanes), F32)
    side_shape = ((face_nodes * rights, owned), F32)
    top_shape = ((face_nodes * rights, count), F32)

    def across(message):
        parts = message.reshape(blocks, 2 * capacity, message.shape[1])
        return lax.all_to_all(parts, "dev", 0, 0, tiled=True).reshape(message.shape)

    def climb(value):
        return lax.ppermute(value, "gz", [(at, (at + 1) % layers) for at in range(layers)])

    def sink(value):
        return lax.ppermute(value, "gz", [((at + 1) % layers, at) for at in range(layers)])

    wishes, marks = call(
        functools.partial(wishes_body, owned, capacity),
        [((lines, owned), I32), ((8, owned), I32)],
        [Raw(ids)],
        [(ids.shape, I32)],
        copies=1,
    )
    wanted = across(wishes)
    solved, sides, bottom, top, table = call(
        functools.partial(start_body, face_nodes),
        [whole + ("raw",)] + faces + [table],
        [Raw(flat_source), Raw(interior_inverse), Raw(coupling), Raw(codes), Raw(scale)],
        [whole, ((nodes, nodes), F32), ((nodes, traces), F32), (codes.shape, I32),
         (scale.shape, I32), whole, flat],
        copies=6,
        flops=6 * flat_rows * nodes * (nodes + traces),
    )
    (send,) = call(
        functools.partial(send_body, capacity),
        [message],
        [marks, wanted, sides],
        flops=4 * lines * side_rows * lanes,
    )
    up, down, received = climb(top), sink(bottom), across(send)
    square = ((2, traces, traces), BF16)
    maps, base, lift, split = call(
        functools.partial(tables_body, owned, capacity),
        [
            ((lines, 7 * owned), BF16),
            faces[0],
            ((2, nodes, traces), BF16, "far"),
            square,
        ],
        [marks, wanted, sides, far(interior_inverse), far(coupling), far(trace_operator)],
        flops=6 * nodes * nodes * traces,
    )
    mine = ((owned + count, lanes), F32)
    own, local, sides, bottom, top, send = call(
        functools.partial(apply_body, owned),
        [mine + ("raw",), flat + ("raw",)] + faces + [message + ("raw",)],
        [base, maps, received, bottom, top, up, down, table, split],
        [grid, mine, flat, flat, message],
        copies=5,
        flops=6 * flat_rows * traces * traces,
    )
    up, down, received = climb(top), sink(bottom), across(send)
    lifted_first, scaled, side_first, top_first, image, base, known, shifts = call(
        functools.partial(beside_body, owned),
        [whole + ("far",), whole + ("far",), side_shape + ("far",), top_shape + ("far",),
         flat + ("raw",), faces[0], ((4 * rights, 2 * face_nodes), F32), ((8, lanes), F32)],
        [far(own), far(local), table, far(lift), far(solved), maps, sides, bottom, top],
        [grid, flat],
        copies=1,
        flops=6 * flat_rows * traces * nodes,
    )
    own, local, stats = call(
        functools.partial(stats_body, owned),
        [mine + ("raw",), flat + ("raw",), ((layers * blocks, 1, 2 * face_nodes), F32)],
        [base, maps, received, bottom, top, up, down, table, split, known, shifts,
         Raw(own), Raw(local), Raw(image)],
        [grid, mine, flat, flat, mine, flat, flat],
        copies=6,
        flops=6 * flat_rows * traces * traces,
    )
    stats = lax.all_to_all(stats, ("gz", "dev"), 0, 0, tiled=True)
    lifted_next, side_next, top_next, lifted_first = call(
        functools.partial(after_body, owned),
        [whole, side_shape + ("far",), top_shape + ("far",), whole],
        [far(own), far(local), far(lift), maps, Raw(lifted_first)],
        copies=1,
        flops=6 * flat_rows * traces * nodes,
    )
    side_form = ((face_nodes, rights, owned), F32)
    top_form = ((face_nodes, rights, count), F32)
    interior, side_traces, top_traces = call(
        finish_body,
        [whole + ("raw",), side_form + ("raw",), top_form + ("raw",)],
        [stats, Raw(side_first.reshape(side_form[0])), Raw(side_next.reshape(side_form[0])),
         Raw(top_first.reshape(top_form[0])), Raw(top_next.reshape(top_form[0])), Raw(scaled),
         lifted_first, lifted_next],
        [whole, side_form, side_form, top_form, top_form],
        copies=2 * rights + 6,
    )
    interior = interior.reshape(rights, count, nodes).transpose(2, 0, 1)
    return (interior, side_traces, top_traces)


def solution(mesh):
    placed = (
        P(None, None, ("gz", "dev")),
        P(),
        P(),
        P(),
        P(("gz", "dev"), None),
        P(("gz", "dev"), None),
        P(("gz", "dev")),
    )
    return jax.shard_map(
        per_device,
        mesh=mesh,
        in_specs=placed,
        out_specs=(
            P(None, None, ("gz", "dev")),
            P(None, None, ("gz", "dev")),
            P(None, None, ("gz", "dev")),
        ),
        check_vma=False,
    )
```

```python
import functools
import math

import jax
import jax.numpy as jnp
from jax import lax
from jax.experimental import pallas as pl
from jax.experimental.pallas import tpu as pltpu
from jax.sharding import PartitionSpec as P

F32, BF16, I32 = jnp.float32, jnp.bfloat16, jnp.int32
VMEM_BYTES = 24 * 1024 * 1024
STATS = 9


def far(arg):
    return pltpu.with_memory_space_constraint(arg, pltpu.HBM)


class Raw:
    def __init__(self, arg):
        self.arg = arg


def call(body, outs, args, scratch=(), copies=0, flops=0):
    anywhere, near = pl.BlockSpec(memory_space=pl.ANY), pl.BlockSpec(memory_space=pltpu.VMEM)
    scratch = [pltpu.VMEM(*entry) for entry in scratch]
    if copies:
        scratch.append(pltpu.SemaphoreType.DMA((copies,)))
    specs = [anywhere if isinstance(arg, Raw) else near for arg in args]
    args = [far(arg.arg) if isinstance(arg, Raw) else arg for arg in args]
    return pl.pallas_call(
        body,
        out_shape=[
            pltpu.HBM(*out[:2]) if len(out) > 2 else jax.ShapeDtypeStruct(*out) for out in outs
        ],
        in_specs=specs,
        out_specs=[anywhere if out[2:] == ("raw",) else near for out in outs],
        scratch_shapes=scratch,
        compiler_params=pltpu.CompilerParams(vmem_limit_bytes=VMEM_BYTES),
        cost_estimate=pl.CostEstimate(
            flops=flops, bytes_accessed=sum(arg.size * 4 for arg in args), transcendentals=0
        ),
    )(*args)


def begin(source, target, semaphore):
    copy = pltpu.make_async_copy(source, target, semaphore)
    copy.start()
    return copy


def halves(value):
    high = value.astype(BF16)
    return high, (value - high.astype(F32)).astype(BF16)


def dot(left, right):
    return jnp.dot(left, right, preferred_element_type=F32)


def dot_split(left, right):
    rows = left[0].shape[0]
    both = dot(jnp.concatenate(left, axis=0), right[0])
    return both[:rows, :] + (both[rows:, :] + dot(left[0], right[1]))


def pick(onehot, value):
    high, low = halves(value)
    return dot(onehot, high) + dot(onehot, low)


def iota(shape, axis):
    return lax.broadcasted_iota(I32, shape, axis)


def column_of(row):
    size = row.shape[1]
    mask = iota((size, size), 0) == iota((size, size), 1)
    spread = jnp.where(mask, row.astype(F32), 0.0)
    return jnp.sum(spread, axis=1, keepdims=True).astype(I32)


def gather_lanes(value, table):
    return jnp.take_along_axis(value, table, axis=1, mode="promise_in_bounds")


def flip_halves(value):
    return pltpu.roll(value, value.shape[1] // 2, 1)


def lower_half(value):
    return iota(value.shape, 1) < value.shape[1] // 2


def to_flat(total, table, flat, count, pairs):
    width = table.shape[1]
    for c in range(0, total.shape[0] // count, 2):
        rows = slice(c * count, (c + 1) * count)
        rows_next = slice((c + 1) * count, (c + 2) * count)
        forward, forward_next = forward_of(table[rows, :]), forward_of(table[rows_next, :])
        for pair in pairs:
            lanes = slice(pair * width, (pair + 1) * width)
            first = gather_lanes(total[rows, lanes], forward)
            second = gather_lanes(total[rows_next, lanes], forward_next)
            low = lower_half(first)
            at = 2 * pair * count
            lanes = slice(c // 2 * width, (c // 2 + 1) * width)
            flat[at : at + count, lanes] = jnp.where(low, first, second)
            flat[at + count : at + 2 * count, lanes] = flip_halves(jnp.where(low, second, first))


def from_flat(flat, table, placed, count, pairs, columns):
    width = table.shape[1]
    for c in columns[::2]:
        back = back_of(table[c * count : (c + 1) * count, :])
        back_next = back_of(table[(c + 1) * count : (c + 2) * count, :])
        for pair in pairs:
            at = 2 * pair * count
            lanes = slice(c // 2 * width, (c // 2 + 1) * width)
            first = flat[at : at + count, lanes]
            second = flip_halves(flat[at + count : at + 2 * count, lanes])
            low = lower_half(first)
            lanes = slice(pair * width, (pair + 1) * width)
            placed(c, lanes, gather_lanes(jnp.where(low, first, second), back))
            placed(c + 1, lanes, gather_lanes(jnp.where(low, second, first), back_next))


def wishes_body(owned, capacity, faces, out, marks, ids, semaphores):
    begin(faces, ids, semaphores.at[0]).wait()
    row = jnp.concatenate([ids[2:3, :], ids[3:4, :]], axis=1)
    owner, slot = lax.div(row, owned), lax.rem(row, owned)
    count = row.shape[1]
    crossing = owner != lax.axis_index("dev")
    same = (column_of(owner) == owner) & (iota((count, count), 0) < iota((count, count), 1))
    rank = jnp.sum(jnp.where(same, 1.0, 0.0), axis=0, keepdims=True).astype(I32)
    first = lax.rem(jnp.concatenate([ids[0:1, :], ids[1:2, :]], axis=1), owned)
    place = jnp.where(crossing, owner * (2 * capacity) + rank, -1)
    here = jnp.where(crossing, -1, slot)
    marks[...] = jnp.concatenate(
        [place, first, here, jnp.zeros((marks.shape[0] - 3, count), I32)], axis=0
    )
    shape = (out.shape[0], count)
    line = iota(shape, 0)
    line = line - jnp.where(lax.rem(line, 2 * capacity) >= capacity, capacity, 0)
    chosen = jnp.where(line == place, (slot + 1).astype(F32), 0.0)
    out[...] = jnp.broadcast_to(
        jnp.sum(chosen, axis=1, keepdims=True).astype(I32), out.shape
    )


def start_body(
    face_nodes, source, inverse, coupling, codes, scales, solved, sides, bottom, top, table,
    source_here, inverse_here, coupling_here, orientation, scale, image, flat, semaphores
):
    small = [begin(codes, orientation, semaphores.at[5]), begin(scales, scale, semaphores.at[6])]
    depth = inverse.shape[0] // 2
    reads = []
    for k in range(2):
        part = pl.ds(k * depth, depth)
        reads.append(
            (
                begin(inverse.at[part], inverse_here.at[part], semaphores.at[2 * k]),
                begin(source.at[:, part], source_here.at[:, part], semaphores.at[2 * k + 1]),
            )
        )
    read_coupling = begin(coupling, coupling_here, semaphores.at[4])
    columns = orientation.shape[0]
    count = orientation.shape[1]
    edge = math.isqrt(face_nodes)
    pair = 2 * face_nodes
    lane = iota((count, pair), 1)
    half = lane - lax.rem(lane, face_nodes)
    node = lax.rem(lane, face_nodes)
    a, b = lax.div(node, edge), lax.rem(node, edge)
    for read in small:
        read.wait()
    scaled = column_of(scale[...]) * (pair * pair)
    for c in range(columns):
        turned = half if c % 2 == 0 else face_nodes - half
        code = jnp.broadcast_to(column_of(orientation[c : c + 1, :]), (count, pair))
        swapped = (code & 4) != 0
        first = (code & 2) != 0
        second = (code & 1) != 0
        i = jnp.where(first, edge - 1 - a, a)
        j = jnp.where(second, edge - 1 - b, b)
        forward = turned + jnp.where(swapped, j * edge + i, i * edge + j)
        i, j = jnp.where(swapped, b, a), jnp.where(swapped, a, b)
        i = jnp.where(first, edge - 1 - i, i)
        j = jnp.where(second, edge - 1 - j, j)
        back = turned + i * edge + j
        table[c * count : (c + 1) * count, :] = forward + pair * back + scaled
    has_below, has_above = layer_masks()
    side_columns = columns - 2

    def placed(column, lanes, value):
        if column < side_columns:
            sides[column * count : (column + 1) * count, lanes] = value
        elif column == side_columns:
            bottom[:, lanes] = value * has_below
        else:
            top[:, lanes] = value * has_above

    pairs = sides.shape[1] // pair
    parts = [range(0, pairs // 2), range(pairs // 2, pairs)]
    for k, pieces in enumerate(reads):
        for piece in pieces:
            piece.wait()
        depths = slice(k * depth, (k + 1) * depth)
        product = dot_split(halves(source_here[:, depths]), halves(inverse_here[depths, :]))
        image[...] = product if k == 0 else image[...] + product
    read_coupling.wait()
    split_coupling = halves(coupling_here[...])
    for part in parts:
        rows = slice(2 * part[0] * count, 2 * (part[-1] + 1) * count)
        flat[rows, :] = dot_split(halves(image[rows, :]), split_coupling)
    write = begin(image, solved, semaphores.at[7])
    for part in parts:
        from_flat(flat, table, placed, count, part, range(columns))
    write.wait()


def forward_of(table):
    return table & (table.shape[1] - 1)


def back_of(table):
    bits = table.shape[1].bit_length() - 1
    return (table >> bits) & (table.shape[1] - 1)


def scale_of(table):
    bits = table.shape[1].bit_length() - 1
    return (table >> (2 * bits)).astype(F32)


def places(capacity, marks, wanted):
    place, first = marks[0:1, :], marks[1:2, :]
    line = iota(wanted.shape, 0)
    named = wanted[...] == first + 1
    later = lax.rem(line, 2 * capacity) >= capacity
    taken = jnp.concatenate([later & named, line == place], axis=1).astype(F32)
    given = jnp.concatenate([~later & named, later & (line - capacity == place)], axis=1)
    return taken, given.astype(F32)


def send_body(capacity, marks, wanted, sides, send):
    taken, _ = places(capacity, marks, wanted)
    send[...] = pick(taken.astype(BF16), sides[...])


class Maps:
    def __init__(self, ref, owned):
        self.ref, self.owned = ref, owned

    def part(self, index, width=1):
        return self.ref[:, index * self.owned : (index + width) * self.owned]

    def message(self, sides):
        return pick(self.part(0, 2), sides)

    def with_partners(self, sides):
        near, far_side = sides[: self.owned, :], sides[self.owned :, :]
        return near + pick(self.part(4), far_side), far_side + pick(self.part(5), near)

    def from_message(self, received):
        return pick(self.part(2), received), pick(self.part(3), received)

    def by_face(self, sides):
        return pick(self.part(6), sides)


def tables_body(
    owned, capacity, marks, wanted, sides, bottom, up, inverse, coupling, operator,
    maps, base, below, lift, split
):
    taken, given = places(capacity, marks, wanted)
    first, here = marks[1:2, :], marks[2:3, :]
    across = (column_of(first) == here).astype(F32)
    sorter = (iota((owned, owned), 0) == first).astype(F32)
    maps[...] = jnp.concatenate(
        [taken, given[:, :owned].T, given[:, owned:].T, across, across.T, sorter], axis=1
    ).astype(BF16)
    below[...] = bottom[...] + up[...]
    base[:owned, :], base[owned:, :] = Maps(maps, owned).with_partners(sides[...])
    high, low = halves(dot_split(halves(inverse[...]), halves(coupling[...])))
    lift[0] = high
    lift[1] = low
    split[0], split[1] = halves(operator[...])


def add_up(base, maps, received, below, top, down, total):
    owned = maps.owned
    count = top.shape[0]
    total[2 * owned : 2 * owned + count, :] = below[...]
    total[2 * owned + count :, :] = top[...] + down[...]
    first, second = maps.from_message(received[...])
    total[:owned, :] = base[:owned, :] + first
    total[owned : 2 * owned, :] = base[owned : 2 * owned, :] + second


def own_faces(total, owned, count):
    return jnp.concatenate([total[:owned, :], total[total.shape[0] - count :, :]], axis=0)


def operate(total, table, split, flat, image, count, turned):
    pairs = total.shape[1] // table.shape[1]
    scale = scale_of(table[:count, :])
    scale = jnp.concatenate([scale] * (flat.shape[1] // scale.shape[1]), axis=1)
    parts = [range(0, pairs // 2), range(pairs // 2, pairs)]
    for part in parts:
        to_flat(total, table, flat, count, part)
        rows = slice(2 * part[0] * count, 2 * (part[-1] + 1) * count)
        turned(pl.ds(rows.start, rows.stop - rows.start))
        product = dot_split(halves(flat[rows, :]), (split[0], split[1]))
        image[rows, :] = product * jnp.concatenate([scale] * (product.shape[0] // count), axis=0)
    return parts


def layer_masks():
    layer = lax.axis_index("gz")
    return (layer > 0).astype(F32), (layer < lax.axis_size("gz") - 1).astype(F32)


def apply_body(
    owned, base, maps, received, below, top, down, table, split,
    mine, flat_out, sides_out, bottom_out, top_out, send,
    total, mine_here, flat, image, message, semaphores
):
    count = top.shape[0]
    maps = Maps(maps, owned)
    add_up(base, maps, received, below, top, down, total)
    mine_here[...] = own_faces(total, owned, count)
    writes = [begin(mine_here, mine, semaphores.at[0])]
    has_below, has_above = layer_masks()
    columns = total.shape[0] // count
    side_columns = columns - 2

    def placed(column, lanes, value):
        if column < side_columns:
            sides_out[column * count : (column + 1) * count, lanes] = value
        elif column == side_columns:
            bottom_out[:, lanes] = value * has_below
        else:
            top_out[:, lanes] = value * has_above

    def turned(rows):
        writes.append(begin(flat.at[rows], flat_out.at[rows], semaphores.at[len(writes)]))

    parts = operate(total, table, split, flat, image, count, turned)
    for part in parts:
        from_flat(image, table, placed, count, part, range(side_columns))
        lanes = slice(part[0] * table.shape[1], (part[-1] + 1) * table.shape[1])
        message[:, lanes] = maps.message(sides_out[:, lanes])
        writes.append(
            begin(message.at[:, lanes], send.at[:, lanes], semaphores.at[len(writes)])
        )
    for part in parts:
        from_flat(image, table, placed, count, part, range(side_columns, columns))
    for write in writes:
        write.wait()


def dot_across(left, right):
    return lax.dot_general(left, right, (((1,), (1,)), ((), ())), preferred_element_type=F32)


def lifted(flat, lift):
    high, low = halves(flat)
    return dot_across(high, lift[0]) + (dot_across(low, lift[0]) + dot_across(high, lift[1]))


def store_traces(mine, maps, side_traces, top_traces, rights):
    sides = maps.by_face(mine[: maps.owned, :]).T
    tops = mine[maps.owned :, :].T
    nodes = sides.shape[0] // rights
    for r in range(rights):
        rows = slice(r * nodes, (r + 1) * nodes)
        side_traces[pl.ds(r, nodes, stride=rights), :] = sides[rows, :]
        top_traces[pl.ds(r, nodes, stride=rights), :] = tops[rows, :]


def by_right(rows, rights):
    width = 2 * rows.shape[1] // rights
    low = iota((1, width), 1) < width // 2
    tiles = [rows[:, at : at + width] for at in range(0, rows.shape[1], width)]
    return [jnp.where(low == (r % 2 == 0), tiles[r // 2], 0.0) for r in range(rights)]


def beside_body(
    owned, mine_in, flat_in, lift_in, table, maps, sides, bottom, top, up,
    lifted_out, side_out, top_out, image_out, base, below, known, shifts,
    mine, flat, lift, placed, image, lifted_here, side_traces, top_traces, semaphores
):
    reads = [
        begin(mine_in, mine, semaphores.at[0]),
        begin(flat_in, flat, semaphores.at[1]),
        begin(lift_in, lift, semaphores.at[2]),
    ]
    count = bottom.shape[0]
    rights = flat.shape[0] // count
    maps = Maps(maps, owned)
    placed[: 2 * owned, :] = sides[...]
    placed[2 * owned : 2 * owned + count, :] = bottom[...]
    below[...] = bottom[...] + up[...]
    placed[2 * owned + count :, :] = top[...]
    to_flat(placed, table, image, count, range(rights // 2))
    writes = [begin(image, image_out, semaphores.at[3])]
    first, second = maps.with_partners(sides[...])
    base[:owned, :], base[owned:, :] = first, second
    reads[0].wait()
    store_traces(mine, maps, side_traces, top_traces, rights)
    writes.append(begin(side_traces, side_out, semaphores.at[4]))
    writes.append(begin(top_traces, top_out, semaphores.at[5]))
    reads[1].wait()
    reads[2].wait()
    lifted_here[...] = lifted(flat[...], lift)
    writes.append(begin(lifted_here, lifted_out, semaphores.at[6]))
    inside = jnp.sum(maps.part(4).astype(F32), axis=1, keepdims=True)
    b, w = mine[:owned, :], base[:owned, :] * inside
    lanes = mine.shape[1]
    width = lanes // rights
    group = lax.div(iota((lanes, lanes), 0), width) == lax.div(iota((lanes, lanes), 1), width)
    rows = [total_rows(b * w), total_rows(w * w), jnp.ones((6, lanes), F32)]
    pair = grouped(jnp.concatenate(rows, axis=0), group.astype(F32).astype(BF16))
    sigma = jnp.where(pair[1:2] > 0.0, pair[0:1] / pair[1:2], 0.0)
    tile = 2 * width
    spread = []
    for r in range(rights):
        piece = sigma[:, r // 2 * tile : (r // 2 + 1) * tile]
        low = lower_half(piece) == (r % 2 == 0)
        spread.append(jnp.where(low, piece, flip_halves(piece)))
    spread = jnp.concatenate(spread, axis=0)
    shifts[...] = jnp.broadcast_to(sigma, shifts.shape)
    known[...] = jnp.concatenate(
        by_right(total_rows(mine[...] * mine[...]), rights)
        + [
            flat_sums(flat[at : at + count, :] * image[at : at + count, :], tile)
            for at in range(0, flat.shape[0], count)
        ]
        + [jnp.where(iota(spread.shape, 1) == 0, spread, 0.0), spread],
        axis=0,
    )
    for write in writes:
        write.wait()


def after_body(
    owned, mine_in, flat_in, lift_in, lifted_first, table, maps,
    lifted_out, side_out, top_out, first_out, inverse_scale,
    mine, flat, lift, side_traces, top_traces, semaphores
):
    reads = [
        begin(mine_in, mine, semaphores.at[0]),
        begin(flat_in, flat, semaphores.at[1]),
        begin(lift_in, lift, semaphores.at[2]),
        begin(lifted_first, first_out, semaphores.at[3]),
    ]
    count = inverse_scale.shape[0]
    inverse_scale[...] = 1.0 / scale_of(table[:count, :])
    reads[0].wait()
    store_traces(mine, Maps(maps, owned), side_traces, top_traces, flat.shape[0] // count)
    writes = [
        begin(side_traces, side_out, semaphores.at[4]),
        begin(top_traces, top_out, semaphores.at[5]),
    ]
    reads[1].wait()
    reads[2].wait()
    lifted_out[...] = lifted(flat[...], lift)
    reads[3].wait()
    for write in writes:
        write.wait()


def total_rows(value):
    return jnp.sum(value, axis=0, keepdims=True)


def grouped(rows, group):
    high, rest = halves(rows)
    middle = rest.astype(F32)
    low = (rows - high.astype(F32) - middle).astype(BF16)
    return dot(high, group) + (dot(rest, group) + dot(low, group))


def fold(value):
    return jnp.sum(value.reshape(value.shape[0] // 8, 8, value.shape[1]), axis=0)


def flat_sums(value, tile):
    value = fold(value)
    parts = [value[:, at : at + tile] for at in range(0, value.shape[1], tile)]
    return total_rows(functools.reduce(jnp.add, parts))


def stats_body(
    owned, base, maps, received, below, top, down, table, split, known, shifts, mine_in,
    flat_in, image_in, next_mine_out, next_flat_out, stats,
    total_next, mine, flat, image, next_mine, next_flat, next_image, semaphores
):
    count = top.shape[0]
    rights = flat.shape[0] // count
    reads = [
        begin(mine_in, mine, semaphores.at[0]),
        begin(flat_in, flat, semaphores.at[1]),
        begin(image_in, image, semaphores.at[2]),
    ]
    maps = Maps(maps, owned)
    add_up(base, maps, received, below, top, down, total_next)
    next_mine[...] = own_faces(total_next, owned, count)
    writes = [begin(next_mine, next_mine_out, semaphores.at[3])]

    def turned(rows):
        writes.append(
            begin(next_flat.at[rows], next_flat_out.at[rows], semaphores.at[3 + len(writes)])
        )

    operate(total_next, table, split, next_flat, next_image, count, turned)
    for read in reads:
        read.wait()
    sigma = shifts[0:1, :]
    rr = rw = ww = 0.0
    for at in range(0, mine.shape[0], count):
        w = next_mine[at : at + count, :]
        r = mine[at : at + count, :] - sigma * w
        rr, rw, ww = rr + fold(r * r), rw + fold(r * w), ww + fold(w * w)
    rows = []
    for part in (rr, rw, ww):
        rows += by_right(total_rows(part), rights)
    tile = stats.shape[2]
    gh, gz, lz = [], [], []
    for r in range(rights):
        part = slice(r * count, (r + 1) * count)
        shift = known[3 * rights + r : 3 * rights + r + 1, :]
        shift = jnp.concatenate([shift] * (flat.shape[1] // tile), axis=1)
        after, z = next_flat[part, :], next_image[part, :]
        g, h = flat[part, :] - shift * after, image[part, :] - shift * z
        gh.append(flat_sums(g * h, tile))
        gz.append(flat_sums(g * z, tile))
        lz.append(flat_sums(after * z, tile))
    rows = jnp.concatenate(
        [known[: 2 * rights, :]]
        + rows + gh + gz + lz
        + [known[2 * rights : 3 * rights, :], jnp.zeros((tile - STATS * rights, tile), F32)],
        axis=0,
    )
    high, low = halves(rows)
    rest = (rows - high.astype(F32) - low.astype(F32)).astype(BF16)
    ones = jnp.ones((8, tile), BF16)
    sums = dot_across(ones, high) + (dot_across(ones, low) + dot_across(ones, rest))
    stats[...] = jnp.broadcast_to(sums[0:1, :][None], stats.shape)
    for write in writes:
        write.wait()


def finish_body(
    stats, side_first, side_next, top_first, top_next, solved, lifted_first, lifted_next,
    inverse_scale, interior, side_traces, top_traces,
    solved_here, side_here, side_next_here, top_here, top_next_here, semaphores
):
    rights = side_traces.shape[1]
    block = solved.shape[0] // rights
    parts = [pl.ds(r * block, block) for r in range(rights)]
    reads = [
        begin(solved.at[part], solved_here.at[part], semaphores.at[r])
        for r, part in enumerate(parts)
    ]
    traces = (
        (side_first, side_here), (side_next, side_next_here), (top_first, top_here),
        (top_next, top_next_here),
    )
    for k, (source, target) in enumerate(traces):
        reads.append(begin(source, target, semaphores.at[rights + k]))
    every = stats[:, 0, :]
    lanes = every.shape[1]

    def quantity(index):
        return every if index == 0 else pltpu.roll(every, lanes - index * rights, 1)

    mu0, mu1 = total_rows(quantity(0)), total_rows(quantity(1))
    alpha = mu0 / mu1
    shift = quantity(8) - alpha
    norm = total_rows(quantity(2) + shift * (2.0 * quantity(3) + shift * quantity(4)))
    energy = total_rows(quantity(5) + shift * (2.0 * quantity(6) + shift * quantity(7)))
    beta = norm / mu0
    alpha_next = norm / (energy - beta * norm / alpha)
    diagonal = iota((rights, lanes), 0) == iota((rights, lanes), 1)

    def column(row):
        return jnp.sum(jnp.where(diagonal, row, 0.0), axis=1, keepdims=True)

    first = column(alpha + alpha_next * (1.0 + beta))
    following = column(-alpha_next * alpha)
    scale = inverse_scale[...]
    scale = jnp.concatenate([scale] * (solved.shape[1] // scale.shape[1]), axis=1)
    writes = []
    for r, part in enumerate(parts):
        reads[r].wait()
        solved_here[part, :] = solved_here[part, :] * scale - (
            first[r : r + 1, :] * lifted_first[part, :]
            + following[r : r + 1, :] * lifted_next[part, :]
        )
        writes.append(begin(solved_here.at[part], interior.at[part], semaphores.at[rights + 4 + r]))
    for k, (here, next_here, out) in enumerate(
        ((side_here, side_next_here, side_traces), (top_here, top_next_here, top_traces))
    ):
        reads[rights + 2 * k].wait()
        reads[rights + 2 * k + 1].wait()
        here[...] = first[None] * here[...] + following[None] * next_here[...]
        writes.append(begin(here, out, semaphores.at[2 * rights + 4 + k]))
    for write in writes:
        write.wait()


def per_device(
    source, interior_inverse, coupling, trace_operator, face_ids, orientation, element_scale
):
    nodes, rights, count = source.shape
    traces = trace_operator.shape[0]
    columns = orientation.shape[1]
    face_nodes = traces // columns
    blocks = lax.axis_size("dev")
    layers = lax.axis_size("gz")
    capacity = count // blocks
    owned = 2 * count
    lines = 2 * blocks * capacity
    flat_rows = rights * count
    lanes = rights * face_nodes
    grid_rows = columns * count
    side_rows = (columns - 2) * count
    ids, codes = face_ids.T, orientation.T
    scale = element_scale.reshape(1, count)
    flat_source = source.transpose(1, 2, 0).reshape(flat_rows, nodes)
    grid = ((grid_rows, lanes), F32)
    faces = [((side_rows, lanes), F32), ((count, lanes), F32), ((count, lanes), F32)]
    flat = ((flat_rows, traces), F32)
    whole = ((flat_rows, nodes), F32)
    table = ((grid_rows, 2 * face_nodes), I32)
    message = ((lines, lanes), F32)
    side_shape = ((face_nodes * rights, owned), F32)
    top_shape = ((face_nodes * rights, count), F32)

    def across(message):
        parts = message.reshape(blocks, 2 * capacity, message.shape[1])
        return lax.all_to_all(parts, "dev", 0, 0, tiled=True).reshape(message.shape)

    def climb(value):
        return lax.ppermute(value, "gz", [(at, (at + 1) % layers) for at in range(layers)])

    def sink(value):
        return lax.ppermute(value, "gz", [((at + 1) % layers, at) for at in range(layers)])

    wishes, marks = call(
        functools.partial(wishes_body, owned, capacity),
        [((lines, owned), I32), ((8, owned), I32)],
        [Raw(ids)],
        [(ids.shape, I32)],
        copies=1,
    )
    wanted = across(wishes)
    solved, sides, bottom, top, table = call(
        functools.partial(start_body, face_nodes),
        [whole + ("raw",)] + faces + [table],
        [Raw(flat_source), Raw(interior_inverse), Raw(coupling), Raw(codes), Raw(scale)],
        [whole, ((nodes, nodes), F32), ((nodes, traces), F32), (codes.shape, I32),
         (scale.shape, I32), whole, flat],
        copies=8,
        flops=6 * flat_rows * nodes * (nodes + traces),
    )
    (send,) = call(
        functools.partial(send_body, capacity),
        [message],
        [marks, wanted, sides],
        flops=400 * lines * side_rows * lanes,
    )
    up, down, received = climb(top), sink(bottom), across(send)
    square = ((2, traces, traces), BF16)
    maps, base, below, lift, split = call(
        functools.partial(tables_body, owned, capacity),
        [
            ((lines, 7 * owned), BF16),
            faces[0],
            faces[1],
            ((2, nodes, traces), BF16, "far"),
            square,
        ],
        [marks, wanted, sides, bottom, up, far(interior_inverse), far(coupling),
         far(trace_operator)],
        flops=40 * nodes * nodes * traces,
    )
    mine = ((owned + count, lanes), F32)
    own, local, sides, bottom, top, send = call(
        functools.partial(apply_body, owned),
        [mine + ("raw",), flat + ("raw",)] + faces + [message + ("raw",)],
        [base, maps, received, below, top, down, table, split],
        [grid, mine, flat, flat, message],
        copies=5,
        flops=6 * flat_rows * traces * traces,
    )
    up, down, received = climb(top), sink(bottom), across(send)
    lift_form = ((2, nodes, traces), BF16)
    lifted_first, side_first, top_first, image, base, below, known, shifts = call(
        functools.partial(beside_body, owned),
        [whole + ("raw",), side_shape + ("raw",), top_shape + ("raw",), flat + ("raw",), faces[0],
         faces[1], ((4 * rights, 2 * face_nodes), F32), ((8, lanes), F32)],
        [Raw(own), Raw(local), Raw(lift), table, maps, sides, bottom, top, up],
        [mine, flat, lift_form, grid, flat, whole, side_shape, top_shape],
        copies=7,
        flops=40 * flat_rows * traces * nodes,
    )
    own, local, stats = call(
        functools.partial(stats_body, owned),
        [mine + ("raw",), flat + ("raw",), ((layers * blocks, 1, 2 * face_nodes), F32)],
        [base, maps, received, below, top, down, table, split, known, shifts,
         Raw(own), Raw(local), Raw(image)],
        [grid, mine, flat, flat, mine, flat, flat],
        copies=6,
        flops=6 * flat_rows * traces * traces,
    )
    stats = lax.all_to_all(stats, ("gz", "dev"), 0, 0, tiled=True)
    lifted_next, side_next, top_next, lifted_first, inverse_scale = call(
        functools.partial(after_body, owned),
        [whole, side_shape + ("raw",), top_shape + ("raw",), whole,
         ((count, 2 * face_nodes), F32)],
        [Raw(own), Raw(local), Raw(lift), Raw(lifted_first), table, maps],
        [mine, flat, lift_form, side_shape, top_shape],
        copies=6,
        flops=6 * flat_rows * traces * nodes,
    )
    side_form = ((face_nodes, rights, owned), F32)
    top_form = ((face_nodes, rights, count), F32)
    interior, side_traces, top_traces = call(
        finish_body,
        [whole + ("raw",), side_form + ("raw",), top_form + ("raw",)],
        [stats, Raw(side_first.reshape(side_form[0])), Raw(side_next.reshape(side_form[0])),
         Raw(top_first.reshape(top_form[0])), Raw(top_next.reshape(top_form[0])), Raw(solved),
         lifted_first, lifted_next, inverse_scale],
        [whole, side_form, side_form, top_form, top_form],
        copies=2 * rights + 6,
    )
    interior = interior.reshape(rights, count, nodes).transpose(2, 0, 1)
    return (interior, side_traces, top_traces)


def solution(mesh):
    placed = (
        P(None, None, ("gz", "dev")),
        P(),
        P(),
        P(),
        P(("gz", "dev"), None),
        P(("gz", "dev"), None),
        P(("gz", "dev")),
    )
    return jax.shard_map(
        per_device,
        mesh=mesh,
        in_specs=placed,
        out_specs=(
            P(None, None, ("gz", "dev")),
            P(None, None, ("gz", "dev")),
            P(None, None, ("gz", "dev")),
        ),
        check_vma=False,
    )
```

```python
import functools
import math

import jax
import jax.numpy as jnp
from jax import lax
from jax.experimental import pallas as pl
from jax.experimental.pallas import tpu as pltpu
from jax.sharding import PartitionSpec as P

F32, BF16, I32 = jnp.float32, jnp.bfloat16, jnp.int32
VMEM_BYTES = 24 * 1024 * 1024
STATS = 9


def far(arg):
    return pltpu.with_memory_space_constraint(arg, pltpu.HBM)


class Raw:
    def __init__(self, arg):
        self.arg = arg


def call(body, outs, args, scratch=(), copies=0, flops=0):
    anywhere, near = pl.BlockSpec(memory_space=pl.ANY), pl.BlockSpec(memory_space=pltpu.VMEM)
    scratch = [pltpu.VMEM(*entry) for entry in scratch]
    if copies:
        scratch.append(pltpu.SemaphoreType.DMA((copies,)))
    specs = [anywhere if isinstance(arg, Raw) else near for arg in args]
    args = [far(arg.arg) if isinstance(arg, Raw) else arg for arg in args]
    return pl.pallas_call(
        body,
        out_shape=[
            pltpu.HBM(*out[:2]) if len(out) > 2 else jax.ShapeDtypeStruct(*out) for out in outs
        ],
        in_specs=specs,
        out_specs=[anywhere if out[2:] == ("raw",) else near for out in outs],
        scratch_shapes=scratch,
        compiler_params=pltpu.CompilerParams(vmem_limit_bytes=VMEM_BYTES),
        cost_estimate=pl.CostEstimate(
            flops=flops, bytes_accessed=sum(arg.size * 4 for arg in args), transcendentals=0
        ),
    )(*args)


def begin(source, target, semaphore):
    copy = pltpu.make_async_copy(source, target, semaphore)
    copy.start()
    return copy


def halves(value):
    high = value.astype(BF16)
    return high, (value - high.astype(F32)).astype(BF16)


def dot(left, right):
    return jnp.dot(left, right, preferred_element_type=F32)


def dot_split(left, right):
    rows = left[0].shape[0]
    both = dot(jnp.concatenate(left, axis=0), right[0])
    return both[:rows, :] + (both[rows:, :] + dot(left[0], right[1]))


def pick(onehot, value):
    high, low = halves(value)
    return dot(onehot, high) + dot(onehot, low)


def iota(shape, axis):
    return lax.broadcasted_iota(I32, shape, axis)


def column_of(row):
    size = row.shape[1]
    mask = iota((size, size), 0) == iota((size, size), 1)
    spread = jnp.where(mask, row.astype(F32), 0.0)
    return jnp.sum(spread, axis=1, keepdims=True).astype(I32)


def gather_lanes(value, table):
    return jnp.take_along_axis(value, table, axis=1, mode="promise_in_bounds")


def flip_halves(value):
    return pltpu.roll(value, value.shape[1] // 2, 1)


def lower_half(value):
    return iota(value.shape, 1) < value.shape[1] // 2


def to_flat(total, table, flat, count, pairs):
    width = table.shape[1]
    for c in range(0, total.shape[0] // count, 2):
        rows = slice(c * count, (c + 1) * count)
        rows_next = slice((c + 1) * count, (c + 2) * count)
        forward, forward_next = forward_of(table[rows, :]), forward_of(table[rows_next, :])
        for pair in pairs:
            lanes = slice(pair * width, (pair + 1) * width)
            first = gather_lanes(total[rows, lanes], forward)
            second = gather_lanes(total[rows_next, lanes], forward_next)
            low = lower_half(first)
            at = 2 * pair * count
            lanes = slice(c // 2 * width, (c // 2 + 1) * width)
            flat[at : at + count, lanes] = jnp.where(low, first, second)
            flat[at + count : at + 2 * count, lanes] = flip_halves(jnp.where(low, second, first))


def from_flat(flat, table, placed, count, pairs, columns):
    width = table.shape[1]
    for c in columns[::2]:
        back = back_of(table[c * count : (c + 1) * count, :])
        back_next = back_of(table[(c + 1) * count : (c + 2) * count, :])
        for pair in pairs:
            at = 2 * pair * count
            lanes = slice(c // 2 * width, (c // 2 + 1) * width)
            first = flat[at : at + count, lanes]
            second = flip_halves(flat[at + count : at + 2 * count, lanes])
            low = lower_half(first)
            lanes = slice(pair * width, (pair + 1) * width)
            placed(c, lanes, gather_lanes(jnp.where(low, first, second), back))
            placed(c + 1, lanes, gather_lanes(jnp.where(low, second, first), back_next))


def solve_body(
    face_nodes, source, inverse, coupling, codes, scales, solved, coupling_here, table,
    source_here, inverse_here, orientation, scale, semaphores
):
    small = [begin(codes, orientation, semaphores.at[4]), begin(scales, scale, semaphores.at[5])]
    depth = inverse.shape[0] // 2
    reads = []
    for k in range(2):
        part = pl.ds(k * depth, depth)
        reads.append(
            (
                begin(inverse.at[part], inverse_here.at[part], semaphores.at[2 * k]),
                begin(source.at[:, part], source_here.at[:, part], semaphores.at[2 * k + 1]),
            )
        )
    read_coupling = begin(coupling, coupling_here, semaphores.at[6])
    columns = orientation.shape[0]
    count = orientation.shape[1]
    edge = math.isqrt(face_nodes)
    pair = 2 * face_nodes
    lane = iota((count, pair), 1)
    side = lane - lax.rem(lane, face_nodes)
    node = lax.rem(lane, face_nodes)
    a, b = lax.div(node, edge), lax.rem(node, edge)
    for read in small:
        read.wait()
    scaled = column_of(scale[...]) * (pair * pair)
    for c in range(columns):
        turned = side if c % 2 == 0 else face_nodes - side
        code = jnp.broadcast_to(column_of(orientation[c : c + 1, :]), (count, pair))
        swapped = (code & 4) != 0
        first = (code & 2) != 0
        second = (code & 1) != 0
        i = jnp.where(first, edge - 1 - a, a)
        j = jnp.where(second, edge - 1 - b, b)
        forward = turned + jnp.where(swapped, j * edge + i, i * edge + j)
        i, j = jnp.where(swapped, b, a), jnp.where(swapped, a, b)
        i = jnp.where(first, edge - 1 - i, i)
        j = jnp.where(second, edge - 1 - j, j)
        back = turned + i * edge + j
        table[c * count : (c + 1) * count, :] = forward + pair * back + scaled
    for k, pieces in enumerate(reads):
        for piece in pieces:
            piece.wait()
        depths = slice(k * depth, (k + 1) * depth)
        product = dot_split(halves(source_here[:, depths]), halves(inverse_here[depths, :]))
        solved[...] = product if k == 0 else solved[...] + product
    read_coupling.wait()


def condense_body(
    solved, coupling, table, solved_out, sides, bottom, top, flat, semaphores
):
    write = begin(solved, solved_out, semaphores.at[0])
    count = bottom.shape[0]
    columns = table.shape[0] // count
    has_below, has_above = layer_masks()
    side_columns = columns - 2

    def placed(column, lanes, value):
        if column < side_columns:
            sides[column * count : (column + 1) * count, lanes] = value
        elif column == side_columns:
            bottom[:, lanes] = value * has_below
        else:
            top[:, lanes] = value * has_above

    pairs = sides.shape[1] // table.shape[1]
    parts = [range(0, pairs // 2), range(pairs // 2, pairs)]
    split = halves(coupling[...])
    for part in parts:
        rows = slice(2 * part[0] * count, 2 * (part[-1] + 1) * count)
        flat[rows, :] = dot_split(halves(solved[rows, :]), split)
    for part in parts:
        from_flat(flat, table, placed, count, part, range(columns))
    write.wait()


def forward_of(table):
    return table & (table.shape[1] - 1)


def back_of(table):
    bits = table.shape[1].bit_length() - 1
    return (table >> bits) & (table.shape[1] - 1)


def scale_of(table):
    bits = table.shape[1].bit_length() - 1
    return (table >> (2 * bits)).astype(F32)


def places(capacity, marks, wanted):
    place, first = marks[0:1, :], marks[1:2, :]
    line = iota(wanted.shape, 0)
    named = wanted[...] == first + 1
    later = lax.rem(line, 2 * capacity) >= capacity
    taken = jnp.concatenate([later & named, line == place], axis=1).astype(F32)
    given = jnp.concatenate([~later & named, later & (line - capacity == place)], axis=1)
    return taken, given.astype(F32)


def names_body(owned, capacity, block_of, ids, *refs):
    *others, sides, send, wanted, marks = refs
    here = lax.axis_index("dev")

    def second(rows, at):
        return jnp.concatenate([rows[at + 2 : at + 3, :], rows[at + 3 : at + 4, :]], axis=1)

    names = jnp.concatenate(
        [second(rows, at) for rows in others for at in range(0, rows.shape[0], ids.shape[0])], axis=0
    )
    blocks, count = names.shape
    earlier = (iota((count, count), 0) < iota((count, count), 1)).astype(F32).astype(BF16)
    block = block_of(iota((blocks, count), 0), here)
    row = second(ids, 0)
    owner, slot = lax.div(row, owned), lax.rem(row, owned)
    crossing = owner != here
    named = (lax.div(names, owned) == here) & (block != here)
    own = (block == owner) & crossing
    masks = jnp.concatenate([named.astype(F32), own.astype(F32)], axis=0).astype(BF16)
    ranks = dot(masks, earlier)
    place = jnp.where(own, (block * (2 * capacity)).astype(F32) + ranks[blocks:, :] + 1.0, 0.0)
    place = jnp.sum(place, axis=0, keepdims=True).astype(I32) - 1
    first = lax.rem(jnp.concatenate([ids[0:1, :], ids[1:2, :]], axis=1), owned)
    marks[...] = jnp.concatenate(
        [place, first, jnp.where(crossing, -1, slot), jnp.zeros((marks.shape[0] - 3, count), I32)],
        axis=0,
    )
    shape = (send.shape[0], blocks)
    line = iota(shape, 0)
    of_line = block_of(iota(shape, 1), here) == lax.div(line, 2 * capacity)
    of_line = of_line.astype(F32).astype(BF16)
    rank_here = dot(of_line, jnp.where(named, ranks[:blocks, :], -1.0).astype(BF16))
    slot_here = dot(of_line, lax.rem(names, owned).astype(F32).astype(BF16))
    line = lax.rem(iota(rank_here.shape, 0), capacity).astype(F32)
    chosen = jnp.where(rank_here == line, slot_here + 1.0, 0.0)
    wanted[...] = jnp.broadcast_to(
        jnp.sum(chosen, axis=1, keepdims=True).astype(I32), wanted.shape
    )
    taken, _ = places(capacity, marks, wanted)
    send[...] = pick(taken.astype(BF16), sides[...])


class Maps:
    def __init__(self, ref, owned):
        self.ref, self.owned = ref, owned

    def part(self, index, width=1):
        return self.ref[:, index * self.owned : (index + width) * self.owned]

    def message(self, sides):
        return pick(self.part(0, 2), sides)

    def with_partners(self, sides):
        near, far_side = sides[: self.owned, :], sides[self.owned :, :]
        return near + pick(self.part(4), far_side), far_side + pick(self.part(5), near)

    def from_message(self, received):
        return pick(self.part(2), received), pick(self.part(3), received)

    def by_face(self, sides):
        return pick(self.part(6), sides)


def tables_body(
    owned, capacity, marks, wanted, sides, bottom, up, inverse, coupling, operator,
    maps, base, below, lift, split
):
    taken, given = places(capacity, marks, wanted)
    first, here = marks[1:2, :], marks[2:3, :]
    across = (column_of(first) == here).astype(F32)
    sorter = (iota((owned, owned), 0) == first).astype(F32)
    maps[...] = jnp.concatenate(
        [taken, given[:, :owned].T, given[:, owned:].T, across, across.T, sorter], axis=1
    ).astype(BF16)
    below[...] = bottom[...] + up[...]
    base[:owned, :], base[owned:, :] = Maps(maps, owned).with_partners(sides[...])
    high, low = halves(dot_split(halves(inverse[...]), halves(coupling[...])))
    lift[0] = high
    lift[1] = low
    split[0], split[1] = halves(operator[...])


def add_up(base, maps, received, below, top, down, total):
    owned = maps.owned
    count = top.shape[0]
    total[2 * owned : 2 * owned + count, :] = below[...]
    total[2 * owned + count :, :] = top[...] + down[...]
    first, second = maps.from_message(received[...])
    total[:owned, :] = base[:owned, :] + first
    total[owned : 2 * owned, :] = base[owned : 2 * owned, :] + second


def own_faces(total, owned, count):
    return jnp.concatenate([total[:owned, :], total[total.shape[0] - count :, :]], axis=0)


def operate(total, table, split, flat, image, count, turned):
    pairs = total.shape[1] // table.shape[1]
    scale = scale_of(table[:count, :])
    scale = jnp.concatenate([scale] * (flat.shape[1] // scale.shape[1]), axis=1)
    parts = [range(0, pairs // 2), range(pairs // 2, pairs)]
    for part in parts:
        to_flat(total, table, flat, count, part)
        rows = slice(2 * part[0] * count, 2 * (part[-1] + 1) * count)
        turned(pl.ds(rows.start, rows.stop - rows.start))
        product = dot_split(halves(flat[rows, :]), (split[0], split[1]))
        image[rows, :] = product * jnp.concatenate([scale] * (product.shape[0] // count), axis=0)
    return parts


def layer_masks():
    layer = lax.axis_index("gz")
    return (layer > 0).astype(F32), (layer < lax.axis_size("gz") - 1).astype(F32)


def apply_body(
    owned, base, maps, received, below, top, down, table, split,
    mine, flat_out, sides_out, bottom_out, top_out, send,
    total, mine_here, flat, image, message, semaphores
):
    count = top.shape[0]
    maps = Maps(maps, owned)
    add_up(base, maps, received, below, top, down, total)
    mine_here[...] = own_faces(total, owned, count)
    writes = [begin(mine_here, mine, semaphores.at[0])]
    has_below, has_above = layer_masks()
    columns = total.shape[0] // count
    side_columns = columns - 2

    def placed(column, lanes, value):
        if column < side_columns:
            sides_out[column * count : (column + 1) * count, lanes] = value
        elif column == side_columns:
            bottom_out[:, lanes] = value * has_below
        else:
            top_out[:, lanes] = value * has_above

    def turned(rows):
        writes.append(begin(flat.at[rows], flat_out.at[rows], semaphores.at[len(writes)]))

    parts = operate(total, table, split, flat, image, count, turned)
    for part in parts:
        from_flat(image, table, placed, count, part, range(side_columns))
        lanes = slice(part[0] * table.shape[1], (part[-1] + 1) * table.shape[1])
        message[:, lanes] = maps.message(sides_out[:, lanes])
        writes.append(
            begin(message.at[:, lanes], send.at[:, lanes], semaphores.at[len(writes)])
        )
    for part in parts:
        from_flat(image, table, placed, count, part, range(side_columns, columns))
    for write in writes:
        write.wait()


def dot_across(left, right):
    return lax.dot_general(left, right, (((1,), (1,)), ((), ())), preferred_element_type=F32)


def lifted(flat, lift):
    high, low = halves(flat)
    return dot_across(high, lift[0]) + (dot_across(low, lift[0]) + dot_across(high, lift[1]))


def store_traces(mine, maps, side_traces, top_traces, rights):
    sides = maps.by_face(mine[: maps.owned, :]).T
    tops = mine[maps.owned :, :].T
    nodes = sides.shape[0] // rights
    for r in range(rights):
        rows = slice(r * nodes, (r + 1) * nodes)
        side_traces[pl.ds(r, nodes, stride=rights), :] = sides[rows, :]
        top_traces[pl.ds(r, nodes, stride=rights), :] = tops[rows, :]


def by_right(rows, rights):
    width = 2 * rows.shape[1] // rights
    low = iota((1, width), 1) < width // 2
    tiles = [rows[:, at : at + width] for at in range(0, rows.shape[1], width)]
    return [jnp.where(low == (r % 2 == 0), tiles[r // 2], 0.0) for r in range(rights)]


def beside_body(
    owned, mine_in, flat_in, lift_in, table, maps, sides, bottom, top, up,
    lifted_out, side_out, top_out, image_out, base, below, known, shifts,
    mine, flat, lift, placed, image, lifted_here, side_traces, top_traces, semaphores
):
    reads = [
        begin(mine_in, mine, semaphores.at[0]),
        begin(flat_in, flat, semaphores.at[1]),
        begin(lift_in, lift, semaphores.at[2]),
    ]
    count = bottom.shape[0]
    rights = flat.shape[0] // count
    maps = Maps(maps, owned)
    placed[: 2 * owned, :] = sides[...]
    placed[2 * owned : 2 * owned + count, :] = bottom[...]
    below[...] = bottom[...] + up[...]
    placed[2 * owned + count :, :] = top[...]
    to_flat(placed, table, image, count, range(rights // 2))
    writes = [begin(image, image_out, semaphores.at[3])]
    first, second = maps.with_partners(sides[...])
    base[:owned, :], base[owned:, :] = first, second
    reads[0].wait()
    store_traces(mine, maps, side_traces, top_traces, rights)
    writes.append(begin(side_traces, side_out, semaphores.at[4]))
    writes.append(begin(top_traces, top_out, semaphores.at[5]))
    reads[1].wait()
    reads[2].wait()
    lifted_here[...] = lifted(flat[...], lift)
    writes.append(begin(lifted_here, lifted_out, semaphores.at[6]))
    inside = jnp.sum(maps.part(4).astype(F32), axis=1, keepdims=True)
    b, w = mine[:owned, :], base[:owned, :] * inside
    lanes = mine.shape[1]
    width = lanes // rights
    group = lax.div(iota((lanes, lanes), 0), width) == lax.div(iota((lanes, lanes), 1), width)
    rows = [total_rows(b * w), total_rows(w * w), jnp.ones((6, lanes), F32)]
    pair = grouped(jnp.concatenate(rows, axis=0), group.astype(F32).astype(BF16))
    sigma = jnp.where(pair[1:2] > 0.0, pair[0:1] / pair[1:2], 0.0)
    tile = 2 * width
    spread = []
    for r in range(rights):
        piece = sigma[:, r // 2 * tile : (r // 2 + 1) * tile]
        low = lower_half(piece) == (r % 2 == 0)
        spread.append(jnp.where(low, piece, flip_halves(piece)))
    spread = jnp.concatenate(spread, axis=0)
    shifts[...] = jnp.broadcast_to(sigma, shifts.shape)
    known[...] = jnp.concatenate(
        by_right(total_rows(mine[...] * mine[...]), rights)
        + [
            flat_sums(flat[at : at + count, :] * image[at : at + count, :], tile)
            for at in range(0, flat.shape[0], count)
        ]
        + [jnp.where(iota(spread.shape, 1) == 0, spread, 0.0), spread],
        axis=0,
    )
    for write in writes:
        write.wait()


def after_body(
    owned, mine_in, flat_in, lift_in, lifted_first, table, maps,
    lifted_out, side_out, top_out, first_out, inverse_scale,
    mine, flat, lift, side_traces, top_traces, semaphores
):
    reads = [
        begin(mine_in, mine, semaphores.at[0]),
        begin(flat_in, flat, semaphores.at[1]),
        begin(lift_in, lift, semaphores.at[2]),
        begin(lifted_first, first_out, semaphores.at[3]),
    ]
    count = inverse_scale.shape[0]
    inverse_scale[...] = 1.0 / scale_of(table[:count, :])
    reads[0].wait()
    store_traces(mine, Maps(maps, owned), side_traces, top_traces, flat.shape[0] // count)
    writes = [
        begin(side_traces, side_out, semaphores.at[4]),
        begin(top_traces, top_out, semaphores.at[5]),
    ]
    reads[1].wait()
    reads[2].wait()
    lifted_out[...] = lifted(flat[...], lift)
    reads[3].wait()
    for write in writes:
        write.wait()


def total_rows(value):
    return jnp.sum(value, axis=0, keepdims=True)


def grouped(rows, group):
    high, rest = halves(rows)
    middle = rest.astype(F32)
    low = (rows - high.astype(F32) - middle).astype(BF16)
    return dot(high, group) + (dot(rest, group) + dot(low, group))


def fold(value):
    return jnp.sum(value.reshape(value.shape[0] // 8, 8, value.shape[1]), axis=0)


def flat_sums(value, tile):
    value = fold(value)
    parts = [value[:, at : at + tile] for at in range(0, value.shape[1], tile)]
    return total_rows(functools.reduce(jnp.add, parts))


def stats_body(
    owned, base, maps, received, below, top, down, table, split, known, shifts, mine_in,
    flat_in, image_in, next_mine_out, next_flat_out, stats,
    total_next, mine, flat, image, next_mine, next_flat, next_image, semaphores
):
    count = top.shape[0]
    rights = flat.shape[0] // count
    reads = [
        begin(mine_in, mine, semaphores.at[0]),
        begin(flat_in, flat, semaphores.at[1]),
        begin(image_in, image, semaphores.at[2]),
    ]
    maps = Maps(maps, owned)
    add_up(base, maps, received, below, top, down, total_next)
    next_mine[...] = own_faces(total_next, owned, count)
    writes = [begin(next_mine, next_mine_out, semaphores.at[3])]

    def turned(rows):
        writes.append(
            begin(next_flat.at[rows], next_flat_out.at[rows], semaphores.at[3 + len(writes)])
        )

    operate(total_next, table, split, next_flat, next_image, count, turned)
    for read in reads:
        read.wait()
    sigma = shifts[0:1, :]
    rr = rw = ww = 0.0
    for at in range(0, mine.shape[0], count):
        w = next_mine[at : at + count, :]
        r = mine[at : at + count, :] - sigma * w
        rr, rw, ww = rr + fold(r * r), rw + fold(r * w), ww + fold(w * w)
    rows = []
    for part in (rr, rw, ww):
        rows += by_right(total_rows(part), rights)
    tile = stats.shape[2]
    gh, gz, lz = [], [], []
    for r in range(rights):
        part = slice(r * count, (r + 1) * count)
        shift = known[3 * rights + r : 3 * rights + r + 1, :]
        shift = jnp.concatenate([shift] * (flat.shape[1] // tile), axis=1)
        after, z = next_flat[part, :], next_image[part, :]
        g, h = flat[part, :] - shift * after, image[part, :] - shift * z
        gh.append(flat_sums(g * h, tile))
        gz.append(flat_sums(g * z, tile))
        lz.append(flat_sums(after * z, tile))
    rows = jnp.concatenate(
        [known[: 2 * rights, :]]
        + rows + gh + gz + lz
        + [known[2 * rights : 3 * rights, :], jnp.zeros((tile - STATS * rights, tile), F32)],
        axis=0,
    )
    high, low = halves(rows)
    rest = (rows - high.astype(F32) - low.astype(F32)).astype(BF16)
    ones = jnp.ones((8, tile), BF16)
    sums = dot_across(ones, high) + (dot_across(ones, low) + dot_across(ones, rest))
    stats[...] = jnp.broadcast_to(sums[0:1, :][None], stats.shape)
    for write in writes:
        write.wait()


def finish_body(
    stats, side_first, side_next, top_first, top_next, solved, lifted_first, lifted_next,
    inverse_scale, interior, side_traces, top_traces,
    solved_here, side_here, side_next_here, top_here, top_next_here, semaphores
):
    rights = side_traces.shape[1]
    block = solved.shape[0] // rights
    parts = [pl.ds(r * block, block) for r in range(rights)]
    reads = [
        begin(solved.at[part], solved_here.at[part], semaphores.at[r])
        for r, part in enumerate(parts)
    ]
    traces = (
        (side_first, side_here), (side_next, side_next_here), (top_first, top_here),
        (top_next, top_next_here),
    )
    for k, (source, target) in enumerate(traces):
        reads.append(begin(source, target, semaphores.at[rights + k]))
    every = stats[:, 0, :]
    lanes = every.shape[1]

    def quantity(index):
        return every if index == 0 else pltpu.roll(every, lanes - index * rights, 1)

    mu0, mu1 = total_rows(quantity(0)), total_rows(quantity(1))
    alpha = mu0 / mu1
    shift = quantity(8) - alpha
    norm = total_rows(quantity(2) + shift * (2.0 * quantity(3) + shift * quantity(4)))
    energy = total_rows(quantity(5) + shift * (2.0 * quantity(6) + shift * quantity(7)))
    beta = norm / mu0
    alpha_next = norm / (energy - beta * norm / alpha)
    diagonal = iota((rights, lanes), 0) == iota((rights, lanes), 1)

    def column(row):
        return jnp.sum(jnp.where(diagonal, row, 0.0), axis=1, keepdims=True)

    first = column(alpha + alpha_next * (1.0 + beta))
    following = column(-alpha_next * alpha)
    scale = inverse_scale[...]
    scale = jnp.concatenate([scale] * (solved.shape[1] // scale.shape[1]), axis=1)
    writes = []
    for r, part in enumerate(parts):
        reads[r].wait()
        solved_here[part, :] = solved_here[part, :] * scale - (
            first[r : r + 1, :] * lifted_first[part, :]
            + following[r : r + 1, :] * lifted_next[part, :]
        )
        writes.append(begin(solved_here.at[part], interior.at[part], semaphores.at[rights + 4 + r]))
    for k, (here, next_here, out) in enumerate(
        ((side_here, side_next_here, side_traces), (top_here, top_next_here, top_traces))
    ):
        reads[rights + 2 * k].wait()
        reads[rights + 2 * k + 1].wait()
        here[...] = first[None] * here[...] + following[None] * next_here[...]
        writes.append(begin(here, out, semaphores.at[2 * rights + 4 + k]))
    for write in writes:
        write.wait()


def per_device(
    source, interior_inverse, coupling, trace_operator, face_ids, orientation, element_scale
):
    nodes, rights, count = source.shape
    traces = trace_operator.shape[0]
    columns = orientation.shape[1]
    face_nodes = traces // columns
    blocks = lax.axis_size("dev")
    layers = lax.axis_size("gz")
    capacity = count // blocks
    owned = 2 * count
    lines = 2 * blocks * capacity
    flat_rows = rights * count
    lanes = rights * face_nodes
    grid_rows = columns * count
    side_rows = (columns - 2) * count
    ids, codes = face_ids.T, orientation.T
    scale = element_scale.reshape(1, count)
    flat_source = source.transpose(1, 2, 0).reshape(flat_rows, nodes)
    grid = ((grid_rows, lanes), F32)
    faces = [((side_rows, lanes), F32), ((count, lanes), F32), ((count, lanes), F32)]
    flat = ((flat_rows, traces), F32)
    whole = ((flat_rows, nodes), F32)
    table = ((grid_rows, 2 * face_nodes), I32)
    message = ((lines, lanes), F32)
    side_shape = ((face_nodes * rights, owned), F32)
    top_shape = ((face_nodes * rights, count), F32)

    def across(message):
        parts = message.reshape(blocks, 2 * capacity, message.shape[1])
        return lax.all_to_all(parts, "dev", 0, 0, tiled=True).reshape(message.shape)

    def climb(value):
        return lax.ppermute(value, "gz", [(at, (at + 1) % layers) for at in range(layers)])

    def sink(value):
        return lax.ppermute(value, "gz", [((at + 1) % layers, at) for at in range(layers)])

    if blocks & (blocks - 1) == 0:
        gathered, received = [], ids
        for step in [2**k for k in range(blocks.bit_length() - 1)]:
            gathered = [jnp.concatenate(gathered + [received], axis=0)]
            pairs = [(at, at ^ step) for at in range(blocks)]
            received = lax.ppermute(gathered[0], "dev", pairs)
        gathered = gathered + [received]
        block_of = lambda row, here: row ^ here
    else:
        gathered = [lax.all_gather(ids, "dev", tiled=True)]
        block_of = lambda row, here: row
    solved, coupling_here, table = call(
        functools.partial(solve_body, face_nodes),
        [whole, ((nodes, traces), F32), table],
        [Raw(flat_source), Raw(interior_inverse), Raw(coupling), Raw(codes), Raw(scale)],
        [whole, ((nodes, nodes), F32), (codes.shape, I32), (scale.shape, I32)],
        copies=7,
        flops=6 * flat_rows * nodes * nodes,
    )
    solved, sides, bottom, top = call(
        condense_body,
        [whole + ("raw",)] + faces,
        [solved, coupling_here, table],
        [flat],
        copies=1,
        flops=6 * flat_rows * nodes * traces,
    )
    send, wanted, marks = call(
        functools.partial(names_body, owned, capacity, block_of),
        [message, ((lines, owned), I32), ((8, owned), I32)],
        [ids] + gathered + [sides],
        flops=400 * lines * side_rows * lanes,
    )
    up, down, received = climb(top), sink(bottom), across(send)
    square = ((2, traces, traces), BF16)
    maps, base, below, lift, split = call(
        functools.partial(tables_body, owned, capacity),
        [
            ((lines, 7 * owned), BF16),
            faces[0],
            faces[1],
            ((2, nodes, traces), BF16, "far"),
            square,
        ],
        [marks, wanted, sides, bottom, up, far(interior_inverse), far(coupling),
         far(trace_operator)],
        flops=40 * nodes * nodes * traces,
    )
    mine = ((owned + count, lanes), F32)
    own, local, sides, bottom, top, send = call(
        functools.partial(apply_body, owned),
        [mine + ("raw",), flat + ("raw",)] + faces + [message + ("raw",)],
        [base, maps, received, below, top, down, table, split],
        [grid, mine, flat, flat, message],
        copies=5,
        flops=6 * flat_rows * traces * traces,
    )
    up, down, received = climb(top), sink(bottom), across(send)
    lift_form = ((2, nodes, traces), BF16)
    lifted_first, side_first, top_first, image, base, below, known, shifts = call(
        functools.partial(beside_body, owned),
        [whole + ("raw",), side_shape + ("raw",), top_shape + ("raw",), flat + ("raw",), faces[0],
         faces[1], ((4 * rights, 2 * face_nodes), F32), ((8, lanes), F32)],
        [Raw(own), Raw(local), Raw(lift), table, maps, sides, bottom, top, up],
        [mine, flat, lift_form, grid, flat, whole, side_shape, top_shape],
        copies=7,
        flops=40 * flat_rows * traces * nodes,
    )
    own, local, stats = call(
        functools.partial(stats_body, owned),
        [mine + ("raw",), flat + ("raw",), ((layers * blocks, 1, 2 * face_nodes), F32)],
        [base, maps, received, below, top, down, table, split, known, shifts,
         Raw(own), Raw(local), Raw(image)],
        [grid, mine, flat, flat, mine, flat, flat],
        copies=6,
        flops=6 * flat_rows * traces * traces,
    )
    stats = lax.all_to_all(stats, ("gz", "dev"), 0, 0, tiled=True)
    lifted_next, side_next, top_next, lifted_first, inverse_scale = call(
        functools.partial(after_body, owned),
        [whole, side_shape + ("raw",), top_shape + ("raw",), whole,
         ((count, 2 * face_nodes), F32)],
        [Raw(own), Raw(local), Raw(lift), Raw(lifted_first), table, maps],
        [mine, flat, lift_form, side_shape, top_shape],
        copies=6,
        flops=6 * flat_rows * traces * nodes,
    )
    side_form = ((face_nodes, rights, owned), F32)
    top_form = ((face_nodes, rights, count), F32)
    interior, side_traces, top_traces = call(
        finish_body,
        [whole + ("raw",), side_form + ("raw",), top_form + ("raw",)],
        [stats, Raw(side_first.reshape(side_form[0])), Raw(side_next.reshape(side_form[0])),
         Raw(top_first.reshape(top_form[0])), Raw(top_next.reshape(top_form[0])), Raw(solved),
         lifted_first, lifted_next, inverse_scale],
        [whole, side_form, side_form, top_form, top_form],
        copies=2 * rights + 6,
    )
    interior = interior.reshape(rights, count, nodes).transpose(2, 0, 1)
    return (interior, side_traces, top_traces)


def solution(mesh):
    placed = (
        P(None, None, ("gz", "dev")),
        P(),
        P(),
        P(),
        P(("gz", "dev"), None),
        P(("gz", "dev"), None),
        P(("gz", "dev")),
    )
    return jax.shard_map(
        per_device,
        mesh=mesh,
        in_specs=placed,
        out_specs=(
            P(None, None, ("gz", "dev")),
            P(None, None, ("gz", "dev")),
            P(None, None, ("gz", "dev")),
        ),
        check_vma=False,
    )
```

```python
import functools
import math

import jax
import jax.numpy as jnp
from jax import lax
from jax.experimental import pallas as pl
from jax.experimental.pallas import tpu as pltpu
from jax.sharding import PartitionSpec as P

F32, BF16, I32 = jnp.float32, jnp.bfloat16, jnp.int32
VMEM_BYTES = 24 * 1024 * 1024
STATS = 9


def far(arg):
    return pltpu.with_memory_space_constraint(arg, pltpu.HBM)


class Raw:
    def __init__(self, arg):
        self.arg = arg


def call(body, outs, args, scratch=(), copies=0, flops=0):
    anywhere, near = pl.BlockSpec(memory_space=pl.ANY), pl.BlockSpec(memory_space=pltpu.VMEM)
    scratch = [pltpu.VMEM(*entry) for entry in scratch]
    if copies:
        scratch.append(pltpu.SemaphoreType.DMA((copies,)))
    specs = [anywhere if isinstance(arg, Raw) else near for arg in args]
    args = [far(arg.arg) if isinstance(arg, Raw) else arg for arg in args]
    return pl.pallas_call(
        body,
        out_shape=[
            pltpu.HBM(*out[:2]) if len(out) > 2 else jax.ShapeDtypeStruct(*out) for out in outs
        ],
        in_specs=specs,
        out_specs=[anywhere if out[2:] == ("raw",) else near for out in outs],
        scratch_shapes=scratch,
        compiler_params=pltpu.CompilerParams(vmem_limit_bytes=VMEM_BYTES),
        cost_estimate=pl.CostEstimate(
            flops=flops, bytes_accessed=sum(arg.size * 4 for arg in args), transcendentals=0
        ),
    )(*args)


def begin(source, target, semaphore):
    copy = pltpu.make_async_copy(source, target, semaphore)
    copy.start()
    return copy


def halves(value):
    high = value.astype(BF16)
    return high, (value - high.astype(F32)).astype(BF16)


def dot(left, right):
    return jnp.dot(left, right, preferred_element_type=F32)


def dot_split(left, right):
    rows = left[0].shape[0]
    both = dot(jnp.concatenate(left, axis=0), right[0])
    return both[:rows, :] + (both[rows:, :] + dot(left[0], right[1]))


def pick(onehot, value):
    high, low = halves(value)
    return dot(onehot, high) + dot(onehot, low)


def iota(shape, axis):
    return lax.broadcasted_iota(I32, shape, axis)


def column_of(row):
    size = row.shape[1]
    mask = iota((size, size), 0) == iota((size, size), 1)
    spread = jnp.where(mask, row.astype(F32), 0.0)
    return jnp.sum(spread, axis=1, keepdims=True).astype(I32)


def gather_lanes(value, table):
    return jnp.take_along_axis(value, table, axis=1, mode="promise_in_bounds")


def flip_halves(value):
    return pltpu.roll(value, value.shape[1] // 2, 1)


def lower_half(value):
    return iota(value.shape, 1) < value.shape[1] // 2


def to_flat(total, table, flat, count, pairs):
    width = table.shape[1]
    for c in range(0, total.shape[0] // count, 2):
        rows = slice(c * count, (c + 1) * count)
        rows_next = slice((c + 1) * count, (c + 2) * count)
        forward, forward_next = forward_of(table[rows, :]), forward_of(table[rows_next, :])
        for pair in pairs:
            lanes = slice(pair * width, (pair + 1) * width)
            first = gather_lanes(total[rows, lanes], forward)
            second = gather_lanes(total[rows_next, lanes], forward_next)
            low = lower_half(first)
            at = 2 * pair * count
            lanes = slice(c // 2 * width, (c // 2 + 1) * width)
            flat[at : at + count, lanes] = jnp.where(low, first, second)
            flat[at + count : at + 2 * count, lanes] = flip_halves(jnp.where(low, second, first))


def from_flat(flat, table, placed, count, pairs, columns):
    width = table.shape[1]
    for c in columns[::2]:
        back = back_of(table[c * count : (c + 1) * count, :])
        back_next = back_of(table[(c + 1) * count : (c + 2) * count, :])
        for pair in pairs:
            at = 2 * pair * count
            lanes = slice(c // 2 * width, (c // 2 + 1) * width)
            first = flat[at : at + count, lanes]
            second = flip_halves(flat[at + count : at + 2 * count, lanes])
            low = lower_half(first)
            lanes = slice(pair * width, (pair + 1) * width)
            placed(c, lanes, gather_lanes(jnp.where(low, first, second), back))
            placed(c + 1, lanes, gather_lanes(jnp.where(low, second, first), back_next))


def solve_body(
    face_nodes, source, inverse, coupling, codes, scales, solved, coupling_here, table,
    source_here, inverse_here, orientation, scale, semaphores
):
    small = [begin(codes, orientation, semaphores.at[4]), begin(scales, scale, semaphores.at[5])]
    depth = inverse.shape[0] // 2
    reads = []
    for k in range(2):
        part = pl.ds(k * depth, depth)
        reads.append(
            (
                begin(inverse.at[part], inverse_here.at[part], semaphores.at[2 * k]),
                begin(source.at[:, part], source_here.at[:, part], semaphores.at[2 * k + 1]),
            )
        )
    read_coupling = begin(coupling, coupling_here, semaphores.at[6])
    columns = orientation.shape[0]
    count = orientation.shape[1]
    edge = math.isqrt(face_nodes)
    pair = 2 * face_nodes
    lane = iota((count, pair), 1)
    side = lane - lax.rem(lane, face_nodes)
    node = lax.rem(lane, face_nodes)
    a, b = lax.div(node, edge), lax.rem(node, edge)
    for read in small:
        read.wait()
    scaled = column_of(scale[...]) * (pair * pair)
    for c in range(columns):
        turned = side if c % 2 == 0 else face_nodes - side
        code = jnp.broadcast_to(column_of(orientation[c : c + 1, :]), (count, pair))
        swapped = (code & 4) != 0
        first = (code & 2) != 0
        second = (code & 1) != 0
        i = jnp.where(first, edge - 1 - a, a)
        j = jnp.where(second, edge - 1 - b, b)
        forward = turned + jnp.where(swapped, j * edge + i, i * edge + j)
        i, j = jnp.where(swapped, b, a), jnp.where(swapped, a, b)
        i = jnp.where(first, edge - 1 - i, i)
        j = jnp.where(second, edge - 1 - j, j)
        back = turned + i * edge + j
        table[c * count : (c + 1) * count, :] = forward + pair * back + scaled
    for k, pieces in enumerate(reads):
        for piece in pieces:
            piece.wait()
        depths = slice(k * depth, (k + 1) * depth)
        product = dot_split(halves(source_here[:, depths]), halves(inverse_here[depths, :]))
        solved[...] = product if k == 0 else solved[...] + product
    read_coupling.wait()


def condense_body(
    solved, coupling, table, solved_out, sides, bottom, top, flat, semaphores
):
    write = begin(solved, solved_out, semaphores.at[0])
    count = bottom.shape[0]
    columns = table.shape[0] // count
    has_below, has_above = layer_masks()
    side_columns = columns - 2

    def placed(column, lanes, value):
        if column < side_columns:
            sides[column * count : (column + 1) * count, lanes] = value
        elif column == side_columns:
            bottom[:, lanes] = value * has_below
        else:
            top[:, lanes] = value * has_above

    pairs = sides.shape[1] // table.shape[1]
    parts = [range(0, pairs // 2), range(pairs // 2, pairs)]
    split = halves(coupling[...])
    for part in parts:
        rows = slice(2 * part[0] * count, 2 * (part[-1] + 1) * count)
        flat[rows, :] = dot_split(halves(solved[rows, :]), split)
    for part in parts:
        from_flat(flat, table, placed, count, part, range(columns))
    write.wait()


def forward_of(table):
    return table & (table.shape[1] - 1)


def back_of(table):
    bits = table.shape[1].bit_length() - 1
    return (table >> bits) & (table.shape[1] - 1)


def scale_of(table):
    bits = table.shape[1].bit_length() - 1
    return (table >> (2 * bits)).astype(F32)


def places(capacity, marks, wanted):
    place, first = marks[0:1, :], marks[1:2, :]
    line = iota(wanted.shape, 0)
    named = wanted[...] == first + 1
    later = lax.rem(line, 2 * capacity) >= capacity
    taken = jnp.concatenate([later & named, line == place], axis=1).astype(F32)
    given = jnp.concatenate([~later & named, later & (line - capacity == place)], axis=1)
    return taken, given.astype(F32)


def names_body(owned, capacity, block_of, ids, *refs):
    *others, sides, send, wanted, marks = refs
    here = lax.axis_index("dev")

    def second(rows, at):
        return jnp.concatenate([rows[at + 2 : at + 3, :], rows[at + 3 : at + 4, :]], axis=1)

    names = jnp.concatenate(
        [second(rows, at) for rows in others for at in range(0, rows.shape[0], ids.shape[0])], axis=0
    )
    blocks, count = names.shape
    earlier = (iota((count, count), 0) < iota((count, count), 1)).astype(F32).astype(BF16)
    block = block_of(iota((blocks, count), 0), here)
    row = second(ids, 0)
    owner, slot = lax.div(row, owned), lax.rem(row, owned)
    crossing = owner != here
    named = (lax.div(names, owned) == here) & (block != here)
    own = (block == owner) & crossing
    masks = jnp.concatenate([named.astype(F32), own.astype(F32)], axis=0).astype(BF16)
    ranks = dot(masks, earlier)
    place = jnp.where(own, (block * (2 * capacity)).astype(F32) + ranks[blocks:, :] + 1.0, 0.0)
    place = jnp.sum(place, axis=0, keepdims=True).astype(I32) - 1
    first = lax.rem(jnp.concatenate([ids[0:1, :], ids[1:2, :]], axis=1), owned)
    marks[...] = jnp.concatenate(
        [place, first, jnp.where(crossing, -1, slot), jnp.zeros((marks.shape[0] - 3, count), I32)],
        axis=0,
    )
    shape = (send.shape[0], blocks)
    line = iota(shape, 0)
    of_line = block_of(iota(shape, 1), here) == lax.div(line, 2 * capacity)
    of_line = of_line.astype(F32).astype(BF16)
    rank_here = dot(of_line, jnp.where(named, ranks[:blocks, :], -1.0).astype(BF16))
    slot_here = dot(of_line, lax.rem(names, owned).astype(F32).astype(BF16))
    line = lax.rem(iota(rank_here.shape, 0), capacity).astype(F32)
    chosen = jnp.where(rank_here == line, slot_here + 1.0, 0.0)
    wanted[...] = jnp.broadcast_to(
        jnp.sum(chosen, axis=1, keepdims=True).astype(I32), wanted.shape
    )
    taken, _ = places(capacity, marks, wanted)
    send[...] = pick(taken.astype(BF16), sides[...])


class Maps:
    def __init__(self, ref, owned):
        self.ref, self.owned = ref, owned

    def part(self, index, width=1):
        return self.ref[:, index * self.owned : (index + width) * self.owned]

    def message(self, sides):
        return pick(self.part(0, 2), sides)

    def with_partners(self, sides):
        near, far_side = sides[: self.owned, :], sides[self.owned :, :]
        return near + pick(self.part(4), far_side), far_side + pick(self.part(5), near)

    def from_message(self, received):
        return pick(self.part(2), received), pick(self.part(3), received)

    def by_face(self, sides):
        return pick(self.part(6), sides)


def tables_body(
    owned, capacity, marks, wanted, sides, bottom, up, inverse, coupling, operator,
    maps, base, below, lift, split
):
    taken, given = places(capacity, marks, wanted)
    first, here = marks[1:2, :], marks[2:3, :]
    across = (column_of(first) == here).astype(F32)
    sorter = (iota((owned, owned), 0) == first).astype(F32)
    maps[...] = jnp.concatenate(
        [taken, given[:, :owned].T, given[:, owned:].T, across, across.T, sorter], axis=1
    ).astype(BF16)
    below[...] = bottom[...] + up[...]
    base[:owned, :], base[owned:, :] = Maps(maps, owned).with_partners(sides[...])
    high, low = halves(dot_split(halves(inverse[...]), halves(coupling[...])))
    lift[0] = high
    lift[1] = low
    split[0], split[1] = halves(operator[...])


def add_up(base, maps, received, below, top, down, total):
    owned = maps.owned
    count = top.shape[0]
    total[2 * owned : 2 * owned + count, :] = below[...]
    total[2 * owned + count :, :] = top[...] + down[...]
    first, second = maps.from_message(received[...])
    total[:owned, :] = base[:owned, :] + first
    total[owned : 2 * owned, :] = base[owned : 2 * owned, :] + second


def own_faces(total, owned, count):
    return jnp.concatenate([total[:owned, :], total[total.shape[0] - count :, :]], axis=0)


def operate(total, table, split, flat, image, count, turned):
    pairs = total.shape[1] // table.shape[1]
    scale = scale_of(table[:count, :])
    scale = jnp.concatenate([scale] * (flat.shape[1] // scale.shape[1]), axis=1)
    parts = [range(0, pairs // 2), range(pairs // 2, pairs)]
    for part in parts:
        to_flat(total, table, flat, count, part)
        rows = slice(2 * part[0] * count, 2 * (part[-1] + 1) * count)
        turned(pl.ds(rows.start, rows.stop - rows.start))
        product = dot_split(halves(flat[rows, :]), (split[0], split[1]))
        image[rows, :] = product * jnp.concatenate([scale] * (product.shape[0] // count), axis=0)
    return parts


def layer_masks():
    layer = lax.axis_index("gz")
    return (layer > 0).astype(F32), (layer < lax.axis_size("gz") - 1).astype(F32)


def apply_body(
    owned, base, maps, received, below, top, down, table, split,
    mine, flat_out, sides_out, bottom_out, top_out, send,
    total, mine_here, flat, image, message, semaphores
):
    count = top.shape[0]
    maps = Maps(maps, owned)
    add_up(base, maps, received, below, top, down, total)
    mine_here[...] = own_faces(total, owned, count)
    writes = [begin(mine_here, mine, semaphores.at[0])]
    has_below, has_above = layer_masks()
    columns = total.shape[0] // count
    side_columns = columns - 2

    def placed(column, lanes, value):
        if column < side_columns:
            sides_out[column * count : (column + 1) * count, lanes] = value
        elif column == side_columns:
            bottom_out[:, lanes] = value * has_below
        else:
            top_out[:, lanes] = value * has_above

    def turned(rows):
        writes.append(begin(flat.at[rows], flat_out.at[rows], semaphores.at[len(writes)]))

    parts = operate(total, table, split, flat, image, count, turned)
    for part in parts:
        from_flat(image, table, placed, count, part, range(side_columns))
        lanes = slice(part[0] * table.shape[1], (part[-1] + 1) * table.shape[1])
        message[:, lanes] = maps.message(sides_out[:, lanes])
        writes.append(
            begin(message.at[:, lanes], send.at[:, lanes], semaphores.at[len(writes)])
        )
    for part in parts:
        from_flat(image, table, placed, count, part, range(side_columns, columns))
    for write in writes:
        write.wait()


def dot_across(left, right):
    return lax.dot_general(left, right, (((1,), (1,)), ((), ())), preferred_element_type=F32)


def lifted(flat, lift):
    high, low = halves(flat)
    return dot_across(high, lift[0]) + (dot_across(low, lift[0]) + dot_across(high, lift[1]))


def store_traces(mine, maps, side_traces, top_traces, rights):
    sides = maps.by_face(mine[: maps.owned, :]).T
    tops = mine[maps.owned :, :].T
    nodes = sides.shape[0] // rights
    for r in range(rights):
        rows = slice(r * nodes, (r + 1) * nodes)
        side_traces[pl.ds(r, nodes, stride=rights), :] = sides[rows, :]
        top_traces[pl.ds(r, nodes, stride=rights), :] = tops[rows, :]


def by_right(rows, rights):
    width = 2 * rows.shape[1] // rights
    low = iota((1, width), 1) < width // 2
    tiles = [rows[:, at : at + width] for at in range(0, rows.shape[1], width)]
    return [jnp.where(low == (r % 2 == 0), tiles[r // 2], 0.0) for r in range(rights)]


def beside_body(
    owned, mine_in, flat_in, lift_in, table, maps, sides, bottom, top, up,
    lifted_out, side_out, top_out, image_out, base, below, known, shifts,
    mine, flat, lift, placed, image, lifted_here, side_traces, top_traces, semaphores
):
    reads = [
        begin(mine_in, mine, semaphores.at[0]),
        begin(flat_in, flat, semaphores.at[1]),
        begin(lift_in, lift, semaphores.at[2]),
    ]
    count = bottom.shape[0]
    rights = flat.shape[0] // count
    maps = Maps(maps, owned)
    placed[: 2 * owned, :] = sides[...]
    placed[2 * owned : 2 * owned + count, :] = bottom[...]
    below[...] = bottom[...] + up[...]
    placed[2 * owned + count :, :] = top[...]
    to_flat(placed, table, image, count, range(rights // 2))
    writes = [begin(image, image_out, semaphores.at[3])]
    first, second = maps.with_partners(sides[...])
    base[:owned, :], base[owned:, :] = first, second
    reads[0].wait()
    store_traces(mine, maps, side_traces, top_traces, rights)
    writes.append(begin(side_traces, side_out, semaphores.at[4]))
    writes.append(begin(top_traces, top_out, semaphores.at[5]))
    reads[1].wait()
    reads[2].wait()
    lifted_here[...] = lifted(flat[...], lift)
    writes.append(begin(lifted_here, lifted_out, semaphores.at[6]))
    inside = jnp.sum(maps.part(4).astype(F32), axis=1, keepdims=True)
    b, w = mine[:owned, :], base[:owned, :] * inside
    lanes = mine.shape[1]
    width = lanes // rights
    group = lax.div(iota((lanes, lanes), 0), width) == lax.div(iota((lanes, lanes), 1), width)
    rows = [total_rows(b * w), total_rows(w * w), jnp.ones((6, lanes), F32)]
    pair = grouped(jnp.concatenate(rows, axis=0), group.astype(F32).astype(BF16))
    sigma = jnp.where(pair[1:2] > 0.0, pair[0:1] / pair[1:2], 0.0)
    tile = 2 * width
    spread = []
    for r in range(rights):
        piece = sigma[:, r // 2 * tile : (r // 2 + 1) * tile]
        low = lower_half(piece) == (r % 2 == 0)
        spread.append(jnp.where(low, piece, flip_halves(piece)))
    spread = jnp.concatenate(spread, axis=0)
    shifts[...] = jnp.broadcast_to(sigma, shifts.shape)
    known[...] = jnp.concatenate(
        by_right(total_rows(mine[...] * mine[...]), rights)
        + [
            flat_sums(flat[at : at + count, :] * image[at : at + count, :], tile)
            for at in range(0, flat.shape[0], count)
        ]
        + [jnp.where(iota(spread.shape, 1) == 0, spread, 0.0), spread],
        axis=0,
    )
    for write in writes:
        write.wait()


def after_body(
    owned, mine_in, flat_in, lift_in, lifted_first, table, maps,
    lifted_out, side_out, top_out, first_out, inverse_scale,
    mine, flat, lift, side_traces, top_traces, semaphores
):
    reads = [
        begin(mine_in, mine, semaphores.at[0]),
        begin(flat_in, flat, semaphores.at[1]),
        begin(lift_in, lift, semaphores.at[2]),
        begin(lifted_first, first_out, semaphores.at[3]),
    ]
    count = inverse_scale.shape[0]
    inverse_scale[...] = 1.0 / scale_of(table[:count, :])
    reads[0].wait()
    store_traces(mine, Maps(maps, owned), side_traces, top_traces, flat.shape[0] // count)
    writes = [
        begin(side_traces, side_out, semaphores.at[4]),
        begin(top_traces, top_out, semaphores.at[5]),
    ]
    reads[1].wait()
    reads[2].wait()
    lifted_out[...] = lifted(flat[...], lift)
    reads[3].wait()
    for write in writes:
        write.wait()


def total_rows(value):
    return jnp.sum(value, axis=0, keepdims=True)


def grouped(rows, group):
    high, rest = halves(rows)
    middle = rest.astype(F32)
    low = (rows - high.astype(F32) - middle).astype(BF16)
    return dot(high, group) + (dot(rest, group) + dot(low, group))


def fold(value):
    return jnp.sum(value.reshape(value.shape[0] // 8, 8, value.shape[1]), axis=0)


def flat_sums(value, tile):
    value = fold(value)
    parts = [value[:, at : at + tile] for at in range(0, value.shape[1], tile)]
    return total_rows(functools.reduce(jnp.add, parts))


def stats_body(
    owned, base, maps, received, below, top, down, table, split, known, shifts, mine_in,
    flat_in, image_in, next_mine_out, next_flat_out, stats,
    total_next, mine, flat, image, next_mine, next_flat, next_image, semaphores
):
    count = top.shape[0]
    rights = flat.shape[0] // count
    reads = [
        begin(mine_in, mine, semaphores.at[0]),
        begin(flat_in, flat, semaphores.at[1]),
        begin(image_in, image, semaphores.at[2]),
    ]
    maps = Maps(maps, owned)
    add_up(base, maps, received, below, top, down, total_next)
    next_mine[...] = own_faces(total_next, owned, count)
    writes = [begin(next_mine, next_mine_out, semaphores.at[3])]

    def turned(rows):
        writes.append(
            begin(next_flat.at[rows], next_flat_out.at[rows], semaphores.at[3 + len(writes)])
        )

    operate(total_next, table, split, next_flat, next_image, count, turned)
    for read in reads:
        read.wait()
    sigma = shifts[0:1, :]
    rr = rw = ww = 0.0
    for at in range(0, mine.shape[0], count):
        w = next_mine[at : at + count, :]
        r = mine[at : at + count, :] - sigma * w
        rr, rw, ww = rr + fold(r * r), rw + fold(r * w), ww + fold(w * w)
    rows = []
    for part in (rr, rw, ww):
        rows += by_right(total_rows(part), rights)
    tile = stats.shape[2]
    gh, gz, lz = [], [], []
    for r in range(rights):
        part = slice(r * count, (r + 1) * count)
        shift = known[3 * rights + r : 3 * rights + r + 1, :]
        shift = jnp.concatenate([shift] * (flat.shape[1] // tile), axis=1)
        after, z = next_flat[part, :], next_image[part, :]
        g, h = flat[part, :] - shift * after, image[part, :] - shift * z
        gh.append(flat_sums(g * h, tile))
        gz.append(flat_sums(g * z, tile))
        lz.append(flat_sums(after * z, tile))
    rows = jnp.concatenate(
        [known[: 2 * rights, :]]
        + rows + gh + gz + lz
        + [known[2 * rights : 3 * rights, :], jnp.zeros((tile - STATS * rights, tile), F32)],
        axis=0,
    )
    high, low = halves(rows)
    rest = (rows - high.astype(F32) - low.astype(F32)).astype(BF16)
    ones = jnp.ones((8, tile), BF16)
    sums = dot_across(ones, high) + (dot_across(ones, low) + dot_across(ones, rest))
    stats[...] = jnp.broadcast_to(sums[0:1, :][None], stats.shape)
    for write in writes:
        write.wait()


def finish_body(
    stats, side_first, side_next, top_first, top_next, solved, lifted_first, lifted_next,
    inverse_scale, interior, side_traces, top_traces,
    solved_here, side_here, side_next_here, top_here, top_next_here, semaphores
):
    rights = side_traces.shape[1]
    block = solved.shape[0] // rights
    parts = [pl.ds(r * block, block) for r in range(rights)]
    reads = [
        begin(solved.at[part], solved_here.at[part], semaphores.at[r])
        for r, part in enumerate(parts)
    ]
    traces = (
        (side_first, side_here), (side_next, side_next_here), (top_first, top_here),
        (top_next, top_next_here),
    )
    for k, (source, target) in enumerate(traces):
        reads.append(begin(source, target, semaphores.at[rights + k]))
    every = stats[:, 0, :]
    lanes = every.shape[1]

    def quantity(index):
        return every if index == 0 else pltpu.roll(every, lanes - index * rights, 1)

    mu0, mu1 = total_rows(quantity(0)), total_rows(quantity(1))
    alpha = mu0 / mu1
    shift = quantity(8) - alpha
    norm = total_rows(quantity(2) + shift * (2.0 * quantity(3) + shift * quantity(4)))
    energy = total_rows(quantity(5) + shift * (2.0 * quantity(6) + shift * quantity(7)))
    beta = norm / mu0
    alpha_next = norm / (energy - beta * norm / alpha)
    diagonal = iota((rights, lanes), 0) == iota((rights, lanes), 1)

    def column(row):
        return jnp.sum(jnp.where(diagonal, row, 0.0), axis=1, keepdims=True)

    first = column(alpha + alpha_next * (1.0 + beta))
    following = column(-alpha_next * alpha)
    scale = inverse_scale[...]
    scale = jnp.concatenate([scale] * (solved.shape[1] // scale.shape[1]), axis=1)
    writes = []
    for r, part in enumerate(parts):
        reads[r].wait()
        solved_here[part, :] = solved_here[part, :] * scale - (
            first[r : r + 1, :] * lifted_first[part, :]
            + following[r : r + 1, :] * lifted_next[part, :]
        )
        writes.append(begin(solved_here.at[part], interior.at[part], semaphores.at[rights + 4 + r]))
    for k, (here, next_here, out) in enumerate(
        ((side_here, side_next_here, side_traces), (top_here, top_next_here, top_traces))
    ):
        reads[rights + 2 * k].wait()
        reads[rights + 2 * k + 1].wait()
        here[...] = first[None] * here[...] + following[None] * next_here[...]
        writes.append(begin(here, out, semaphores.at[2 * rights + 4 + k]))
    for write in writes:
        write.wait()


def per_device(
    source, interior_inverse, coupling, trace_operator, face_ids, orientation, element_scale
):
    nodes, rights, count = source.shape
    traces = trace_operator.shape[0]
    columns = orientation.shape[1]
    face_nodes = traces // columns
    blocks = lax.axis_size("dev")
    layers = lax.axis_size("gz")
    capacity = count // blocks
    owned = 2 * count
    lines = 2 * blocks * capacity
    flat_rows = rights * count
    lanes = rights * face_nodes
    grid_rows = columns * count
    side_rows = (columns - 2) * count
    ids, codes = face_ids.T, orientation.T
    scale = element_scale.reshape(1, count)
    flat_source = source.transpose(1, 2, 0).reshape(flat_rows, nodes)
    grid = ((grid_rows, lanes), F32)
    faces = [((side_rows, lanes), F32), ((count, lanes), F32), ((count, lanes), F32)]
    flat = ((flat_rows, traces), F32)
    whole = ((flat_rows, nodes), F32)
    table = ((grid_rows, 2 * face_nodes), I32)
    message = ((lines, lanes), F32)
    side_shape = ((face_nodes * rights, owned), F32)
    top_shape = ((face_nodes * rights, count), F32)

    def across(message):
        parts = message.reshape(blocks, 2 * capacity, message.shape[1])
        return lax.all_to_all(parts, "dev", 0, 0, tiled=True).reshape(message.shape)

    def climb(value):
        return lax.ppermute(value, "gz", [(at, (at + 1) % layers) for at in range(layers)])

    def sink(value):
        return lax.ppermute(value, "gz", [((at + 1) % layers, at) for at in range(layers)])

    if blocks & (blocks - 1) == 0:
        gathered = [ids]
        for step in [2**k for k in range(blocks.bit_length() - 1)]:
            if len(gathered) == 4:
                gathered = [jnp.concatenate(gathered, axis=0)]
            pairs = [(at, at ^ step) for at in range(blocks)]
            gathered = gathered + [lax.ppermute(entry, "dev", pairs) for entry in gathered]
        block_of = lambda row, here: row ^ here
    else:
        gathered = [lax.all_gather(ids, "dev", tiled=True)]
        block_of = lambda row, here: row
    solved, coupling_here, table = call(
        functools.partial(solve_body, face_nodes),
        [whole, ((nodes, traces), F32), table],
        [Raw(flat_source), Raw(interior_inverse), Raw(coupling), Raw(codes), Raw(scale)],
        [whole, ((nodes, nodes), F32), (codes.shape, I32), (scale.shape, I32)],
        copies=7,
        flops=6 * flat_rows * nodes * nodes,
    )
    solved, sides, bottom, top = call(
        condense_body,
        [whole + ("raw",)] + faces,
        [solved, coupling_here, table],
        [flat],
        copies=1,
        flops=6 * flat_rows * nodes * traces,
    )
    send, wanted, marks = call(
        functools.partial(names_body, owned, capacity, block_of),
        [message, ((lines, owned), I32), ((8, owned), I32)],
        [ids] + gathered + [sides],
        flops=400 * lines * side_rows * lanes,
    )
    up, down, received = climb(top), sink(bottom), across(send)
    square = ((2, traces, traces), BF16)
    maps, base, below, lift, split = call(
        functools.partial(tables_body, owned, capacity),
        [
            ((lines, 7 * owned), BF16),
            faces[0],
            faces[1],
            ((2, nodes, traces), BF16, "far"),
            square,
        ],
        [marks, wanted, sides, bottom, up, far(interior_inverse), far(coupling),
         far(trace_operator)],
        flops=40 * nodes * nodes * traces,
    )
    mine = ((owned + count, lanes), F32)
    own, local, sides, bottom, top, send = call(
        functools.partial(apply_body, owned),
        [mine + ("raw",), flat + ("raw",)] + faces + [message + ("raw",)],
        [base, maps, received, below, top, down, table, split],
        [grid, mine, flat, flat, message],
        copies=5,
        flops=6 * flat_rows * traces * traces,
    )
    up, down, received = climb(top), sink(bottom), across(send)
    lift_form = ((2, nodes, traces), BF16)
    lifted_first, side_first, top_first, image, base, below, known, shifts = call(
        functools.partial(beside_body, owned),
        [whole + ("raw",), side_shape + ("raw",), top_shape + ("raw",), flat + ("raw",), faces[0],
         faces[1], ((4 * rights, 2 * face_nodes), F32), ((8, lanes), F32)],
        [Raw(own), Raw(local), Raw(lift), table, maps, sides, bottom, top, up],
        [mine, flat, lift_form, grid, flat, whole, side_shape, top_shape],
        copies=7,
        flops=40 * flat_rows * traces * nodes,
    )
    own, local, stats = call(
        functools.partial(stats_body, owned),
        [mine + ("raw",), flat + ("raw",), ((layers * blocks, 1, 2 * face_nodes), F32)],
        [base, maps, received, below, top, down, table, split, known, shifts,
         Raw(own), Raw(local), Raw(image)],
        [grid, mine, flat, flat, mine, flat, flat],
        copies=6,
        flops=6 * flat_rows * traces * traces,
    )
    stats = lax.all_to_all(stats, ("gz", "dev"), 0, 0, tiled=True)
    lifted_next, side_next, top_next, lifted_first, inverse_scale = call(
        functools.partial(after_body, owned),
        [whole, side_shape + ("raw",), top_shape + ("raw",), whole,
         ((count, 2 * face_nodes), F32)],
        [Raw(own), Raw(local), Raw(lift), Raw(lifted_first), table, maps],
        [mine, flat, lift_form, side_shape, top_shape],
        copies=6,
        flops=6 * flat_rows * traces * nodes,
    )
    side_form = ((face_nodes, rights, owned), F32)
    top_form = ((face_nodes, rights, count), F32)
    interior, side_traces, top_traces = call(
        finish_body,
        [whole + ("raw",), side_form + ("raw",), top_form + ("raw",)],
        [stats, Raw(side_first.reshape(side_form[0])), Raw(side_next.reshape(side_form[0])),
         Raw(top_first.reshape(top_form[0])), Raw(top_next.reshape(top_form[0])), Raw(solved),
         lifted_first, lifted_next, inverse_scale],
        [whole, side_form, side_form, top_form, top_form],
        copies=2 * rights + 6,
    )
    interior = interior.reshape(rights, count, nodes).transpose(2, 0, 1)
    return (interior, side_traces, top_traces)


def solution(mesh):
    placed = (
        P(None, None, ("gz", "dev")),
        P(),
        P(),
        P(),
        P(("gz", "dev"), None),
        P(("gz", "dev"), None),
        P(("gz", "dev")),
    )
    return jax.shard_map(
        per_device,
        mesh=mesh,
        in_specs=placed,
        out_specs=(
            P(None, None, ("gz", "dev")),
            P(None, None, ("gz", "dev")),
            P(None, None, ("gz", "dev")),
        ),
        check_vma=False,
    )
```

```python
import functools
import math

import jax
import jax.numpy as jnp
from jax import lax
from jax.experimental import pallas as pl
from jax.experimental.pallas import tpu as pltpu
from jax.sharding import PartitionSpec as P

F32, BF16, I32 = jnp.float32, jnp.bfloat16, jnp.int32
VMEM_BYTES = 24 * 1024 * 1024
STATS = 9


def far(arg):
    return pltpu.with_memory_space_constraint(arg, pltpu.HBM)


class Raw:
    def __init__(self, arg):
        self.arg = arg


def call(body, outs, args, scratch=(), copies=0, flops=0):
    anywhere, near = pl.BlockSpec(memory_space=pl.ANY), pl.BlockSpec(memory_space=pltpu.VMEM)
    scratch = [pltpu.VMEM(*entry) for entry in scratch]
    if copies:
        scratch.append(pltpu.SemaphoreType.DMA((copies,)))
    specs = [anywhere if isinstance(arg, Raw) else near for arg in args]
    args = [far(arg.arg) if isinstance(arg, Raw) else arg for arg in args]
    return pl.pallas_call(
        body,
        out_shape=[
            pltpu.HBM(*out[:2]) if len(out) > 2 else jax.ShapeDtypeStruct(*out) for out in outs
        ],
        in_specs=specs,
        out_specs=[anywhere if out[2:] == ("raw",) else near for out in outs],
        scratch_shapes=scratch,
        compiler_params=pltpu.CompilerParams(vmem_limit_bytes=VMEM_BYTES),
        cost_estimate=pl.CostEstimate(
            flops=flops, bytes_accessed=sum(arg.size * 4 for arg in args), transcendentals=0
        ),
    )(*args)


def begin(source, target, semaphore):
    copy = pltpu.make_async_copy(source, target, semaphore)
    copy.start()
    return copy


def halves(value):
    high = value.astype(BF16)
    return high, (value - high.astype(F32)).astype(BF16)


def dot(left, right):
    return jnp.dot(left, right, preferred_element_type=F32)


def dot_split(left, right):
    rows = left[0].shape[0]
    both = dot(jnp.concatenate(left, axis=0), right[0])
    return both[:rows, :] + (both[rows:, :] + dot(left[0], right[1]))


def pick(onehot, value):
    high, low = halves(value)
    return dot(onehot, high) + dot(onehot, low)


def iota(shape, axis):
    return lax.broadcasted_iota(I32, shape, axis)


def column_of(row):
    size = row.shape[1]
    mask = iota((size, size), 0) == iota((size, size), 1)
    spread = jnp.where(mask, row.astype(F32), 0.0)
    return jnp.sum(spread, axis=1, keepdims=True).astype(I32)


def gather_lanes(value, table):
    return jnp.take_along_axis(value, table, axis=1, mode="promise_in_bounds")


def flip_halves(value):
    return pltpu.roll(value, value.shape[1] // 2, 1)


def lower_half(value):
    return iota(value.shape, 1) < value.shape[1] // 2


def to_flat(total, table, flat, count, pairs):
    width = table.shape[1]
    for c in range(0, total.shape[0] // count, 2):
        rows = slice(c * count, (c + 1) * count)
        rows_next = slice((c + 1) * count, (c + 2) * count)
        forward, forward_next = forward_of(table[rows, :]), forward_of(table[rows_next, :])
        for pair in pairs:
            lanes = slice(pair * width, (pair + 1) * width)
            first = gather_lanes(total[rows, lanes], forward)
            second = gather_lanes(total[rows_next, lanes], forward_next)
            low = lower_half(first)
            at = 2 * pair * count
            lanes = slice(c // 2 * width, (c // 2 + 1) * width)
            flat[at : at + count, lanes] = jnp.where(low, first, second)
            flat[at + count : at + 2 * count, lanes] = flip_halves(jnp.where(low, second, first))


def from_flat(flat, table, placed, count, pairs, columns):
    width = table.shape[1]
    for c in columns[::2]:
        back = back_of(table[c * count : (c + 1) * count, :])
        back_next = back_of(table[(c + 1) * count : (c + 2) * count, :])
        for pair in pairs:
            at = 2 * pair * count
            lanes = slice(c // 2 * width, (c // 2 + 1) * width)
            first = flat[at : at + count, lanes]
            second = flip_halves(flat[at + count : at + 2 * count, lanes])
            low = lower_half(first)
            lanes = slice(pair * width, (pair + 1) * width)
            placed(c, lanes, gather_lanes(jnp.where(low, first, second), back))
            placed(c + 1, lanes, gather_lanes(jnp.where(low, second, first), back_next))


def store_marks(owned, capacity, ids, marks):
    row = jnp.concatenate([ids[2:3, :], ids[3:4, :]], axis=1)
    owner, slot = lax.div(row, owned), lax.rem(row, owned)
    crossing = owner != lax.axis_index("dev")
    count = row.shape[1]
    blocks = lax.axis_size("dev")
    block = iota((blocks, count), 0)
    earlier = (iota((count, count), 0) < iota((count, count), 1)).astype(F32).astype(BF16)
    own = (block == owner) & crossing
    ranks = dot(own.astype(F32).astype(BF16), earlier)
    place = jnp.where(own, (block * (2 * capacity)).astype(F32) + ranks + 1.0, 0.0)
    place = jnp.sum(place, axis=0, keepdims=True).astype(I32) - 1
    first = lax.rem(jnp.concatenate([ids[0:1, :], ids[1:2, :]], axis=1), owned)
    marks[...] = jnp.concatenate(
        [place, first, jnp.where(crossing, -1, slot), jnp.zeros((marks.shape[0] - 3, count), I32)],
        axis=0,
    )


def solve_body(
    face_nodes, owned, capacity, source, inverse, coupling, codes, scales, faces,
    solved, coupling_here, table, marks,
    source_here, inverse_here, orientation, scale, ids, semaphores
):
    small = [
        begin(codes, orientation, semaphores.at[4]),
        begin(scales, scale, semaphores.at[5]),
        begin(faces, ids, semaphores.at[7]),
    ]
    depth = inverse.shape[0] // 2
    reads = []
    for k in range(2):
        part = pl.ds(k * depth, depth)
        reads.append(
            (
                begin(inverse.at[part], inverse_here.at[part], semaphores.at[2 * k]),
                begin(source.at[:, part], source_here.at[:, part], semaphores.at[2 * k + 1]),
            )
        )
    read_coupling = begin(coupling, coupling_here, semaphores.at[6])
    columns = orientation.shape[0]
    count = orientation.shape[1]
    edge = math.isqrt(face_nodes)
    pair = 2 * face_nodes
    lane = iota((count, pair), 1)
    side = lane - lax.rem(lane, face_nodes)
    node = lax.rem(lane, face_nodes)
    a, b = lax.div(node, edge), lax.rem(node, edge)
    for read in small:
        read.wait()
    scaled = column_of(scale[...]) * (pair * pair)
    for c in range(columns):
        turned = side if c % 2 == 0 else face_nodes - side
        code = jnp.broadcast_to(column_of(orientation[c : c + 1, :]), (count, pair))
        swapped = (code & 4) != 0
        first = (code & 2) != 0
        second = (code & 1) != 0
        i = jnp.where(first, edge - 1 - a, a)
        j = jnp.where(second, edge - 1 - b, b)
        forward = turned + jnp.where(swapped, j * edge + i, i * edge + j)
        i, j = jnp.where(swapped, b, a), jnp.where(swapped, a, b)
        i = jnp.where(first, edge - 1 - i, i)
        j = jnp.where(second, edge - 1 - j, j)
        back = turned + i * edge + j
        table[c * count : (c + 1) * count, :] = forward + pair * back + scaled
    store_marks(owned, capacity, ids, marks)
    for k, pieces in enumerate(reads):
        for piece in pieces:
            piece.wait()
        depths = slice(k * depth, (k + 1) * depth)
        product = dot_split(halves(source_here[:, depths]), halves(inverse_here[depths, :]))
        solved[...] = product if k == 0 else solved[...] + product
    read_coupling.wait()


def condense_body(
    solved, coupling, table, solved_out, sides, bottom, top, flat, semaphores
):
    write = begin(solved, solved_out, semaphores.at[0])
    count = bottom.shape[0]
    columns = table.shape[0] // count
    has_below, has_above = layer_masks()
    side_columns = columns - 2

    def placed(column, lanes, value):
        if column < side_columns:
            sides[column * count : (column + 1) * count, lanes] = value
        elif column == side_columns:
            bottom[:, lanes] = value * has_below
        else:
            top[:, lanes] = value * has_above

    pairs = sides.shape[1] // table.shape[1]
    parts = [range(0, pairs // 2), range(pairs // 2, pairs)]
    split = halves(coupling[...])
    for part in parts:
        rows = slice(2 * part[0] * count, 2 * (part[-1] + 1) * count)
        flat[rows, :] = dot_split(halves(solved[rows, :]), split)
    for part in parts:
        from_flat(flat, table, placed, count, part, range(columns))
    write.wait()


def forward_of(table):
    return table & (table.shape[1] - 1)


def back_of(table):
    bits = table.shape[1].bit_length() - 1
    return (table >> bits) & (table.shape[1] - 1)


def scale_of(table):
    bits = table.shape[1].bit_length() - 1
    return (table >> (2 * bits)).astype(F32)


def places(capacity, marks, wanted):
    place, first = marks[0:1, :], marks[1:2, :]
    line = iota(wanted.shape, 0)
    named = wanted[...] == first + 1
    later = lax.rem(line, 2 * capacity) >= capacity
    taken = jnp.concatenate([later & named, line == place], axis=1).astype(F32)
    given = jnp.concatenate([~later & named, later & (line - capacity == place)], axis=1)
    return taken, given.astype(F32)


def names_body(owned, capacity, block_of, ids, *refs):
    *others, marks, sides, send, wanted = refs
    here = lax.axis_index("dev")

    def second(rows, at):
        return jnp.concatenate([rows[at + 2 : at + 3, :], rows[at + 3 : at + 4, :]], axis=1)

    names = jnp.concatenate(
        [second(rows, at) for rows in others for at in range(0, rows.shape[0], ids.shape[0])], axis=0
    )
    blocks, count = names.shape
    earlier = (iota((count, count), 0) < iota((count, count), 1)).astype(F32).astype(BF16)
    block = block_of(iota((blocks, count), 0), here)
    named = (lax.div(names, owned) == here) & (block != here)
    ranks = dot(named.astype(F32).astype(BF16), earlier)
    shape = (send.shape[0], blocks)
    line = iota(shape, 0)
    of_line = block_of(iota(shape, 1), here) == lax.div(line, 2 * capacity)
    of_line = of_line.astype(F32).astype(BF16)
    rank_here = dot(of_line, jnp.where(named, ranks, -1.0).astype(BF16))
    slot_here = dot(of_line, lax.rem(names, owned).astype(F32).astype(BF16))
    line = lax.rem(iota(rank_here.shape, 0), capacity).astype(F32)
    chosen = jnp.where(rank_here == line, slot_here + 1.0, 0.0)
    wanted[...] = jnp.broadcast_to(
        jnp.sum(chosen, axis=1, keepdims=True).astype(I32), wanted.shape
    )
    taken, _ = places(capacity, marks, wanted)
    send[...] = pick(taken.astype(BF16), sides[...])


class Maps:
    def __init__(self, ref, owned):
        self.ref, self.owned = ref, owned

    def part(self, index, width=1):
        return self.ref[:, index * self.owned : (index + width) * self.owned]

    def message(self, sides):
        return pick(self.part(0, 2), sides)

    def with_partners(self, sides):
        near, far_side = sides[: self.owned, :], sides[self.owned :, :]
        return near + pick(self.part(4), far_side), far_side + pick(self.part(5), near)

    def from_message(self, received):
        return pick(self.part(2), received), pick(self.part(3), received)

    def by_face(self, sides):
        return pick(self.part(6), sides)


def tables_body(
    owned, capacity, marks, wanted, sides, bottom, up, inverse, coupling, operator,
    maps, base, below, lift, split
):
    taken, given = places(capacity, marks, wanted)
    first, here = marks[1:2, :], marks[2:3, :]
    across = (column_of(first) == here).astype(F32)
    sorter = (iota((owned, owned), 0) == first).astype(F32)
    maps[...] = jnp.concatenate(
        [taken, given[:, :owned].T, given[:, owned:].T, across, across.T, sorter], axis=1
    ).astype(BF16)
    below[...] = bottom[...] + up[...]
    base[:owned, :], base[owned:, :] = Maps(maps, owned).with_partners(sides[...])
    high, low = halves(dot_split(halves(inverse[...]), halves(coupling[...])))
    lift[0] = high
    lift[1] = low
    split[0], split[1] = halves(operator[...])


def add_up(base, maps, received, below, top, down, total):
    owned = maps.owned
    count = top.shape[0]
    total[2 * owned : 2 * owned + count, :] = below[...]
    total[2 * owned + count :, :] = top[...] + down[...]
    first, second = maps.from_message(received[...])
    total[:owned, :] = base[:owned, :] + first
    total[owned : 2 * owned, :] = base[owned : 2 * owned, :] + second


def own_faces(total, owned, count):
    return jnp.concatenate([total[:owned, :], total[total.shape[0] - count :, :]], axis=0)


def operate(total, table, split, flat, image, count, turned):
    pairs = total.shape[1] // table.shape[1]
    scale = scale_of(table[:count, :])
    scale = jnp.concatenate([scale] * (flat.shape[1] // scale.shape[1]), axis=1)
    parts = [range(0, pairs // 2), range(pairs // 2, pairs)]
    for part in parts:
        to_flat(total, table, flat, count, part)
        rows = slice(2 * part[0] * count, 2 * (part[-1] + 1) * count)
        turned(pl.ds(rows.start, rows.stop - rows.start))
        product = dot_split(halves(flat[rows, :]), (split[0], split[1]))
        image[rows, :] = product * jnp.concatenate([scale] * (product.shape[0] // count), axis=0)
    return parts


def layer_masks():
    layer = lax.axis_index("gz")
    return (layer > 0).astype(F32), (layer < lax.axis_size("gz") - 1).astype(F32)


def apply_body(
    owned, base, maps, received, below, top, down, table, split,
    mine, flat_out, sides_out, bottom_out, top_out, send,
    total, mine_here, flat, image, message, semaphores
):
    count = top.shape[0]
    maps = Maps(maps, owned)
    add_up(base, maps, received, below, top, down, total)
    mine_here[...] = own_faces(total, owned, count)
    writes = [begin(mine_here, mine, semaphores.at[0])]
    has_below, has_above = layer_masks()
    columns = total.shape[0] // count
    side_columns = columns - 2

    def placed(column, lanes, value):
        if column < side_columns:
            sides_out[column * count : (column + 1) * count, lanes] = value
        elif column == side_columns:
            bottom_out[:, lanes] = value * has_below
        else:
            top_out[:, lanes] = value * has_above

    def turned(rows):
        writes.append(begin(flat.at[rows], flat_out.at[rows], semaphores.at[len(writes)]))

    parts = operate(total, table, split, flat, image, count, turned)
    for part in parts:
        from_flat(image, table, placed, count, part, range(side_columns))
        lanes = slice(part[0] * table.shape[1], (part[-1] + 1) * table.shape[1])
        message[:, lanes] = maps.message(sides_out[:, lanes])
        writes.append(
            begin(message.at[:, lanes], send.at[:, lanes], semaphores.at[len(writes)])
        )
    for part in parts:
        from_flat(image, table, placed, count, part, range(side_columns, columns))
    for write in writes:
        write.wait()


def dot_across(left, right):
    return lax.dot_general(left, right, (((1,), (1,)), ((), ())), preferred_element_type=F32)


def lifted(flat, lift):
    high, low = halves(flat)
    return dot_across(high, lift[0]) + (dot_across(low, lift[0]) + dot_across(high, lift[1]))


def store_traces(mine, maps, side_traces, top_traces, rights):
    sides = maps.by_face(mine[: maps.owned, :]).T
    tops = mine[maps.owned :, :].T
    nodes = sides.shape[0] // rights
    for r in range(rights):
        rows = slice(r * nodes, (r + 1) * nodes)
        side_traces[pl.ds(r, nodes, stride=rights), :] = sides[rows, :]
        top_traces[pl.ds(r, nodes, stride=rights), :] = tops[rows, :]


def by_right(rows, rights):
    width = 2 * rows.shape[1] // rights
    low = iota((1, width), 1) < width // 2
    tiles = [rows[:, at : at + width] for at in range(0, rows.shape[1], width)]
    return [jnp.where(low == (r % 2 == 0), tiles[r // 2], 0.0) for r in range(rights)]


def beside_body(
    owned, mine_in, flat_in, lift_in, table, maps, sides, bottom, top, up,
    lifted_out, side_out, top_out, image_out, base, below, known, shifts,
    mine, flat, lift, placed, image, lifted_here, side_traces, top_traces, semaphores
):
    reads = [
        begin(mine_in, mine, semaphores.at[0]),
        begin(flat_in, flat, semaphores.at[1]),
        begin(lift_in, lift, semaphores.at[2]),
    ]
    count = bottom.shape[0]
    rights = flat.shape[0] // count
    maps = Maps(maps, owned)
    placed[: 2 * owned, :] = sides[...]
    placed[2 * owned : 2 * owned + count, :] = bottom[...]
    below[...] = bottom[...] + up[...]
    placed[2 * owned + count :, :] = top[...]
    to_flat(placed, table, image, count, range(rights // 2))
    writes = [begin(image, image_out, semaphores.at[3])]
    first, second = maps.with_partners(sides[...])
    base[:owned, :], base[owned:, :] = first, second
    reads[0].wait()
    store_traces(mine, maps, side_traces, top_traces, rights)
    writes.append(begin(side_traces, side_out, semaphores.at[4]))
    writes.append(begin(top_traces, top_out, semaphores.at[5]))
    reads[1].wait()
    reads[2].wait()
    lifted_here[...] = lifted(flat[...], lift)
    writes.append(begin(lifted_here, lifted_out, semaphores.at[6]))
    inside = jnp.sum(maps.part(4).astype(F32), axis=1, keepdims=True)
    b, w = mine[:owned, :], base[:owned, :] * inside
    lanes = mine.shape[1]
    width = lanes // rights
    group = lax.div(iota((lanes, lanes), 0), width) == lax.div(iota((lanes, lanes), 1), width)
    rows = [total_rows(b * w), total_rows(w * w), jnp.ones((6, lanes), F32)]
    pair = grouped(jnp.concatenate(rows, axis=0), group.astype(F32).astype(BF16))
    sigma = jnp.where(pair[1:2] > 0.0, pair[0:1] / pair[1:2], 0.0)
    tile = 2 * width
    spread = []
    for r in range(rights):
        piece = sigma[:, r // 2 * tile : (r // 2 + 1) * tile]
        low = lower_half(piece) == (r % 2 == 0)
        spread.append(jnp.where(low, piece, flip_halves(piece)))
    spread = jnp.concatenate(spread, axis=0)
    shifts[...] = jnp.broadcast_to(sigma, shifts.shape)
    known[...] = jnp.concatenate(
        by_right(total_rows(mine[...] * mine[...]), rights)
        + [
            flat_sums(flat[at : at + count, :] * image[at : at + count, :], tile)
            for at in range(0, flat.shape[0], count)
        ]
        + [jnp.where(iota(spread.shape, 1) == 0, spread, 0.0), spread],
        axis=0,
    )
    for write in writes:
        write.wait()


def after_body(
    owned, mine_in, flat_in, lift_in, lifted_first, table, maps,
    lifted_out, side_out, top_out, first_out, inverse_scale,
    mine, flat, lift, side_traces, top_traces, semaphores
):
    reads = [
        begin(mine_in, mine, semaphores.at[0]),
        begin(flat_in, flat, semaphores.at[1]),
        begin(lift_in, lift, semaphores.at[2]),
        begin(lifted_first, first_out, semaphores.at[3]),
    ]
    count = inverse_scale.shape[0]
    inverse_scale[...] = 1.0 / scale_of(table[:count, :])
    reads[0].wait()
    store_traces(mine, Maps(maps, owned), side_traces, top_traces, flat.shape[0] // count)
    writes = [
        begin(side_traces, side_out, semaphores.at[4]),
        begin(top_traces, top_out, semaphores.at[5]),
    ]
    reads[1].wait()
    reads[2].wait()
    lifted_out[...] = lifted(flat[...], lift)
    reads[3].wait()
    for write in writes:
        write.wait()


def total_rows(value):
    return jnp.sum(value, axis=0, keepdims=True)


def grouped(rows, group):
    high, rest = halves(rows)
    middle = rest.astype(F32)
    low = (rows - high.astype(F32) - middle).astype(BF16)
    return dot(high, group) + (dot(rest, group) + dot(low, group))


def fold(value):
    return jnp.sum(value.reshape(value.shape[0] // 8, 8, value.shape[1]), axis=0)


def flat_sums(value, tile):
    value = fold(value)
    parts = [value[:, at : at + tile] for at in range(0, value.shape[1], tile)]
    return total_rows(functools.reduce(jnp.add, parts))


def stats_body(
    owned, base, maps, received, below, top, down, table, split, known, shifts, mine_in,
    flat_in, image_in, next_mine_out, next_flat_out, stats,
    total_next, mine, flat, image, next_mine, next_flat, next_image, semaphores
):
    count = top.shape[0]
    rights = flat.shape[0] // count
    reads = [
        begin(mine_in, mine, semaphores.at[0]),
        begin(flat_in, flat, semaphores.at[1]),
        begin(image_in, image, semaphores.at[2]),
    ]
    maps = Maps(maps, owned)
    add_up(base, maps, received, below, top, down, total_next)
    next_mine[...] = own_faces(total_next, owned, count)
    writes = [begin(next_mine, next_mine_out, semaphores.at[3])]

    def turned(rows):
        writes.append(
            begin(next_flat.at[rows], next_flat_out.at[rows], semaphores.at[3 + len(writes)])
        )

    operate(total_next, table, split, next_flat, next_image, count, turned)
    for read in reads:
        read.wait()
    sigma = shifts[0:1, :]
    rr = rw = ww = 0.0
    for at in range(0, mine.shape[0], count):
        w = next_mine[at : at + count, :]
        r = mine[at : at + count, :] - sigma * w
        rr, rw, ww = rr + fold(r * r), rw + fold(r * w), ww + fold(w * w)
    rows = []
    for part in (rr, rw, ww):
        rows += by_right(total_rows(part), rights)
    tile = stats.shape[2]
    gh, gz, lz = [], [], []
    for r in range(rights):
        part = slice(r * count, (r + 1) * count)
        shift = known[3 * rights + r : 3 * rights + r + 1, :]
        shift = jnp.concatenate([shift] * (flat.shape[1] // tile), axis=1)
        after, z = next_flat[part, :], next_image[part, :]
        g, h = flat[part, :] - shift * after, image[part, :] - shift * z
        gh.append(flat_sums(g * h, tile))
        gz.append(flat_sums(g * z, tile))
        lz.append(flat_sums(after * z, tile))
    rows = jnp.concatenate(
        [known[: 2 * rights, :]]
        + rows + gh + gz + lz
        + [known[2 * rights : 3 * rights, :], jnp.zeros((tile - STATS * rights, tile), F32)],
        axis=0,
    )
    high, low = halves(rows)
    rest = (rows - high.astype(F32) - low.astype(F32)).astype(BF16)
    ones = jnp.ones((8, tile), BF16)
    sums = dot_across(ones, high) + (dot_across(ones, low) + dot_across(ones, rest))
    stats[...] = jnp.broadcast_to(sums[0:1, :][None], stats.shape)
    for write in writes:
        write.wait()


def finish_body(
    stats, side_first, side_next, top_first, top_next, solved, lifted_first, lifted_next,
    inverse_scale, interior, side_traces, top_traces,
    solved_here, side_here, side_next_here, top_here, top_next_here, semaphores
):
    rights = side_traces.shape[1]
    block = solved.shape[0] // rights
    parts = [pl.ds(r * block, block) for r in range(rights)]
    reads = [
        begin(solved.at[part], solved_here.at[part], semaphores.at[r])
        for r, part in enumerate(parts)
    ]
    traces = (
        (side_first, side_here), (side_next, side_next_here), (top_first, top_here),
        (top_next, top_next_here),
    )
    for k, (source, target) in enumerate(traces):
        reads.append(begin(source, target, semaphores.at[rights + k]))
    every = stats[:, 0, :]
    lanes = every.shape[1]

    def quantity(index):
        return every if index == 0 else pltpu.roll(every, lanes - index * rights, 1)

    mu0, mu1 = total_rows(quantity(0)), total_rows(quantity(1))
    alpha = mu0 / mu1
    shift = quantity(8) - alpha
    norm = total_rows(quantity(2) + shift * (2.0 * quantity(3) + shift * quantity(4)))
    energy = total_rows(quantity(5) + shift * (2.0 * quantity(6) + shift * quantity(7)))
    beta = norm / mu0
    alpha_next = norm / (energy - beta * norm / alpha)
    diagonal = iota((rights, lanes), 0) == iota((rights, lanes), 1)

    def column(row):
        return jnp.sum(jnp.where(diagonal, row, 0.0), axis=1, keepdims=True)

    first = column(alpha + alpha_next * (1.0 + beta))
    following = column(-alpha_next * alpha)
    scale = inverse_scale[...]
    scale = jnp.concatenate([scale] * (solved.shape[1] // scale.shape[1]), axis=1)
    writes = []
    for r, part in enumerate(parts):
        reads[r].wait()
        solved_here[part, :] = solved_here[part, :] * scale - (
            first[r : r + 1, :] * lifted_first[part, :]
            + following[r : r + 1, :] * lifted_next[part, :]
        )
        writes.append(begin(solved_here.at[part], interior.at[part], semaphores.at[rights + 4 + r]))
    for k, (here, next_here, out) in enumerate(
        ((side_here, side_next_here, side_traces), (top_here, top_next_here, top_traces))
    ):
        reads[rights + 2 * k].wait()
        reads[rights + 2 * k + 1].wait()
        here[...] = first[None] * here[...] + following[None] * next_here[...]
        writes.append(begin(here, out, semaphores.at[2 * rights + 4 + k]))
    for write in writes:
        write.wait()


def per_device(
    source, interior_inverse, coupling, trace_operator, face_ids, orientation, element_scale
):
    nodes, rights, count = source.shape
    traces = trace_operator.shape[0]
    columns = orientation.shape[1]
    face_nodes = traces // columns
    blocks = lax.axis_size("dev")
    layers = lax.axis_size("gz")
    capacity = count // blocks
    owned = 2 * count
    lines = 2 * blocks * capacity
    flat_rows = rights * count
    lanes = rights * face_nodes
    grid_rows = columns * count
    side_rows = (columns - 2) * count
    ids, codes = face_ids.T, orientation.T
    scale = element_scale.reshape(1, count)
    flat_source = source.transpose(1, 2, 0).reshape(flat_rows, nodes)
    grid = ((grid_rows, lanes), F32)
    faces = [((side_rows, lanes), F32), ((count, lanes), F32), ((count, lanes), F32)]
    flat = ((flat_rows, traces), F32)
    whole = ((flat_rows, nodes), F32)
    table = ((grid_rows, 2 * face_nodes), I32)
    message = ((lines, lanes), F32)
    side_shape = ((face_nodes * rights, owned), F32)
    top_shape = ((face_nodes * rights, count), F32)

    def across(message):
        parts = message.reshape(blocks, 2 * capacity, message.shape[1])
        return lax.all_to_all(parts, "dev", 0, 0, tiled=True).reshape(message.shape)

    def climb(value):
        return lax.ppermute(value, "gz", [(at, (at + 1) % layers) for at in range(layers)])

    def sink(value):
        return lax.ppermute(value, "gz", [((at + 1) % layers, at) for at in range(layers)])

    if blocks & (blocks - 1) == 0:
        gathered = [ids]
        for step in [2**k for k in range(blocks.bit_length() - 1)]:
            if len(gathered) == 4:
                gathered = [jnp.concatenate(gathered, axis=0)]
            pairs = [(at, at ^ step) for at in range(blocks)]
            gathered = gathered + [lax.ppermute(entry, "dev", pairs) for entry in gathered]
        block_of = lambda row, here: row ^ here
    else:
        gathered = [lax.all_gather(ids, "dev", tiled=True)]
        block_of = lambda row, here: row
    solved, coupling_here, table, marks = call(
        functools.partial(solve_body, face_nodes, owned, capacity),
        [whole, ((nodes, traces), F32), table, ((8, owned), I32)],
        [Raw(flat_source), Raw(interior_inverse), Raw(coupling), Raw(codes), Raw(scale), Raw(ids)],
        [whole, ((nodes, nodes), F32), (codes.shape, I32), (scale.shape, I32), (ids.shape, I32)],
        copies=8,
        flops=6 * flat_rows * nodes * nodes,
    )
    solved, sides, bottom, top = call(
        condense_body,
        [whole + ("raw",)] + faces,
        [solved, coupling_here, table],
        [flat],
        copies=1,
        flops=6 * flat_rows * nodes * traces,
    )
    send, wanted = call(
        functools.partial(names_body, owned, capacity, block_of),
        [message, ((lines, owned), I32)],
        [ids] + gathered + [marks, sides],
        flops=400 * lines * side_rows * lanes,
    )
    up, down, received = climb(top), sink(bottom), across(send)
    square = ((2, traces, traces), BF16)
    maps, base, below, lift, split = call(
        functools.partial(tables_body, owned, capacity),
        [
            ((lines, 7 * owned), BF16),
            faces[0],
            faces[1],
            ((2, nodes, traces), BF16, "far"),
            square,
        ],
        [marks, wanted, sides, bottom, up, far(interior_inverse), far(coupling),
         far(trace_operator)],
        flops=40 * nodes * nodes * traces,
    )
    mine = ((owned + count, lanes), F32)
    own, local, sides, bottom, top, send = call(
        functools.partial(apply_body, owned),
        [mine + ("raw",), flat + ("raw",)] + faces + [message + ("raw",)],
        [base, maps, received, below, top, down, table, split],
        [grid, mine, flat, flat, message],
        copies=5,
        flops=6 * flat_rows * traces * traces,
    )
    up, down, received = climb(top), sink(bottom), across(send)
    lift_form = ((2, nodes, traces), BF16)
    lifted_first, side_first, top_first, image, base, below, known, shifts = call(
        functools.partial(beside_body, owned),
        [whole + ("raw",), side_shape + ("raw",), top_shape + ("raw",), flat + ("raw",), faces[0],
         faces[1], ((4 * rights, 2 * face_nodes), F32), ((8, lanes), F32)],
        [Raw(own), Raw(local), Raw(lift), table, maps, sides, bottom, top, up],
        [mine, flat, lift_form, grid, flat, whole, side_shape, top_shape],
        copies=7,
        flops=40 * flat_rows * traces * nodes,
    )
    own, local, stats = call(
        functools.partial(stats_body, owned),
        [mine + ("raw",), flat + ("raw",), ((layers * blocks, 1, 2 * face_nodes), F32)],
        [base, maps, received, below, top, down, table, split, known, shifts,
         Raw(own), Raw(local), Raw(image)],
        [grid, mine, flat, flat, mine, flat, flat],
        copies=6,
        flops=6 * flat_rows * traces * traces,
    )
    stats = lax.all_to_all(stats, ("gz", "dev"), 0, 0, tiled=True)
    lifted_next, side_next, top_next, lifted_first, inverse_scale = call(
        functools.partial(after_body, owned),
        [whole, side_shape + ("raw",), top_shape + ("raw",), whole,
         ((count, 2 * face_nodes), F32)],
        [Raw(own), Raw(local), Raw(lift), Raw(lifted_first), table, maps],
        [mine, flat, lift_form, side_shape, top_shape],
        copies=6,
        flops=6 * flat_rows * traces * nodes,
    )
    side_form = ((face_nodes, rights, owned), F32)
    top_form = ((face_nodes, rights, count), F32)
    interior, side_traces, top_traces = call(
        finish_body,
        [whole + ("raw",), side_form + ("raw",), top_form + ("raw",)],
        [stats, Raw(side_first.reshape(side_form[0])), Raw(side_next.reshape(side_form[0])),
         Raw(top_first.reshape(top_form[0])), Raw(top_next.reshape(top_form[0])), Raw(solved),
         lifted_first, lifted_next, inverse_scale],
        [whole, side_form, side_form, top_form, top_form],
        copies=2 * rights + 6,
    )
    interior = interior.reshape(rights, count, nodes).transpose(2, 0, 1)
    return (interior, side_traces, top_traces)


def solution(mesh):
    placed = (
        P(None, None, ("gz", "dev")),
        P(),
        P(),
        P(),
        P(("gz", "dev"), None),
        P(("gz", "dev"), None),
        P(("gz", "dev")),
    )
    return jax.shard_map(
        per_device,
        mesh=mesh,
        in_specs=placed,
        out_specs=(
            P(None, None, ("gz", "dev")),
            P(None, None, ("gz", "dev")),
            P(None, None, ("gz", "dev")),
        ),
        check_vma=False,
    )
```

```python
import functools
import math

import jax
import jax.numpy as jnp
from jax import lax
from jax.experimental import pallas as pl
from jax.experimental.pallas import tpu as pltpu
from jax.sharding import PartitionSpec as P

F32, BF16, I32 = jnp.float32, jnp.bfloat16, jnp.int32
VMEM_BYTES = 24 * 1024 * 1024
STATS = 9


def far(arg):
    return pltpu.with_memory_space_constraint(arg, pltpu.HBM)


class Raw:
    def __init__(self, arg):
        self.arg = arg


def call(body, outs, args, scratch=(), copies=0, flops=0):
    anywhere, near = pl.BlockSpec(memory_space=pl.ANY), pl.BlockSpec(memory_space=pltpu.VMEM)
    scratch = [pltpu.VMEM(*entry) for entry in scratch]
    if copies:
        scratch.append(pltpu.SemaphoreType.DMA((copies,)))
    specs = [anywhere if isinstance(arg, Raw) else near for arg in args]
    args = [far(arg.arg) if isinstance(arg, Raw) else arg for arg in args]
    return pl.pallas_call(
        body,
        out_shape=[
            pltpu.HBM(*out[:2]) if len(out) > 2 else jax.ShapeDtypeStruct(*out) for out in outs
        ],
        in_specs=specs,
        out_specs=[anywhere if out[2:] == ("raw",) else near for out in outs],
        scratch_shapes=scratch,
        compiler_params=pltpu.CompilerParams(vmem_limit_bytes=VMEM_BYTES),
        cost_estimate=pl.CostEstimate(
            flops=flops, bytes_accessed=sum(arg.size * 4 for arg in args), transcendentals=0
        ),
    )(*args)


def begin(source, target, semaphore):
    copy = pltpu.make_async_copy(source, target, semaphore)
    copy.start()
    return copy


def halves(value):
    high = value.astype(BF16)
    return high, (value - high.astype(F32)).astype(BF16)


def dot(left, right):
    return jnp.dot(left, right, preferred_element_type=F32)


def dot_split(left, right):
    rows = left[0].shape[0]
    both = dot(jnp.concatenate(left, axis=0), right[0])
    return both[:rows, :] + (both[rows:, :] + dot(left[0], right[1]))


def pick(onehot, value):
    high, low = halves(value)
    return dot(onehot, high) + dot(onehot, low)


def iota(shape, axis):
    return lax.broadcasted_iota(I32, shape, axis)


def column_of(row):
    size = row.shape[1]
    mask = iota((size, size), 0) == iota((size, size), 1)
    spread = jnp.where(mask, row.astype(F32), 0.0)
    return jnp.sum(spread, axis=1, keepdims=True).astype(I32)


def gather_lanes(value, table):
    return jnp.take_along_axis(value, table, axis=1, mode="promise_in_bounds")


def flip_halves(value):
    return pltpu.roll(value, value.shape[1] // 2, 1)


def lower_half(value):
    return iota(value.shape, 1) < value.shape[1] // 2


def to_flat(total, table, flat, count, pairs):
    width = table.shape[1]
    for c in range(0, total.shape[0] // count, 2):
        rows = slice(c * count, (c + 1) * count)
        rows_next = slice((c + 1) * count, (c + 2) * count)
        forward, forward_next = forward_of(table[rows, :]), forward_of(table[rows_next, :])
        for pair in pairs:
            lanes = slice(pair * width, (pair + 1) * width)
            first = gather_lanes(total[rows, lanes], forward)
            second = gather_lanes(total[rows_next, lanes], forward_next)
            low = lower_half(first)
            at = 2 * pair * count
            lanes = slice(c // 2 * width, (c // 2 + 1) * width)
            flat[at : at + count, lanes] = jnp.where(low, first, second)
            flat[at + count : at + 2 * count, lanes] = flip_halves(jnp.where(low, second, first))


def from_flat(flat, table, placed, count, pairs, columns):
    width = table.shape[1]
    for c in columns[::2]:
        back = back_of(table[c * count : (c + 1) * count, :])
        back_next = back_of(table[(c + 1) * count : (c + 2) * count, :])
        for pair in pairs:
            at = 2 * pair * count
            lanes = slice(c // 2 * width, (c // 2 + 1) * width)
            first = flat[at : at + count, lanes]
            second = flip_halves(flat[at + count : at + 2 * count, lanes])
            low = lower_half(first)
            lanes = slice(pair * width, (pair + 1) * width)
            placed(c, lanes, gather_lanes(jnp.where(low, first, second), back))
            placed(c + 1, lanes, gather_lanes(jnp.where(low, second, first), back_next))


def solve_body(
    face_nodes, source, inverse, coupling, codes, scales, solved, coupling_here, table,
    source_here, inverse_here, orientation, scale, semaphores
):
    small = [begin(codes, orientation, semaphores.at[4]), begin(scales, scale, semaphores.at[5])]
    depth = inverse.shape[0] // 2
    reads = []
    for k in range(2):
        part = pl.ds(k * depth, depth)
        reads.append(
            (
                begin(inverse.at[part], inverse_here.at[part], semaphores.at[2 * k]),
                begin(source.at[:, part], source_here.at[:, part], semaphores.at[2 * k + 1]),
            )
        )
    read_coupling = begin(coupling, coupling_here, semaphores.at[6])
    columns = orientation.shape[0]
    count = orientation.shape[1]
    edge = math.isqrt(face_nodes)
    pair = 2 * face_nodes
    lane = iota((count, pair), 1)
    side = lane - lax.rem(lane, face_nodes)
    node = lax.rem(lane, face_nodes)
    a, b = lax.div(node, edge), lax.rem(node, edge)
    for read in small:
        read.wait()
    scaled = column_of(scale[...]) * (pair * pair)
    for c in range(columns):
        turned = side if c % 2 == 0 else face_nodes - side
        code = jnp.broadcast_to(column_of(orientation[c : c + 1, :]), (count, pair))
        swapped = (code & 4) != 0
        first = (code & 2) != 0
        second = (code & 1) != 0
        i = jnp.where(first, edge - 1 - a, a)
        j = jnp.where(second, edge - 1 - b, b)
        forward = turned + jnp.where(swapped, j * edge + i, i * edge + j)
        i, j = jnp.where(swapped, b, a), jnp.where(swapped, a, b)
        i = jnp.where(first, edge - 1 - i, i)
        j = jnp.where(second, edge - 1 - j, j)
        back = turned + i * edge + j
        table[c * count : (c + 1) * count, :] = forward + pair * back + scaled
    for k, pieces in enumerate(reads):
        for piece in pieces:
            piece.wait()
        depths = slice(k * depth, (k + 1) * depth)
        product = dot_split(halves(source_here[:, depths]), halves(inverse_here[depths, :]))
        solved[...] = product if k == 0 else solved[...] + product
    read_coupling.wait()


def condense_body(
    solved, coupling, table, solved_out, sides, bottom, top, flat, semaphores
):
    write = begin(solved, solved_out, semaphores.at[0])
    count = bottom.shape[0]
    columns = table.shape[0] // count
    has_below, has_above = layer_masks()
    side_columns = columns - 2

    def placed(column, lanes, value):
        if column < side_columns:
            sides[column * count : (column + 1) * count, lanes] = value
        elif column == side_columns:
            bottom[:, lanes] = value * has_below
        else:
            top[:, lanes] = value * has_above

    pairs = sides.shape[1] // table.shape[1]
    parts = [range(0, pairs // 2), range(pairs // 2, pairs)]
    split = halves(coupling[...])
    for part in parts:
        rows = slice(2 * part[0] * count, 2 * (part[-1] + 1) * count)
        flat[rows, :] = dot_split(halves(solved[rows, :]), split)
    for part in parts:
        from_flat(flat, table, placed, count, part, range(columns))
    write.wait()


def forward_of(table):
    return table & (table.shape[1] - 1)


def back_of(table):
    bits = table.shape[1].bit_length() - 1
    return (table >> bits) & (table.shape[1] - 1)


def scale_of(table):
    bits = table.shape[1].bit_length() - 1
    return (table >> (2 * bits)).astype(F32)


def places(capacity, marks, wanted):
    place, first = marks[0:1, :], marks[1:2, :]
    line = iota(wanted.shape, 0)
    named = wanted[...] == first + 1
    later = lax.rem(line, 2 * capacity) >= capacity
    taken = jnp.concatenate([later & named, line == place], axis=1).astype(F32)
    given = jnp.concatenate([~later & named, later & (line - capacity == place)], axis=1)
    return taken, given.astype(F32)


def names_body(owned, capacity, block_of, ids, *refs):
    *others, sides, send, wanted, marks = refs
    here = lax.axis_index("dev")

    def second(rows, at):
        return jnp.concatenate([rows[at + 2 : at + 3, :], rows[at + 3 : at + 4, :]], axis=1)

    names = jnp.concatenate(
        [second(rows, at) for rows in others for at in range(0, rows.shape[0], ids.shape[0])], axis=0
    )
    blocks, count = names.shape
    earlier = (iota((count, count), 0) < iota((count, count), 1)).astype(F32).astype(BF16)
    block = block_of(iota((blocks, count), 0), here)
    row = second(ids, 0)
    owner, slot = lax.div(row, owned), lax.rem(row, owned)
    crossing = owner != here
    named = (lax.div(names, owned) == here) & (block != here)
    own = (block == owner) & crossing
    masks = jnp.concatenate([named.astype(F32), own.astype(F32)], axis=0).astype(BF16)
    ranks = dot(masks, earlier)
    place = jnp.where(own, (block * (2 * capacity)).astype(F32) + ranks[blocks:, :] + 1.0, 0.0)
    place = jnp.sum(place, axis=0, keepdims=True).astype(I32) - 1
    first = lax.rem(jnp.concatenate([ids[0:1, :], ids[1:2, :]], axis=1), owned)
    marks[...] = jnp.concatenate(
        [place, first, jnp.where(crossing, -1, slot), jnp.zeros((marks.shape[0] - 3, count), I32)],
        axis=0,
    )
    shape = (send.shape[0], blocks)
    line = iota(shape, 0)
    of_line = block_of(iota(shape, 1), here) == lax.div(line, 2 * capacity)
    of_line = of_line.astype(F32).astype(BF16)
    rank_here = dot(of_line, jnp.where(named, ranks[:blocks, :], -1.0).astype(BF16))
    slot_here = dot(of_line, lax.rem(names, owned).astype(F32).astype(BF16))
    line = lax.rem(iota(rank_here.shape, 0), capacity).astype(F32)
    chosen = jnp.where(rank_here == line, slot_here + 1.0, 0.0)
    wanted[...] = jnp.broadcast_to(
        jnp.sum(chosen, axis=1, keepdims=True).astype(I32), wanted.shape
    )
    taken, _ = places(capacity, marks, wanted)
    send[...] = pick(taken.astype(BF16), sides[...])


class Maps:
    def __init__(self, ref, owned):
        self.ref, self.owned = ref, owned

    def part(self, index, width=1):
        return self.ref[:, index * self.owned : (index + width) * self.owned]

    def message(self, sides):
        return pick(self.part(0, 2), sides)

    def with_partners(self, sides):
        near, far_side = sides[: self.owned, :], sides[self.owned :, :]
        return near + pick(self.part(4), far_side), far_side + pick(self.part(5), near)

    def from_message(self, received):
        return pick(self.part(2), received), pick(self.part(3), received)

    def by_face(self, sides):
        return pick(self.part(6), sides)


def tables_body(
    owned, capacity, marks, wanted, sides, bottom, up, inverse, coupling, operator,
    maps, base, below, lift, split
):
    taken, given = places(capacity, marks, wanted)
    first, here = marks[1:2, :], marks[2:3, :]
    across = (column_of(first) == here).astype(F32)
    sorter = (iota((owned, owned), 0) == first).astype(F32)
    maps[...] = jnp.concatenate(
        [taken, given[:, :owned].T, given[:, owned:].T, across, across.T, sorter], axis=1
    ).astype(BF16)
    below[...] = bottom[...] + up[...]
    base[:owned, :], base[owned:, :] = Maps(maps, owned).with_partners(sides[...])
    high, low = halves(dot_split(halves(inverse[...]), halves(coupling[...])))
    lift[0] = high
    lift[1] = low
    split[0], split[1] = halves(operator[...])


def add_up(base, maps, received, below, top, down, total):
    owned = maps.owned
    count = top.shape[0]
    total[2 * owned : 2 * owned + count, :] = below[...]
    total[2 * owned + count :, :] = top[...] + down[...]
    first, second = maps.from_message(received[...])
    total[:owned, :] = base[:owned, :] + first
    total[owned : 2 * owned, :] = base[owned : 2 * owned, :] + second


def own_faces(total, owned, count):
    return jnp.concatenate([total[:owned, :], total[total.shape[0] - count :, :]], axis=0)


def operate(total, table, split, flat, image, count, turned):
    pairs = total.shape[1] // table.shape[1]
    scale = scale_of(table[:count, :])
    scale = jnp.concatenate([scale] * (flat.shape[1] // scale.shape[1]), axis=1)
    parts = [range(0, pairs // 2), range(pairs // 2, pairs)]
    for part in parts:
        to_flat(total, table, flat, count, part)
        rows = slice(2 * part[0] * count, 2 * (part[-1] + 1) * count)
        turned(pl.ds(rows.start, rows.stop - rows.start))
        product = dot_split(halves(flat[rows, :]), (split[0], split[1]))
        image[rows, :] = product * jnp.concatenate([scale] * (product.shape[0] // count), axis=0)
    return parts


def layer_masks():
    layer = lax.axis_index("gz")
    return (layer > 0).astype(F32), (layer < lax.axis_size("gz") - 1).astype(F32)


def apply_body(
    owned, base, maps, received, below, top, down, table, split,
    mine, flat_out, sides_out, bottom_out, top_out, send,
    total, mine_here, flat, image, message, semaphores
):
    count = top.shape[0]
    maps = Maps(maps, owned)
    add_up(base, maps, received, below, top, down, total)
    mine_here[...] = own_faces(total, owned, count)
    writes = [begin(mine_here, mine, semaphores.at[0])]
    has_below, has_above = layer_masks()
    columns = total.shape[0] // count
    side_columns = columns - 2

    def placed(column, lanes, value):
        if column < side_columns:
            sides_out[column * count : (column + 1) * count, lanes] = value
        elif column == side_columns:
            bottom_out[:, lanes] = value * has_below
        else:
            top_out[:, lanes] = value * has_above

    def turned(rows):
        writes.append(begin(flat.at[rows], flat_out.at[rows], semaphores.at[len(writes)]))

    parts = operate(total, table, split, flat, image, count, turned)
    for part in parts:
        from_flat(image, table, placed, count, part, range(side_columns))
        lanes = slice(part[0] * table.shape[1], (part[-1] + 1) * table.shape[1])
        message[:, lanes] = maps.message(sides_out[:, lanes])
        writes.append(
            begin(message.at[:, lanes], send.at[:, lanes], semaphores.at[len(writes)])
        )
    for part in parts:
        from_flat(image, table, placed, count, part, range(side_columns, columns))
    for write in writes:
        write.wait()


def dot_across(left, right):
    return lax.dot_general(left, right, (((1,), (1,)), ((), ())), preferred_element_type=F32)


def lifted(flat, lift):
    high, low = halves(flat)
    return dot_across(high, lift[0]) + (dot_across(low, lift[0]) + dot_across(high, lift[1]))


def store_traces(mine, maps, side_traces, top_traces, rights):
    sides = maps.by_face(mine[: maps.owned, :]).T
    tops = mine[maps.owned :, :].T
    nodes = sides.shape[0] // rights
    for r in range(rights):
        rows = slice(r * nodes, (r + 1) * nodes)
        side_traces[pl.ds(r, nodes, stride=rights), :] = sides[rows, :]
        top_traces[pl.ds(r, nodes, stride=rights), :] = tops[rows, :]


def by_right(rows, rights):
    width = 2 * rows.shape[1] // rights
    low = iota((1, width), 1) < width // 2
    tiles = [rows[:, at : at + width] for at in range(0, rows.shape[1], width)]
    return [jnp.where(low == (r % 2 == 0), tiles[r // 2], 0.0) for r in range(rights)]


def beside_body(
    owned, mine_in, flat_in, lift_in, table, maps, sides, bottom, top, up,
    lifted_out, side_out, top_out, image_out, base, below, known, shifts,
    mine, flat, lift, placed, image, lifted_here, side_traces, top_traces, semaphores
):
    reads = [
        begin(mine_in, mine, semaphores.at[0]),
        begin(flat_in, flat, semaphores.at[1]),
        begin(lift_in, lift, semaphores.at[2]),
    ]
    count = bottom.shape[0]
    rights = flat.shape[0] // count
    maps = Maps(maps, owned)
    placed[: 2 * owned, :] = sides[...]
    placed[2 * owned : 2 * owned + count, :] = bottom[...]
    below[...] = bottom[...] + up[...]
    placed[2 * owned + count :, :] = top[...]
    to_flat(placed, table, image, count, range(rights // 2))
    writes = [begin(image, image_out, semaphores.at[3])]
    first, second = maps.with_partners(sides[...])
    base[:owned, :], base[owned:, :] = first, second
    reads[0].wait()
    store_traces(mine, maps, side_traces, top_traces, rights)
    writes.append(begin(side_traces, side_out, semaphores.at[4]))
    writes.append(begin(top_traces, top_out, semaphores.at[5]))
    reads[1].wait()
    reads[2].wait()
    lifted_here[...] = lifted(flat[...], lift)
    writes.append(begin(lifted_here, lifted_out, semaphores.at[6]))
    inside = jnp.sum(maps.part(4).astype(F32), axis=1, keepdims=True)
    b, w = mine[:owned, :], base[:owned, :] * inside
    lanes = mine.shape[1]
    width = lanes // rights
    group = lax.div(iota((lanes, lanes), 0), width) == lax.div(iota((lanes, lanes), 1), width)
    rows = [total_rows(b * w), total_rows(w * w), jnp.ones((6, lanes), F32)]
    pair = grouped(jnp.concatenate(rows, axis=0), group.astype(F32).astype(BF16))
    sigma = jnp.where(pair[1:2] > 0.0, pair[0:1] / pair[1:2], 0.0)
    tile = 2 * width
    spread = []
    for r in range(rights):
        piece = sigma[:, r // 2 * tile : (r // 2 + 1) * tile]
        low = lower_half(piece) == (r % 2 == 0)
        spread.append(jnp.where(low, piece, flip_halves(piece)))
    spread = jnp.concatenate(spread, axis=0)
    shifts[...] = jnp.broadcast_to(sigma, shifts.shape)
    known[...] = jnp.concatenate(
        by_right(total_rows(mine[...] * mine[...]), rights)
        + [
            flat_sums(flat[at : at + count, :] * image[at : at + count, :], tile)
            for at in range(0, flat.shape[0], count)
        ]
        + [jnp.where(iota(spread.shape, 1) == 0, spread, 0.0), spread],
        axis=0,
    )
    for write in writes:
        write.wait()


def after_body(
    owned, mine_in, flat_in, lift_in, lifted_first, table, maps,
    lifted_out, side_out, top_out, first_out, inverse_scale,
    mine, flat, lift, side_traces, top_traces, semaphores
):
    reads = [
        begin(mine_in, mine, semaphores.at[0]),
        begin(flat_in, flat, semaphores.at[1]),
        begin(lift_in, lift, semaphores.at[2]),
        begin(lifted_first, first_out, semaphores.at[3]),
    ]
    count = inverse_scale.shape[0]
    inverse_scale[...] = 1.0 / scale_of(table[:count, :])
    reads[0].wait()
    store_traces(mine, Maps(maps, owned), side_traces, top_traces, flat.shape[0] // count)
    writes = [
        begin(side_traces, side_out, semaphores.at[4]),
        begin(top_traces, top_out, semaphores.at[5]),
    ]
    reads[1].wait()
    reads[2].wait()
    lifted_out[...] = lifted(flat[...], lift)
    reads[3].wait()
    for write in writes:
        write.wait()


def total_rows(value):
    return jnp.sum(value, axis=0, keepdims=True)


def grouped(rows, group):
    high, rest = halves(rows)
    middle = rest.astype(F32)
    low = (rows - high.astype(F32) - middle).astype(BF16)
    return dot(high, group) + (dot(rest, group) + dot(low, group))


def fold(value):
    return jnp.sum(value.reshape(value.shape[0] // 8, 8, value.shape[1]), axis=0)


def flat_sums(value, tile):
    value = fold(value)
    parts = [value[:, at : at + tile] for at in range(0, value.shape[1], tile)]
    return total_rows(functools.reduce(jnp.add, parts))


def stats_body(
    owned, base, maps, received, below, top, down, table, split, known, shifts, mine_in,
    flat_in, image_in, next_mine_out, next_flat_out, stats,
    total_next, mine, flat, image, next_mine, next_flat, next_image, semaphores
):
    count = top.shape[0]
    rights = flat.shape[0] // count
    reads = [
        begin(mine_in, mine, semaphores.at[0]),
        begin(flat_in, flat, semaphores.at[1]),
        begin(image_in, image, semaphores.at[2]),
    ]
    maps = Maps(maps, owned)
    add_up(base, maps, received, below, top, down, total_next)
    next_mine[...] = own_faces(total_next, owned, count)
    writes = [begin(next_mine, next_mine_out, semaphores.at[3])]

    def turned(rows):
        writes.append(
            begin(next_flat.at[rows], next_flat_out.at[rows], semaphores.at[3 + len(writes)])
        )

    operate(total_next, table, split, next_flat, next_image, count, turned)
    for read in reads:
        read.wait()
    sigma = shifts[0:1, :]
    rr = rw = ww = 0.0
    for at in range(0, mine.shape[0], count):
        w = next_mine[at : at + count, :]
        r = mine[at : at + count, :] - sigma * w
        rr, rw, ww = rr + fold(r * r), rw + fold(r * w), ww + fold(w * w)
    rows = []
    for part in (rr, rw, ww):
        rows += by_right(total_rows(part), rights)
    tile = stats.shape[2]
    gh, gz, lz = [], [], []
    for r in range(rights):
        part = slice(r * count, (r + 1) * count)
        shift = known[3 * rights + r : 3 * rights + r + 1, :]
        shift = jnp.concatenate([shift] * (flat.shape[1] // tile), axis=1)
        after, z = next_flat[part, :], next_image[part, :]
        g, h = flat[part, :] - shift * after, image[part, :] - shift * z
        gh.append(flat_sums(g * h, tile))
        gz.append(flat_sums(g * z, tile))
        lz.append(flat_sums(after * z, tile))
    rows = jnp.concatenate(
        [known[: 2 * rights, :]]
        + rows + gh + gz + lz
        + [known[2 * rights : 3 * rights, :], jnp.zeros((tile - STATS * rights, tile), F32)],
        axis=0,
    )
    high, low = halves(rows)
    rest = (rows - high.astype(F32) - low.astype(F32)).astype(BF16)
    ones = jnp.ones((8, tile), BF16)
    sums = dot_across(ones, high) + (dot_across(ones, low) + dot_across(ones, rest))
    stats[...] = jnp.broadcast_to(sums[0:1, :][None], stats.shape)
    for write in writes:
        write.wait()


def finish_body(
    stats, side_first, side_next, top_first, top_next, solved, lifted_first, lifted_next,
    inverse_scale, interior, side_traces, top_traces,
    solved_here, side_here, side_next_here, top_here, top_next_here, semaphores
):
    rights = side_traces.shape[1]
    block = solved.shape[0] // rights
    group = 2
    parts = [pl.ds(r * block, group * block) for r in range(0, rights, group)]
    reads = [
        begin(solved.at[part], solved_here.at[part], semaphores.at[r])
        for r, part in enumerate(parts)
    ]
    traces = (
        (side_first, side_here), (side_next, side_next_here), (top_first, top_here),
        (top_next, top_next_here),
    )
    for k, (source, target) in enumerate(traces):
        reads.append(begin(source, target, semaphores.at[rights + k]))
    every = stats[:, 0, :]
    lanes = every.shape[1]

    def quantity(index):
        return every if index == 0 else pltpu.roll(every, lanes - index * rights, 1)

    mu0, mu1 = total_rows(quantity(0)), total_rows(quantity(1))
    alpha = mu0 / mu1
    shift = quantity(8) - alpha
    norm = total_rows(quantity(2) + shift * (2.0 * quantity(3) + shift * quantity(4)))
    energy = total_rows(quantity(5) + shift * (2.0 * quantity(6) + shift * quantity(7)))
    beta = norm / mu0
    alpha_next = norm / (energy - beta * norm / alpha)
    diagonal = iota((rights, lanes), 0) == iota((rights, lanes), 1)

    def column(row):
        return jnp.sum(jnp.where(diagonal, row, 0.0), axis=1, keepdims=True)

    first = column(alpha + alpha_next * (1.0 + beta))
    following = column(-alpha_next * alpha)
    scale = inverse_scale[...]
    scale = jnp.concatenate([scale] * (solved.shape[1] // scale.shape[1]), axis=1)
    writes = []
    for r, part in enumerate(parts):
        reads[r].wait()
        for at in range(r * group, (r + 1) * group):
            rows = slice(at * block, (at + 1) * block)
            solved_here[rows, :] = solved_here[rows, :] * scale - (
                first[at : at + 1, :] * lifted_first[rows, :]
                + following[at : at + 1, :] * lifted_next[rows, :]
            )
        writes.append(begin(solved_here.at[part], interior.at[part], semaphores.at[rights + 4 + r]))
    for k, (here, next_here, out) in enumerate(
        ((side_here, side_next_here, side_traces), (top_here, top_next_here, top_traces))
    ):
        reads[rights // group + 2 * k].wait()
        reads[rights // group + 2 * k + 1].wait()
        here[...] = first[None] * here[...] + following[None] * next_here[...]
        writes.append(begin(here, out, semaphores.at[2 * rights + 4 + k]))
    for write in writes:
        write.wait()


def per_device(
    source, interior_inverse, coupling, trace_operator, face_ids, orientation, element_scale
):
    nodes, rights, count = source.shape
    traces = trace_operator.shape[0]
    columns = orientation.shape[1]
    face_nodes = traces // columns
    blocks = lax.axis_size("dev")
    layers = lax.axis_size("gz")
    capacity = count // blocks
    owned = 2 * count
    lines = 2 * blocks * capacity
    flat_rows = rights * count
    lanes = rights * face_nodes
    grid_rows = columns * count
    side_rows = (columns - 2) * count
    ids, codes = face_ids.T, orientation.T
    scale = element_scale.reshape(1, count)
    flat_source = source.transpose(1, 2, 0).reshape(flat_rows, nodes)
    grid = ((grid_rows, lanes), F32)
    faces = [((side_rows, lanes), F32), ((count, lanes), F32), ((count, lanes), F32)]
    flat = ((flat_rows, traces), F32)
    whole = ((flat_rows, nodes), F32)
    table = ((grid_rows, 2 * face_nodes), I32)
    message = ((lines, lanes), F32)
    side_shape = ((face_nodes * rights, owned), F32)
    top_shape = ((face_nodes * rights, count), F32)

    def across(message):
        parts = message.reshape(blocks, 2 * capacity, message.shape[1])
        return lax.all_to_all(parts, "dev", 0, 0, tiled=True).reshape(message.shape)

    def climb(value):
        return lax.ppermute(value, "gz", [(at, (at + 1) % layers) for at in range(layers)])

    def sink(value):
        return lax.ppermute(value, "gz", [((at + 1) % layers, at) for at in range(layers)])

    if blocks & (blocks - 1) == 0:
        gathered = [ids]
        for step in [2**k for k in range(blocks.bit_length() - 1)]:
            if len(gathered) == 4:
                gathered = [jnp.concatenate(gathered, axis=0)]
            pairs = [(at, at ^ step) for at in range(blocks)]
            gathered = gathered + [lax.ppermute(entry, "dev", pairs) for entry in gathered]
        block_of = lambda row, here: row ^ here
    else:
        gathered = [lax.all_gather(ids, "dev", tiled=True)]
        block_of = lambda row, here: row
    solved, coupling_here, table = call(
        functools.partial(solve_body, face_nodes),
        [whole, ((nodes, traces), F32), table],
        [Raw(flat_source), Raw(interior_inverse), Raw(coupling), Raw(codes), Raw(scale)],
        [whole, ((nodes, nodes), F32), (codes.shape, I32), (scale.shape, I32)],
        copies=7,
        flops=6 * flat_rows * nodes * nodes,
    )
    solved, sides, bottom, top = call(
        condense_body,
        [whole + ("raw",)] + faces,
        [solved, coupling_here, table],
        [flat],
        copies=1,
        flops=6 * flat_rows * nodes * traces,
    )
    send, wanted, marks = call(
        functools.partial(names_body, owned, capacity, block_of),
        [message, ((lines, owned), I32), ((8, owned), I32)],
        [ids] + gathered + [sides],
        flops=400 * lines * side_rows * lanes,
    )
    up, down, received = climb(top), sink(bottom), across(send)
    square = ((2, traces, traces), BF16)
    maps, base, below, lift, split = call(
        functools.partial(tables_body, owned, capacity),
        [
            ((lines, 7 * owned), BF16),
            faces[0],
            faces[1],
            ((2, nodes, traces), BF16, "far"),
            square,
        ],
        [marks, wanted, sides, bottom, up, far(interior_inverse), far(coupling),
         far(trace_operator)],
        flops=40 * nodes * nodes * traces,
    )
    mine = ((owned + count, lanes), F32)
    own, local, sides, bottom, top, send = call(
        functools.partial(apply_body, owned),
        [mine + ("raw",), flat + ("raw",)] + faces + [message + ("raw",)],
        [base, maps, received, below, top, down, table, split],
        [grid, mine, flat, flat, message],
        copies=5,
        flops=6 * flat_rows * traces * traces,
    )
    up, down, received = climb(top), sink(bottom), across(send)
    lift_form = ((2, nodes, traces), BF16)
    lifted_first, side_first, top_first, image, base, below, known, shifts = call(
        functools.partial(beside_body, owned),
        [whole + ("raw",), side_shape + ("raw",), top_shape + ("raw",), flat + ("raw",), faces[0],
         faces[1], ((4 * rights, 2 * face_nodes), F32), ((8, lanes), F32)],
        [Raw(own), Raw(local), Raw(lift), table, maps, sides, bottom, top, up],
        [mine, flat, lift_form, grid, flat, whole, side_shape, top_shape],
        copies=7,
        flops=40 * flat_rows * traces * nodes,
    )
    own, local, stats = call(
        functools.partial(stats_body, owned),
        [mine + ("raw",), flat + ("raw",), ((layers * blocks, 1, 2 * face_nodes), F32)],
        [base, maps, received, below, top, down, table, split, known, shifts,
         Raw(own), Raw(local), Raw(image)],
        [grid, mine, flat, flat, mine, flat, flat],
        copies=6,
        flops=6 * flat_rows * traces * traces,
    )
    stats = lax.all_to_all(stats, ("gz", "dev"), 0, 0, tiled=True)
    lifted_next, side_next, top_next, lifted_first, inverse_scale = call(
        functools.partial(after_body, owned),
        [whole, side_shape + ("raw",), top_shape + ("raw",), whole,
         ((count, 2 * face_nodes), F32)],
        [Raw(own), Raw(local), Raw(lift), Raw(lifted_first), table, maps],
        [mine, flat, lift_form, side_shape, top_shape],
        copies=6,
        flops=6 * flat_rows * traces * nodes,
    )
    side_form = ((face_nodes, rights, owned), F32)
    top_form = ((face_nodes, rights, count), F32)
    interior, side_traces, top_traces = call(
        finish_body,
        [whole + ("raw",), side_form + ("raw",), top_form + ("raw",)],
        [stats, Raw(side_first.reshape(side_form[0])), Raw(side_next.reshape(side_form[0])),
         Raw(top_first.reshape(top_form[0])), Raw(top_next.reshape(top_form[0])), Raw(solved),
         lifted_first, lifted_next, inverse_scale],
        [whole, side_form, side_form, top_form, top_form],
        copies=2 * rights + 6,
    )
    interior = interior.reshape(rights, count, nodes).transpose(2, 0, 1)
    return (interior, side_traces, top_traces)


def solution(mesh):
    placed = (
        P(None, None, ("gz", "dev")),
        P(),
        P(),
        P(),
        P(("gz", "dev"), None),
        P(("gz", "dev"), None),
        P(("gz", "dev")),
    )
    return jax.shard_map(
        per_device,
        mesh=mesh,
        in_specs=placed,
        out_specs=(
            P(None, None, ("gz", "dev")),
            P(None, None, ("gz", "dev")),
            P(None, None, ("gz", "dev")),
        ),
        check_vma=False,
    )
```
